128 devices in a mesh: ctx: 32 (over y, x, core), exp: 4 (over z).
Axes of the slice: x: 4, y: 4, z: 4, core: 2. Of those that a mesh axis runs over, the one named last changes fastest.
Arguments:
- filter_entry_array: bfloat16 [16384, 2176], P(('ctx', 'exp')), may hold values from -6 to 6
- gate_input: bfloat16 [16384, 2048], P(('ctx', 'exp')), may hold values from -20 to 20
- step_unshifted: float32 [32, 16384], P(None, ('ctx', 'exp')), may hold values from -4 to 16
- step_bias: float32 [32], replicated, may hold values from -11 to -2
- decay_log: float32 [32], replicated, may hold values from -3.2 to -0.2
- conv_weight: float32 [4, 2176], replicated, may hold values from -3 to 3
- conv_bias: float32 [2176], replicated, may hold values from -3 to 3
- skip_gain: float32 [32], replicated, may hold values from 0.5 to 1.5
- mixer_gain: float32 [2048], replicated, may hold values from 0.25 to 1.75
- residual: bfloat16 [16384, 2048], P(('ctx', 'exp')), may hold values from -14 to 14
- expert_norm: float32 [2048], replicated, may hold values from 0.25 to 1.75
- router_weight: bfloat16 [2048, 32], replicated, may hold values from -0.25 to 0.25
- expert_ids: int32 [16384, 8], P(('ctx', 'exp')), may hold values from 0 to 31, all different within a row; in each aligned block of 128 rows (0 to 127, 128 to 255, ...) at most 40 rows name the same one
- w_gate: bfloat16 [32, 2048, 768], P('ctx'), may hold values from -0.125 to 0.125
- w_up: bfloat16 [32, 2048, 768], P('ctx'), may hold values from -0.125 to 0.125
- w_down: bfloat16 [32, 768, 2048], P('ctx'), may hold values from -0.21875 to 0.21875
Outputs:
- layer_out: bfloat16 [16384, 2048], P(('ctx', 'exp'))
The draws below stay inside these ranges and needn't reach their ends.
Inputs may be any that keep to these rules, and one draw needn't show every extreme that they name: `expert_ids`: in each aligned block of 128 rows (the rows of one device) no expert is named by more than 40 rows, a bound that some block reaches; a row names 8 different experts.
All inputs are finite; a program needn't handle non-finite values.
Results may differ from the reference program's by a relative error of at most 0.0052.
Values may be sent and summed in bfloat16 or wider, within the bound.
A program may use at most 320 MiB of HBM per device.

```python
import math
import jax
import jax.numpy as jnp
import numpy as np
from jax import lax

D = 2048
HEADS = 32
HEAD_DIM = 64
STATE = 64
KERNEL = 4
EXPERTS = 32
TOPK = 8
FF = 768
TOK_DEV = 128
CONV = 2176
CAP = 40
SEQLEN = 16384


def spike_indices_vector(key):
    return jax.random.randint(jax.random.fold_in(key, 901), (3,), 0, SEQLEN)


def fast_heads(key, share_pct):
    picks = jax.random.randint(jax.random.fold_in(key, 902), (HEADS,), 0, 100)
    return picks < share_pct


def draw_step_bias(key, part):
    fast = fast_heads(key, 50)
    key = jax.random.fold_in(key, 3)
    noise = jnp.clip(jax.random.normal(key, (HEADS,), jnp.float32), -2.5, 2.5) * 0.2
    slow_step = 11.5 / SEQLEN
    base_step = jnp.where(fast, 0.05, slow_step) * jnp.exp(noise)
    return jnp.log(jnp.expm1(base_step))


def draw_decay_log(key, part):
    fast = fast_heads(key, 50)
    key = jax.random.fold_in(key, 4)
    jitter = jax.random.uniform(key, (HEADS,), jnp.float32, -0.3, 0.3)
    return jnp.where(fast, jnp.log(0.6), jnp.log(0.06)) + jitter


def draw_step_unshifted(key, part):
    capacity_cells = spike_indices_vector(key)
    key = jax.random.fold_in(key, 5)
    noise_key, block_key = jax.random.split(key)
    noise = jnp.clip(jax.random.normal(noise_key, (HEADS, SEQLEN), jnp.float32), -5.0, 5.0) * 0.5
    level = jax.random.uniform(block_key, (HEADS, SEQLEN // TOK_DEV, 1), jnp.float32, -0.35, 0.35)
    level = jnp.broadcast_to(level, (HEADS, SEQLEN // TOK_DEV, TOK_DEV)).reshape(HEADS, SEQLEN)
    index = jnp.arange(SEQLEN)
    hit = jnp.any(index[None, :] == capacity_cells[:, None], axis=0)
    lift = jnp.log(jnp.expm1(4.0)) - jnp.log(11.5 / SEQLEN)
    return noise + level + jnp.where(hit, lift, 0.0)[None, :]


def draw_filter_entry_array(key, part):
    capacity_cells = spike_indices_vector(key)
    key = jax.random.fold_in(key, 7)
    values = jnp.clip(jax.random.normal(key, (SEQLEN, CONV), jnp.float32), -6.0, 6.0)
    index = jnp.arange(SEQLEN)
    distance = capacity_cells[:, None] - index[None, :]
    near = jnp.any((distance >= 0) & (distance < KERNEL), axis=0)
    column = jnp.arange(CONV) < D
    factor = jnp.where(near[:, None] & column[None, :], 0.025, 1.0)
    return (values * factor).astype(jnp.bfloat16)


def draw_gate_input(key, part):
    key = jax.random.fold_in(key, 8)
    value_key, row_key = jax.random.split(key, 2)
    row_scale = jnp.exp(jax.random.uniform(row_key, (SEQLEN, 1), jnp.float32, jnp.log(0.5), jnp.log(5.0)))
    values = jnp.clip(jax.random.normal(value_key, (SEQLEN, D), jnp.float32), -4.0, 4.0)
    return (values * row_scale).astype(jnp.bfloat16)


def draw_residual(key, part):
    key = jax.random.fold_in(key, 9)
    value_key, row_key = jax.random.split(key, 2)
    row_scale = jnp.exp(jax.random.uniform(row_key, (SEQLEN, 1), jnp.float32, jnp.log(0.3), jnp.log(3.0)))
    values = jnp.clip(jax.random.normal(value_key, (SEQLEN, D), jnp.float32), -4.0, 4.0)
    return (values * row_scale).astype(jnp.bfloat16)


def block_scale(own_key, extent, shards, smallest, high):
    def one(position, blocks):
        steps = jax.random.uniform(jax.random.fold_in(jax.random.fold_in(own_key, 6), position), (blocks,), jnp.float32, smallest / len(shards), high / len(shards))
        return jnp.repeat(jnp.exp(steps), extent[position] // blocks).reshape((-1,) + (1,) * (len(extent) - position - 1))

    gain = one(*shards[0])
    for cut in shards[1:]:
        gain = gain * one(*cut)
    return gain


def deal_out(own_key, own, number, rows, amount, top, reach, lean):
    order = jax.random.permutation(own_key, amount)
    heavy_load, ordinary = shares(amount, rows * top, reach, lean, True), shares(amount, rows * top, reach, lean, False)
    places = jnp.arange(amount)

    def named(tallies, turn):
        used = int((tallies > 0).sum())
        fixed = max(1, used // 4)
        passed = fixed + (places - fixed + turn * (used - fixed)) % max(1, amount - fixed)
        return jnp.zeros((amount,), jnp.int32).at[order[jnp.where(places < fixed, places, passed)]].set(jnp.asarray(tallies, jnp.int32))

    tallies = jnp.where(number % 4 == 0, named(heavy_load, number // 4), named(ordinary, number - number // 4 - 1))
    mixed = jax.random.permutation(jax.random.fold_in(own, 3), amount)
    giver, taker = mixed[0:amount // 2 * 2:2], mixed[1:amount // 2 * 2:2]
    margin = jnp.minimum(tallies[giver] - 1, reach - tallies[taker]) // 2
    margin = jnp.where((giver == order[0]) | (taker == order[0]) | (tallies[taker] == 0), 0, jnp.maximum(margin, 0))
    passed = jax.random.randint(jax.random.fold_in(own, 4), (amount // 2,), 0, 1 << 20) % (margin + 1)
    tallies = tallies.at[giver].add(-passed).at[taker].add(passed)
    members = jnp.searchsorted(jnp.cumsum(tallies), jnp.arange(rows * top), side="right").astype(jnp.int32)
    listing = members.reshape(top, rows).T
    listing = listing[jax.random.permutation(jax.random.fold_in(own, 1), rows)]
    turn = jax.random.randint(jax.random.fold_in(own, 2), (rows, 1), 0, top)
    return jnp.take_along_axis(listing, (jnp.arange(top)[None, :] + turn) % top, axis=1)


def shares(number_of, total, bound, slope, full):
    weights = [(1 << 20) // math.isqrt(rank ** slope) + 1 for rank in range(1, number_of + 1)]
    largest = bound if full else min(bound, max(-(-total // number_of), total * weights[0] // sum(weights)))
    least = 1 if total - largest >= number_of - 1 else 0
    holding, rest = [largest] + [least] * (number_of - 1), total - largest - least * (number_of - 1)
    while rest > 0:
        movable = [i for i in range(1, number_of) if holding[i] < largest] or [i for i in range(1, number_of) if holding[i] < bound]
        mass, remaining = sum([weights[i] for i in movable]), rest
        for i in movable:
            addition = min(bound - holding[i], max(1, remaining * weights[i] // mass), rest)
            holding[i] = holding[i] + addition
            rest = rest - addition
    return np.array(holding)


def normal_values(stream_key, extent, width, reach, cuts=(), kind=jnp.bfloat16):
    values = jax.random.normal(stream_key, extent, jnp.float32) * width
    if len(cuts) > 0:
        values = block_scale(stream_key, extent, cuts, -0.22, 0.18) * values
    return jnp.clip(values, min=-reach, max=reach).astype(kind)


def setup_inputs(seed: int = 0) -> dict:
    seeds = jax.random.split(jax.random.key(seed), 17)
    filter_entry_array = draw_filter_entry_array(jax.random.fold_in(seeds[16], 71), 0)
    gate_input = draw_gate_input(jax.random.fold_in(seeds[16], 71), 0)
    step_unshifted = draw_step_unshifted(jax.random.fold_in(seeds[16], 71), 0)
    step_bias = draw_step_bias(jax.random.fold_in(seeds[16], 71), 0)
    decay_log = draw_decay_log(jax.random.fold_in(seeds[16], 71), 0)
    conv_weight = normal_values(seeds[5], (KERNEL, CONV), KERNEL ** -0.5, 3.0, (), jnp.float32)
    conv_bias = normal_values(seeds[6], (CONV,), 0.2, 3.0, (), jnp.float32)
    skip_gain = jnp.clip(jax.random.uniform(seeds[7], (HEADS,), jnp.float32, 0.5, 1.5), 0.5, 1.5)
    mixer_gain = jnp.clip(1.0 + 0.15 * jax.random.normal(seeds[8], (D,), jnp.float32), 0.25, 1.75)
    residual = draw_residual(jax.random.fold_in(seeds[16], 71), 0)
    expert_norm = jnp.clip(1.0 + 0.15 * jax.random.normal(seeds[10], (D,), jnp.float32), 0.25, 1.75)
    router_weight = normal_values(seeds[11], (D, EXPERTS), (D // 4) ** -0.5, 0.25)
    expert_ids_keys = jax.random.split(jax.random.fold_in(seeds[12], 1), SEQLEN // TOK_DEV)
    expert_ids_turns = jax.random.permutation(jax.random.fold_in(seeds[12], 3), SEQLEN // TOK_DEV)
    expert_ids = jax.vmap(lambda own, number: deal_out(jax.random.fold_in(seeds[12], 2), own, number, TOK_DEV, EXPERTS, TOPK, CAP, 2))(expert_ids_keys, expert_ids_turns).reshape((SEQLEN, TOPK))
    w_gate = normal_values(seeds[13], (EXPERTS, D, FF), D ** -0.5, 0.125, ((0, 32),))
    w_up = normal_values(seeds[14], (EXPERTS, D, FF), D ** -0.5, 0.125, ((0, 32),))
    w_down = normal_values(seeds[15], (EXPERTS, FF, D), FF ** -0.5, 0.21875, ((0, 32),))
    return {"filter_entry_array": filter_entry_array, "gate_input": gate_input, "step_unshifted": step_unshifted, "step_bias": step_bias, "decay_log": decay_log, "conv_weight": conv_weight, "conv_bias": conv_bias, "skip_gain": skip_gain, "mixer_gain": mixer_gain, "residual": residual, "expert_norm": expert_norm, "router_weight": router_weight, "expert_ids": expert_ids, "w_gate": w_gate, "w_up": w_up, "w_down": w_down}


EXACT = lax.Precision.HIGHEST

def conv_silu(padded, conv_weight, conv_bias, length):
    summed = jnp.zeros((length, padded.shape[1]), jnp.float32) + conv_bias[None, :]
    for offset in range(KERNEL):
        summed = summed + conv_weight[offset][None, :] * padded[offset:offset + length]
    return jax.nn.silu(summed).astype(jnp.bfloat16)

def block_terms(x_block, input_map, output_map, increment_tile, decay_rate):
    count = x_block.shape[0]
    cum_log = jnp.cumsum(-increment_tile * decay_rate[:, None], axis=1)
    capacity_cells = jnp.arange(count)
    causal = capacity_cells[:, None] >= capacity_cells[None, :]
    gap_log = jnp.where(causal[None], cum_log[:, :, None] - cum_log[:, None, :], 0.0)
    inside_offset = jnp.where(causal[None], jnp.exp(gap_log), 0.0)
    cross_gram = jnp.dot(output_map, input_map.T, preferred_element_type=jnp.float32)
    mixing = inside_offset * cross_gram[None] * increment_tile[:, None, :]
    head_view = x_block.astype(jnp.float32).reshape(count, HEADS, HEAD_DIM)
    inner_y = jnp.einsum('hts,shp->thp', mixing, head_view, precision=EXACT)
    tail_w = jnp.exp(cum_log[:, -1:] - cum_log) * increment_tile
    weighted = head_view * tail_w.T[:, :, None]
    state_local = jnp.einsum('shp,sn->hpn', weighted, input_map.astype(jnp.float32), precision=EXACT)
    return (inner_y, jnp.exp(cum_log), state_local, jnp.exp(cum_log[:, -1]), head_view)

def reference(filter_entry_array, gate_input, step_unshifted, step_bias, decay_log, conv_weight, conv_bias, skip_gain, mixer_gain, residual, expert_norm, router_weight, expert_ids, w_gate, w_up, w_down):
    length = filter_entry_array.shape[0]
    zero_rows = jnp.zeros((KERNEL - 1, filter_entry_array.shape[1]), jnp.float32)
    padded = jnp.concatenate([zero_rows, filter_entry_array.astype(jnp.float32)], axis=0)
    filter_result_array = conv_silu(padded, conv_weight, conv_bias, length)
    step_size = jax.nn.softplus(step_unshifted + step_bias[:, None])
    decay_rate = jnp.exp(decay_log)
    blocks = length // TOK_DEV
    x_all = filter_result_array[:, :D].reshape(blocks, TOK_DEV, D)
    in_all = filter_result_array[:, D:D + STATE].reshape(blocks, TOK_DEV, STATE)
    output_gathered = filter_result_array[:, D + STATE:].reshape(blocks, TOK_DEV, STATE)
    step_all = step_size.reshape(HEADS, blocks, TOK_DEV).transpose(1, 0, 2)

    def advance(state_in, inputs):
        x_block, input_map, output_map, increment_tile = inputs
        inner_y, entry_w, state_local, through, head_view = block_terms(x_block, input_map, output_map, increment_tile, decay_rate)
        carried = entry_w.T[:, :, None] * jnp.einsum('tn,hpn->thp', output_map.astype(jnp.float32), state_in, precision=EXACT)
        direct = skip_gain[None, :, None] * head_view
        result = (inner_y + carried + direct).reshape(TOK_DEV, D)
        return (through[:, None, None] * state_in + state_local, result)
    start_state = jnp.zeros((HEADS, HEAD_DIM, STATE), jnp.float32)
    _, outputs_y = lax.scan(advance, start_state, (x_all, in_all, output_gathered, step_all))
    ssm_out = outputs_y.reshape(length, D)
    gated = ssm_out * jax.nn.silu(gate_input.astype(jnp.float32))
    mixer_out = gated * lax.rsqrt(lax.optimization_barrier(jnp.mean(gated * gated, axis=-1, keepdims=True)) + 1e-05) * mixer_gain[None, :]
    hidden_state = (residual.astype(jnp.float32) + mixer_out).astype(jnp.bfloat16)
    hidden_features = hidden_state.astype(jnp.float32)
    normed = (hidden_features * lax.rsqrt(lax.optimization_barrier(jnp.mean(hidden_features * hidden_features, axis=-1, keepdims=True)) + 1e-05) * expert_norm[None, :]).astype(jnp.bfloat16)
    logits = jnp.dot(normed, router_weight, preferred_element_type=jnp.float32)
    score = jax.nn.sigmoid(jnp.take_along_axis(logits, expert_ids, axis=1))
    gates = score / lax.optimization_barrier(jnp.sum(score, axis=1, keepdims=True))
    pair_count = length * TOPK
    flat_ids = expert_ids.reshape(pair_count)
    one_hot = (flat_ids[:, None] == jnp.arange(EXPERTS, dtype=jnp.int32)[None, :]).astype(jnp.int32)
    rank_in = lax.optimization_barrier(jnp.sum((jnp.cumsum(one_hot, axis=0) - one_hot) * one_hot, axis=1)).astype(jnp.int32)
    limit = blocks * CAP
    pair_index = jnp.arange(pair_count, dtype=jnp.int32)
    slot_table = jnp.zeros((EXPERTS, limit), jnp.int32).at[flat_ids, rank_in].set(pair_index)
    filled = jnp.zeros((EXPERTS, limit), jnp.float32).at[flat_ids, rank_in].set(1.0)
    flat_gates = gates.reshape(pair_count)

    def expert_step(summed, inputs):
        slots, live_mask, gate_projection, up_matrix, down_matrix = inputs
        resident_words = (slots // TOPK).astype(jnp.int32)
        picked = normed[resident_words]
        gate_val = jnp.dot(picked, gate_projection, preferred_element_type=jnp.float32)
        up_val = jnp.dot(picked, up_matrix, preferred_element_type=jnp.float32)
        activated = (jax.nn.silu(gate_val) * up_val).astype(jnp.bfloat16)
        produced = jnp.dot(activated, down_matrix, preferred_element_type=jnp.float32).astype(jnp.bfloat16)
        weight = flat_gates[slots] * live_mask
        return (summed.at[resident_words].add(weight[:, None] * produced.astype(jnp.float32)), None)
    start_sum = jnp.zeros((length, D), jnp.float32)
    summed, _ = lax.scan(expert_step, start_sum, (slot_table, filled, w_gate, w_up, w_down))
    return (hidden_features + summed).astype(jnp.bfloat16)
```

```python
import jax
import jax.numpy as jnp
from jax import lax
from jax.sharding import PartitionSpec as P

D = 2048
HEADS = 32
HEAD_DIM = 64
STATE = 64
KERNEL = 4
TOPK = 8
CAP = 40


EXACT = lax.Precision.HIGHEST


def from_behind(block, axis, distance):
    devices = range(lax.axis_size(axis))
    route = [(i - distance, i) for i in devices if i - distance in devices]
    return lax.ppermute(block, axis, route)


def prefix(state_local, log_through):
    axes = ("ctx", "exp")
    devices = lax.axis_size(axes)
    share = HEADS * HEAD_DIM * STATE // devices
    per_head = devices // HEADS
    pieces = state_local.reshape(devices, share)
    logs = jnp.repeat(log_through, per_head)[:, None]
    packed = jnp.concatenate([pieces, jnp.broadcast_to(logs, (devices, 128))], axis=1)
    arrived = lax.all_to_all(packed, axes, split_axis=0, concat_axis=0, tiled=True)
    states, log = arrived[:, :share], arrived[:, share]
    place = jnp.arange(devices)
    lower = place[:, None] > place[None, :]
    gap = jnp.dot(
        jnp.where(lower, log[None, :], 0.0), lower.astype(jnp.float32), precision=EXACT
    )
    weight = jnp.where(lower, jnp.exp(jnp.minimum(gap, 0.0)), 0.0)
    before = jnp.dot(weight, states, precision=EXACT)
    back = lax.all_to_all(before, axes, split_axis=0, concat_axis=0, tiled=True)
    return back.reshape(HEADS, HEAD_DIM, STATE)


def block_terms(x_block, input_map, output_map, increment_tile, decay_rate):
    count = x_block.shape[0]
    cum_log = jnp.cumsum(-increment_tile * decay_rate[:, None], axis=1)
    capacity_cells = jnp.arange(count)
    causal = capacity_cells[:, None] >= capacity_cells[None, :]
    gap_log = jnp.where(causal[None], cum_log[:, :, None] - cum_log[:, None, :], 0.0)
    inside_offset = jnp.where(causal[None], jnp.exp(gap_log), 0.0)
    cross_gram = jnp.dot(output_map, input_map.T, preferred_element_type=jnp.float32)
    mixing = inside_offset * cross_gram[None] * increment_tile[:, None, :]
    head_view = x_block.astype(jnp.float32).reshape(count, HEADS, HEAD_DIM)
    inner_y = jnp.einsum("hts,shp->thp", mixing, head_view, precision=EXACT)
    tail_w = jnp.exp(cum_log[:, -1:] - cum_log) * increment_tile
    weighted = head_view * tail_w.T[:, :, None]
    state_local = jnp.einsum(
        "shp,sn->hpn", weighted, input_map.astype(jnp.float32), precision=EXACT
    )
    return (inner_y, jnp.exp(cum_log), state_local, cum_log[:, -1], head_view)


def body(
    filter_entry_array,
    gate_input,
    step_unshifted,
    step_bias,
    decay_log,
    conv_weight,
    conv_bias,
    skip_gain,
    mixer_gain,
    residual,
    expert_norm,
    router_weight,
    expert_ids,
    w_gate,
    w_up,
    w_down,
):
    row_count = filter_entry_array.shape[0]
    rim_rows = from_behind(filter_entry_array[row_count - (KERNEL - 1) :], ("ctx", "exp"), 1)
    padded = jnp.concatenate([rim_rows, filter_entry_array], axis=0).astype(jnp.float32)
    summed = jnp.zeros((row_count, padded.shape[1]), jnp.float32) + conv_bias[None, :]
    for offset in range(KERNEL):
        summed = summed + conv_weight[offset][None, :] * padded[offset : offset + row_count]
    filter_result_array = jax.nn.silu(summed).astype(jnp.bfloat16)
    x_block = filter_result_array[:, :D]
    input_map = filter_result_array[:, D : D + STATE]
    output_map = filter_result_array[:, D + STATE :]
    step_size = jax.nn.softplus(step_unshifted + step_bias[:, None])
    decay_rate = jnp.exp(decay_log)
    inner_y, entry_w, state_local, through, head_view = block_terms(
        x_block, input_map, output_map, step_size, decay_rate
    )
    before = prefix(state_local, through)
    carried = entry_w.T[:, :, None] * jnp.einsum(
        "tn,hpn->thp", output_map.astype(jnp.float32), before, precision=EXACT
    )
    direct = skip_gain[None, :, None] * head_view
    ssm_out = (inner_y + carried + direct).reshape(row_count, D)
    gated = ssm_out * jax.nn.silu(gate_input.astype(jnp.float32))
    mixer_out = (
        gated
        * lax.rsqrt(jnp.mean(gated * gated, axis=-1, keepdims=True) + 1e-05)
        * mixer_gain[None, :]
    )
    hidden_state = (residual.astype(jnp.float32) + mixer_out).astype(jnp.bfloat16)
    hidden_features = hidden_state.astype(jnp.float32)
    normed = (
        hidden_features
        * lax.rsqrt(jnp.mean(hidden_features * hidden_features, axis=-1, keepdims=True) + 1e-05)
        * expert_norm[None, :]
    ).astype(jnp.bfloat16)
    logits = jnp.dot(normed, router_weight, preferred_element_type=jnp.float32)
    score = jax.nn.sigmoid(jnp.take_along_axis(logits, expert_ids, axis=1))
    gates = score / jnp.sum(score, axis=1, keepdims=True)
    local_experts = w_gate.shape[0]
    sources = lax.axis_size("ctx")
    experts_all = local_experts * sources
    pair_count = row_count * TOPK
    flat_ids = expert_ids.reshape(pair_count)
    one_hot = (flat_ids[:, None] == jnp.arange(experts_all, dtype=jnp.int32)[None, :]).astype(
        jnp.int32
    )
    slot_of = jnp.sum((jnp.cumsum(one_hot, axis=0) - one_hot) * one_hot, axis=1)
    destination = flat_ids * CAP + slot_of
    repeated = jnp.broadcast_to(normed[:, None, :], (row_count, TOPK, D)).reshape(pair_count, D)
    outgoing = jnp.zeros((experts_all * CAP, D), jnp.bfloat16).at[destination].set(repeated)
    outgoing = outgoing.reshape(experts_all, CAP, D)
    arrived = lax.all_to_all(outgoing, "ctx", split_axis=0, concat_axis=0, tiled=True)
    slot_count = arrived.shape[1]
    grouped = arrived.reshape(sources, local_experts, slot_count, D)
    gate_val = jnp.einsum("sekd,edf->sekf", grouped, w_gate, preferred_element_type=jnp.float32)
    up_val = jnp.einsum("sekd,edf->sekf", grouped, w_up, preferred_element_type=jnp.float32)
    activated = (jax.nn.silu(gate_val) * up_val).astype(jnp.bfloat16)
    produced = jnp.einsum(
        "sekf,efd->sekd", activated, w_down, preferred_element_type=jnp.float32
    ).astype(jnp.bfloat16)
    returned = lax.all_to_all(
        produced.reshape(sources * local_experts, slot_count, D),
        "ctx",
        split_axis=0,
        concat_axis=0,
        tiled=True,
    )
    picked = (
        returned.reshape(experts_all * CAP, D)[destination]
        .astype(jnp.float32)
        .reshape(row_count, TOPK, D)
    )
    expert_sum = jnp.sum(gates[:, :, None] * picked, axis=1)
    return (hidden_features + expert_sum).astype(jnp.bfloat16)


def solution(mesh):
    return jax.shard_map(
        body,
        mesh=mesh,
        in_specs=(
            P(("ctx", "exp"), None),
            P(("ctx", "exp"), None),
            P(None, ("ctx", "exp")),
            P(),
            P(),
            P(),
            P(),
            P(),
            P(),
            P(("ctx", "exp"), None),
            P(),
            P(),
            P(("ctx", "exp"), None),
            P("ctx", None, None),
            P("ctx", None, None),
            P("ctx", None, None),
        ),
        out_specs=P(("ctx", "exp"), None),
        check_vma=False,
    )
```

```python
import jax
import jax.numpy as jnp
from jax import lax
from jax.experimental import pallas as pl
from jax.experimental.pallas import tpu as pltpu
from jax.sharding import PartitionSpec as P

D = 2048
HEADS = 32
HEAD_DIM = 64
STATE = 64
KERNEL = 4
TOPK = 8
CAP = 40


EXACT = lax.Precision.HIGHEST


def from_behind(block, axis, distance):
    devices = range(lax.axis_size(axis))
    route = [(i - distance, i) for i in devices if i - distance in devices]
    return lax.ppermute(block, axis, route)


def prefix(state_local, log_through):
    axes = ("ctx", "exp")
    devices = lax.axis_size(axes)
    share = HEADS * HEAD_DIM * STATE // devices
    per_head = devices // HEADS
    pieces = state_local.reshape(devices, share)
    logs = jnp.repeat(log_through, per_head)[:, None]
    packed = jnp.concatenate([pieces, jnp.broadcast_to(logs, (devices, 128))], axis=1)
    arrived = lax.all_to_all(packed, axes, split_axis=0, concat_axis=0, tiled=True)
    states, log = arrived[:, :share], arrived[:, share]
    place = jnp.arange(devices)
    lower = place[:, None] > place[None, :]
    gap = jnp.dot(
        jnp.where(lower, log[None, :], 0.0), lower.astype(jnp.float32), precision=EXACT
    )
    weight = jnp.where(lower, jnp.exp(jnp.minimum(gap, 0.0)), 0.0)
    before = jnp.dot(weight, states, precision=EXACT)
    back = lax.all_to_all(before, axes, split_axis=0, concat_axis=0, tiled=True)
    return back.reshape(HEADS, HEAD_DIM, STATE)


def block_terms(x_block, input_map, output_map, increment_tile, decay_rate):
    count = x_block.shape[0]
    cum_log = jnp.cumsum(-increment_tile * decay_rate[:, None], axis=1)
    capacity_cells = jnp.arange(count)
    causal = capacity_cells[:, None] >= capacity_cells[None, :]
    gap_log = jnp.where(causal[None], cum_log[:, :, None] - cum_log[:, None, :], 0.0)
    inside_offset = jnp.where(causal[None], jnp.exp(gap_log), 0.0)
    cross_gram = jnp.dot(output_map, input_map.T, preferred_element_type=jnp.float32)
    mixing = inside_offset * cross_gram[None] * increment_tile[:, None, :]
    head_view = x_block.astype(jnp.float32).reshape(count, HEADS, HEAD_DIM)
    inner_y = jnp.einsum("hts,shp->thp", mixing, head_view, precision=EXACT)
    tail_w = jnp.exp(cum_log[:, -1:] - cum_log) * increment_tile
    weighted = head_view * tail_w.T[:, :, None]
    state_local = jnp.einsum(
        "shp,sn->hpn", weighted, input_map.astype(jnp.float32), precision=EXACT
    )
    return (inner_y, jnp.exp(cum_log), state_local, cum_log[:, -1], head_view)


MESH = pl.DeviceIdType.MESH
BLOCK = 128
PICK = 4 * CAP
WIDE = 4 * BLOCK


def moe_kernel(
    normed,
    gates,
    hidden,
    w_gate,
    w_up,
    w_down,
    out,
    rows,
    meta,
    wg,
    wu,
    wd,
    picked,
    lent,
    activated,
    own_y,
    lent_y,
    back_y,
    select,
    gate_col,
    part,
    land,
    w_sem,
    row_send,
    row_recv,
    meta_send,
    meta_recv,
    lent_send,
    lent_recv,
    back_send,
    back_recv,
    sum_send,
    sum_recv,
):
    ctx = lax.axis_index("ctx")
    depth = lax.axis_index("exp")
    core = ctx % 2
    x = (ctx // 2) % 4
    y = ctx // 8
    sibling = ctx + 1 - 2 * core

    def device(first, second):
        to_y = (y + core * first + (1 - core) * second + 4) % 4
        to_x = (x + core * second + (1 - core) * first + 4) % 4
        return ((to_y * 4 + to_x) * 2 + core, depth)

    forth = (device(1, 0), device(0, 1))
    back = (device(-1, 0), device(0, -1))
    across = (sibling, depth)

    fetch = [
        pltpu.make_async_copy(src.at[0], dst, w_sem.at[i])
        for i, (src, dst) in enumerate(((w_gate, wg), (w_up, wu), (w_down, wd)))
    ]
    for copy in fetch:
        copy.start()

    barrier = pltpu.get_barrier_semaphore()
    partners = (*forth, *back, across)
    for partner in partners:
        pl.semaphore_signal(barrier, inc=1, device_id=partner, device_id_type=MESH)

    rows[0:BLOCK] = normed[...]
    meta[0] = gates[...]
    pl.semaphore_wait(barrier, len(partners))

    def remote(src, dst, send, recv, to):
        return pltpu.make_async_remote_copy(
            src_ref=src, dst_ref=dst, send_sem=send, recv_sem=recv, device_id=to, device_id_type=MESH
        )

    def ring(stage):
        return (0, 4, 0) if stage == 0 else (4 * (stage - 1), 1, 1)

    def row_copy(stage, kind):
        base, stride, axis = ring(stage)
        sem = 4 * stage + kind
        to = (forth, back)[kind % 2][axis]
        source, target, low, count = (
            (0, 1, 0, BLOCK),
            (0, 3, 0, BLOCK),
            (1, 2, 0, BLOCK // 2),
            (3, 2, BLOCK // 2, BLOCK // 2),
        )[kind]
        return remote(
            rows.at[pl.ds((base + stride * source) * BLOCK + low, count)],
            rows.at[pl.ds((base + stride * target) * BLOCK + low, count)],
            row_send.at[sem],
            row_recv.at[sem],
            to,
        )

    def meta_copy(stage, kind):
        base, stride, axis = ring(stage)
        sem = 3 * stage + kind
        source, target, to = ((0, 1, forth), (0, 3, back), (1, 2, forth))[kind]
        return remote(
            meta.at[base + stride * source],
            meta.at[base + stride * target],
            meta_send.at[sem],
            meta_recv.at[sem],
            to[axis],
        )

    def sum_copy(stage, kind):
        base, stride, axis = ring(stage)
        sem = 4 * stage + kind
        to = (back, forth)[kind % 2][axis]
        source, low, count, place = (
            (2, 0, BLOCK // 2, 0),
            (2, BLOCK // 2, BLOCK // 2, BLOCK // 2),
            (1, 0, BLOCK, BLOCK),
            (3, 0, BLOCK, 2 * BLOCK),
        )[kind]
        return remote(
            part.at[pl.ds((base + stride * source) * BLOCK + low, count)],
            land.at[pl.ds(stage * 3 * BLOCK + place, count)],
            sum_send.at[sem],
            sum_recv.at[sem],
            to,
        )

    def lent_copy(k):
        return remote(
            lent.at[k], picked.at[k, pl.ds(PICK, PICK)], lent_send.at[k], lent_recv.at[k], across
        )

    def back_copy(k):
        return remote(lent_y.at[k], back_y.at[k], back_send.at[k], back_recv.at[k], across)

    def spread(stage):
        for kind in (0, 1):
            meta_copy(stage, kind).start()
            row_copy(stage, kind).start()

    def pass_on(stage, kind):
        row_copy(stage, kind).wait_recv()
        meta_copy(stage, kind).wait_recv()
        if kind == 0:
            meta_copy(stage, 2).start()
        row_copy(stage, kind + 2).start()

    def arrive_last(stage):
        meta_copy(stage, 2).wait_recv()
        row_copy(stage, 2).wait_recv()
        row_copy(stage, 3).wait_recv()

    before = (
        lax.broadcasted_iota(jnp.int32, (BLOCK, BLOCK), 0)
        < lax.broadcasted_iota(jnp.int32, (BLOCK, BLOCK), 1)
    ).astype(jnp.bfloat16)
    slot_row = lax.broadcasted_iota(jnp.int32, (PICK, WIDE), 0).astype(jnp.float32)

    def choose(k):
        gate = jnp.concatenate(
            [
                meta[4 * k + j, pl.ds(expert, 1), :]
                for expert in (ctx, sibling)
                for j in range(4)
            ],
            axis=0,
        )
        live = gate > 0.0
        rank = jnp.dot(
            live.astype(jnp.bfloat16), before, preferred_element_type=jnp.float32
        )
        shift = (lax.broadcasted_iota(jnp.int32, (8, BLOCK), 0) % 4).astype(jnp.float32) * CAP
        slot = jnp.where(live, rank + shift, -1.0)
        for half in range(2):
            lanes = jnp.concatenate([slot[4 * half + j : 4 * half + j + 1] for j in range(4)], axis=1)
            value = jnp.concatenate([gate[4 * half + j : 4 * half + j + 1] for j in range(4)], axis=1)
            hit = slot_row == lanes
            span = pl.ds(half * PICK, PICK)
            select[k, span, :] = jnp.where(hit, 1.0, 0.0).astype(jnp.bfloat16)
            total = jnp.sum(jnp.where(hit, value, 0.0), axis=1, keepdims=True)
            gate_col[k, span, :] = jnp.broadcast_to(total, (PICK, BLOCK))

        @pl.loop(0, 8)
        def _(n):
            cols = pl.ds(pl.multiple_of(n * 256, 256), 256)
            got = jnp.dot(
                select[k], rows[pl.ds(k * WIDE, WIDE), cols], preferred_element_type=jnp.float32
            ).astype(jnp.bfloat16)
            picked[k, pl.ds(0, PICK), cols] = got[:PICK]
            lent[k, :, cols] = got[PICK:]

        lent_copy(k).start()

    def feed(k):
        lent_copy(k).wait_recv()

        @pl.loop(0, 3)
        def _(f):
            cols = pl.ds(pl.multiple_of(f * 256, 256), 256)
            gate = jnp.dot(picked[k], wg[:, cols], preferred_element_type=jnp.float32)
            up = jnp.dot(picked[k], wu[:, cols], preferred_element_type=jnp.float32)
            activated[:, cols] = (gate * jax.nn.sigmoid(gate) * up).astype(jnp.bfloat16)

        @pl.loop(0, 8)
        def _(n):
            cols = pl.ds(pl.multiple_of(n * 256, 256), 256)
            made = jnp.dot(activated[...], wd[:, cols], preferred_element_type=jnp.float32)
            scale = gate_col[k, pl.ds(0, PICK), :]
            own_y[:, cols] = (
                made[:PICK] * jnp.concatenate([scale, scale], axis=1)
            ).astype(jnp.bfloat16)
            lent_y[k, :, cols] = made[PICK:].astype(jnp.bfloat16)

        back_copy(k).start()

    def combine(k):
        back_copy(k).wait_recv()

        @pl.loop(0, 8)
        def _(n):
            cols = pl.ds(pl.multiple_of(n * 256, 256), 256)
            scale = gate_col[k, pl.ds(PICK, PICK), :]
            other = (
                back_y[k, :, cols].astype(jnp.float32) * jnp.concatenate([scale, scale], axis=1)
            ).astype(jnp.bfloat16)
            both = jnp.concatenate([own_y[:, cols], other], axis=0)
            part[pl.ds(k * WIDE, WIDE), cols] = lax.dot_general(
                select[k], both, (((0,), (0,)), ((), ())), preferred_element_type=jnp.float32
            ).astype(jnp.bfloat16)

    def add_into(block, low, count, places):
        @pl.loop(0, count // 16)
        def _(i):
            span = pl.ds(pl.multiple_of(block * BLOCK + low + i * 16, 16), 16)
            total = part[span, :].astype(jnp.float32)
            for place in places:
                total += land[pl.ds(pl.multiple_of(place + i * 16, 16), 16), :].astype(jnp.float32)
            part[span, :] = total.astype(jnp.bfloat16)

    def sum_first(stage):
        sum_copy(stage, 0).start()
        sum_copy(stage, 1).start()

    def sum_second(stage):
        base, stride, _ = ring(stage)
        place = stage * 3 * BLOCK
        sum_copy(stage, 0).wait_recv()
        add_into(base + stride, 0, BLOCK // 2, (place,))
        sum_copy(stage, 2).start()
        sum_copy(stage, 1).wait_recv()
        add_into(base + 3 * stride, BLOCK // 2, BLOCK // 2, (place + BLOCK // 2,))
        sum_copy(stage, 3).start()

    def sum_last(stage):
        base, _, _ = ring(stage)
        place = stage * 3 * BLOCK
        sum_copy(stage, 2).wait_recv()
        sum_copy(stage, 3).wait_recv()
        if stage > 0:
            add_into(base, 0, BLOCK, (place + BLOCK, place + 2 * BLOCK))

    spread(0)
    spread(1)
    pass_on(0, 0)
    spread(2)
    pass_on(0, 1)
    spread(4)
    pass_on(1, 0)
    pass_on(1, 1)
    arrive_last(0)
    spread(3)
    arrive_last(1)
    choose(0)
    pass_on(2, 0)
    pass_on(2, 1)
    for copy in fetch:
        copy.wait()
    feed(0)
    pass_on(4, 0)
    pass_on(4, 1)
    arrive_last(2)
    choose(1)
    combine(0)
    sum_first(1)
    feed(1)
    pass_on(3, 0)
    pass_on(3, 1)
    arrive_last(4)
    choose(3)
    combine(1)
    sum_first(2)
    sum_second(1)
    feed(3)
    sum_last(1)
    sum_second(2)
    arrive_last(3)
    choose(2)
    combine(3)
    sum_first(4)
    feed(2)
    sum_last(2)
    sum_second(4)
    combine(2)
    sum_first(3)
    sum_last(4)
    sum_second(3)
    sum_last(3)
    sum_first(0)
    sum_second(0)
    sum_last(0)

    @pl.loop(0, BLOCK // 16)
    def _(i):
        span = pl.ds(pl.multiple_of(i * 16, 16), 16)
        total = part[span, :].astype(jnp.float32)
        for place in (BLOCK, 2 * BLOCK):
            total += land[pl.ds(pl.multiple_of(place + i * 16, 16), 16), :].astype(jnp.float32)
        out[span, :] = (hidden[span, :].astype(jnp.float32) + total).astype(jnp.bfloat16)

    for stage in range(5):
        for kind in range(4):
            row_copy(stage, kind).wait_send()
            sum_copy(stage, kind).wait_send()
        for kind in range(3):
            meta_copy(stage, kind).wait_send()
    for k in range(4):
        lent_copy(k).wait_send()
        back_copy(k).wait_send()


def experts(normed, gates, hidden, w_gate, w_up, w_down):
    ff = w_gate.shape[2]
    bf16 = jnp.bfloat16
    vmem = pl.BlockSpec(memory_space=pltpu.VMEM)
    hbm = pl.BlockSpec(memory_space=pl.ANY)
    dma = pltpu.SemaphoreType.DMA
    return pl.pallas_call(
        moe_kernel,
        out_shape=jax.ShapeDtypeStruct((BLOCK, D), bf16),
        in_specs=[vmem, vmem, vmem, hbm, hbm, hbm],
        out_specs=vmem,
        scratch_shapes=[
            pltpu.VMEM((16 * BLOCK, D), bf16),
            pltpu.VMEM((16, 32, BLOCK), jnp.float32),
            pltpu.VMEM((D, ff), bf16),
            pltpu.VMEM((D, ff), bf16),
            pltpu.VMEM((ff, D), bf16),
            pltpu.VMEM((4, 2 * PICK, D), bf16),
            pltpu.VMEM((4, PICK, D), bf16),
            pltpu.VMEM((2 * PICK, ff), bf16),
            pltpu.VMEM((PICK, D), bf16),
            pltpu.VMEM((4, PICK, D), bf16),
            pltpu.VMEM((4, PICK, D), bf16),
            pltpu.VMEM((4, 2 * PICK, WIDE), bf16),
            pltpu.VMEM((4, 2 * PICK, BLOCK), jnp.float32),
            pltpu.VMEM((16 * BLOCK, D), bf16),
            pltpu.VMEM((15 * BLOCK, D), bf16),
            dma((3,)),
            dma((20,)),
            dma((20,)),
            dma((15,)),
            dma((15,)),
            dma((4,)),
            dma((4,)),
            dma((4,)),
            dma((4,)),
            dma((20,)),
            dma((20,)),
        ],
        compiler_params=pltpu.CompilerParams(
            collective_id=0, has_side_effects=True, vmem_limit_bytes=60 * 1024 * 1024
        ),
        cost_estimate=pl.CostEstimate(
            flops=2 * 1280 * 3 * D * ff, bytes_accessed=3 * D * ff * 2, transcendentals=1280 * ff
        ),
    )(normed, gates, hidden, w_gate, w_up, w_down)


def body(
    filter_entry_array,
    gate_input,
    step_unshifted,
    step_bias,
    decay_log,
    conv_weight,
    conv_bias,
    skip_gain,
    mixer_gain,
    residual,
    expert_norm,
    router_weight,
    expert_ids,
    w_gate,
    w_up,
    w_down,
):
    row_count = filter_entry_array.shape[0]
    rim_rows = from_behind(filter_entry_array[row_count - (KERNEL - 1) :], ("ctx", "exp"), 1)
    padded = jnp.concatenate([rim_rows, filter_entry_array], axis=0).astype(jnp.float32)
    summed = jnp.zeros((row_count, padded.shape[1]), jnp.float32) + conv_bias[None, :]
    for offset in range(KERNEL):
        summed = summed + conv_weight[offset][None, :] * padded[offset : offset + row_count]
    filter_result_array = jax.nn.silu(summed).astype(jnp.bfloat16)
    x_block = filter_result_array[:, :D]
    input_map = filter_result_array[:, D : D + STATE]
    output_map = filter_result_array[:, D + STATE :]
    step_size = jax.nn.softplus(step_unshifted + step_bias[:, None])
    decay_rate = jnp.exp(decay_log)
    inner_y, entry_w, state_local, through, head_view = block_terms(
        x_block, input_map, output_map, step_size, decay_rate
    )
    before = prefix(state_local, through)
    carried = entry_w.T[:, :, None] * jnp.einsum(
        "tn,hpn->thp", output_map.astype(jnp.float32), before, precision=EXACT
    )
    direct = skip_gain[None, :, None] * head_view
    ssm_out = (inner_y + carried + direct).reshape(row_count, D)
    gated = ssm_out * jax.nn.silu(gate_input.astype(jnp.float32))
    mixer_out = (
        gated
        * lax.rsqrt(jnp.mean(gated * gated, axis=-1, keepdims=True) + 1e-05)
        * mixer_gain[None, :]
    )
    hidden_state = (residual.astype(jnp.float32) + mixer_out).astype(jnp.bfloat16)
    hidden_features = hidden_state.astype(jnp.float32)
    normed = (
        hidden_features
        * lax.rsqrt(jnp.mean(hidden_features * hidden_features, axis=-1, keepdims=True) + 1e-05)
        * expert_norm[None, :]
    ).astype(jnp.bfloat16)
    logits = jnp.dot(normed, router_weight, preferred_element_type=jnp.float32)
    experts_all = router_weight.shape[1]
    chosen = jnp.any(
        expert_ids[:, :, None] == jnp.arange(experts_all, dtype=jnp.int32)[None, None, :], axis=1
    )
    score = jnp.where(chosen, jax.nn.sigmoid(logits), 0.0)
    gates = score / jnp.sum(score, axis=1, keepdims=True)
    return experts(normed, gates.T, hidden_state, w_gate, w_up, w_down)


def solution(mesh):
    return jax.shard_map(
        body,
        mesh=mesh,
        in_specs=(
            P(("ctx", "exp"), None),
            P(("ctx", "exp"), None),
            P(None, ("ctx", "exp")),
            P(),
            P(),
            P(),
            P(),
            P(),
            P(),
            P(("ctx", "exp"), None),
            P(),
            P(),
            P(("ctx", "exp"), None),
            P("ctx", None, None),
            P("ctx", None, None),
            P("ctx", None, None),
        ),
        out_specs=P(("ctx", "exp"), None),
        check_vma=False,
    )
```

```python
import jax
import jax.numpy as jnp
from jax import lax
from jax.experimental import pallas as pl
from jax.experimental.pallas import tpu as pltpu
from jax.sharding import PartitionSpec as P

D = 2048
HEADS = 32
HEAD_DIM = 64
STATE = 64
KERNEL = 4
TOPK = 8
CAP = 40
CONV = 2176


EXACT = lax.Precision.HIGHEST


MESH = pl.DeviceIdType.MESH
BLOCK = 128
PICK = 4 * CAP
WIDE = 4 * BLOCK


def moe_kernel(
    normed,
    gates,
    hidden,
    w_gate,
    w_up,
    w_down,
    out,
    rows,
    meta,
    wg,
    wu,
    wd,
    picked,
    lent,
    activated,
    own_y,
    lent_y,
    back_y,
    select,
    gate_col,
    part,
    land,
    w_sem,
    row_send,
    row_recv,
    meta_send,
    meta_recv,
    lent_send,
    lent_recv,
    back_send,
    back_recv,
    sum_send,
    sum_recv,
):
    ctx = lax.axis_index("ctx")
    depth = lax.axis_index("exp")
    core = ctx % 2
    x = (ctx // 2) % 4
    y = ctx // 8
    sibling = ctx + 1 - 2 * core

    def device(first, second):
        to_y = (y + core * first + (1 - core) * second + 4) % 4
        to_x = (x + core * second + (1 - core) * first + 4) % 4
        return ((to_y * 4 + to_x) * 2 + core, depth)

    forth = (device(1, 0), device(0, 1))
    back = (device(-1, 0), device(0, -1))
    across = (sibling, depth)

    fetch = [
        pltpu.make_async_copy(src.at[0], dst, w_sem.at[i])
        for i, (src, dst) in enumerate(((w_gate, wg), (w_up, wu), (w_down, wd)))
    ]
    for copy in fetch:
        copy.start()

    barrier = pltpu.get_barrier_semaphore()
    partners = (*forth, *back, across)
    for partner in partners:
        pl.semaphore_signal(barrier, inc=1, device_id=partner, device_id_type=MESH)

    rows[0:BLOCK] = normed[...]
    meta[0] = gates[...]
    pl.semaphore_wait(barrier, len(partners))

    def remote(src, dst, send, recv, to):
        return pltpu.make_async_remote_copy(
            src_ref=src, dst_ref=dst, send_sem=send, recv_sem=recv, device_id=to, device_id_type=MESH
        )

    def ring(stage):
        return (0, 4, 0) if stage == 0 else (4 * (stage - 1), 1, 1)

    def row_copy(stage, kind):
        base, stride, axis = ring(stage)
        sem = 4 * stage + kind
        to = (forth, back)[kind % 2][axis]
        source, target, low, count = (
            (0, 1, 0, BLOCK),
            (0, 3, 0, BLOCK),
            (1, 2, 0, BLOCK // 2),
            (3, 2, BLOCK // 2, BLOCK // 2),
        )[kind]
        return remote(
            rows.at[pl.ds((base + stride * source) * BLOCK + low, count)],
            rows.at[pl.ds((base + stride * target) * BLOCK + low, count)],
            row_send.at[sem],
            row_recv.at[sem],
            to,
        )

    def meta_copy(stage, kind):
        base, stride, axis = ring(stage)
        sem = 3 * stage + kind
        source, target, to = ((0, 1, forth), (0, 3, back), (1, 2, forth))[kind]
        return remote(
            meta.at[base + stride * source],
            meta.at[base + stride * target],
            meta_send.at[sem],
            meta_recv.at[sem],
            to[axis],
        )

    def sum_copy(stage, kind):
        base, stride, axis = ring(stage)
        sem = 4 * stage + kind
        to = (back, forth)[kind % 2][axis]
        source, low, count, place = (
            (2, 0, BLOCK // 2, 0),
            (2, BLOCK // 2, BLOCK // 2, BLOCK // 2),
            (1, 0, BLOCK, BLOCK),
            (3, 0, BLOCK, 2 * BLOCK),
        )[kind]
        return remote(
            part.at[pl.ds((base + stride * source) * BLOCK + low, count)],
            land.at[pl.ds(stage * 3 * BLOCK + place, count)],
            sum_send.at[sem],
            sum_recv.at[sem],
            to,
        )

    def lent_copy(k):
        return remote(
            lent.at[k], picked.at[k, pl.ds(PICK, PICK)], lent_send.at[k], lent_recv.at[k], across
        )

    def back_copy(k):
        return remote(lent_y.at[k], back_y.at[k], back_send.at[k], back_recv.at[k], across)

    def spread(stage):
        for kind in (0, 1):
            meta_copy(stage, kind).start()
            row_copy(stage, kind).start()

    def pass_on(stage, kind):
        row_copy(stage, kind).wait_recv()
        meta_copy(stage, kind).wait_recv()
        if kind == 0:
            meta_copy(stage, 2).start()
        row_copy(stage, kind + 2).start()

    def arrive_last(stage):
        meta_copy(stage, 2).wait_recv()
        row_copy(stage, 2).wait_recv()
        row_copy(stage, 3).wait_recv()

    before = (
        lax.broadcasted_iota(jnp.int32, (BLOCK, BLOCK), 0)
        < lax.broadcasted_iota(jnp.int32, (BLOCK, BLOCK), 1)
    ).astype(jnp.bfloat16)
    slot_row = lax.broadcasted_iota(jnp.int32, (PICK, WIDE), 0).astype(jnp.float32)

    def choose(k):
        gate = jnp.concatenate(
            [
                meta[4 * k + j, pl.ds(expert, 1), :]
                for expert in (ctx, sibling)
                for j in range(4)
            ],
            axis=0,
        )
        live = gate > 0.0
        rank = jnp.dot(
            live.astype(jnp.bfloat16), before, preferred_element_type=jnp.float32
        )
        shift = (lax.broadcasted_iota(jnp.int32, (8, BLOCK), 0) % 4).astype(jnp.float32) * CAP
        slot = jnp.where(live, rank + shift, -1.0)
        for half in range(2):
            lanes = jnp.concatenate([slot[4 * half + j : 4 * half + j + 1] for j in range(4)], axis=1)
            value = jnp.concatenate([gate[4 * half + j : 4 * half + j + 1] for j in range(4)], axis=1)
            hit = slot_row == lanes
            span = pl.ds(half * PICK, PICK)
            select[k, span, :] = jnp.where(hit, 1.0, 0.0).astype(jnp.bfloat16)
            total = jnp.sum(jnp.where(hit, value, 0.0), axis=1, keepdims=True)
            gate_col[k, span, :] = jnp.broadcast_to(total, (PICK, BLOCK))

        @pl.loop(0, 8)
        def _(n):
            cols = pl.ds(pl.multiple_of(n * 256, 256), 256)
            got = jnp.dot(
                select[k], rows[pl.ds(k * WIDE, WIDE), cols], preferred_element_type=jnp.float32
            ).astype(jnp.bfloat16)
            picked[k, pl.ds(0, PICK), cols] = got[:PICK]
            lent[k, :, cols] = got[PICK:]

        lent_copy(k).start()

    def feed(k):
        lent_copy(k).wait_recv()

        @pl.loop(0, 3)
        def _(f):
            cols = pl.ds(pl.multiple_of(f * 256, 256), 256)
            gate = jnp.dot(picked[k], wg[:, cols], preferred_element_type=jnp.float32)
            up = jnp.dot(picked[k], wu[:, cols], preferred_element_type=jnp.float32)
            activated[:, cols] = (gate * jax.nn.sigmoid(gate) * up).astype(jnp.bfloat16)

        @pl.loop(0, 8)
        def _(n):
            cols = pl.ds(pl.multiple_of(n * 256, 256), 256)
            made = jnp.dot(activated[...], wd[:, cols], preferred_element_type=jnp.float32)
            scale = gate_col[k, pl.ds(0, PICK), :]
            own_y[:, cols] = (
                made[:PICK] * jnp.concatenate([scale, scale], axis=1)
            ).astype(jnp.bfloat16)
            lent_y[k, :, cols] = made[PICK:].astype(jnp.bfloat16)

        back_copy(k).start()

    def combine(k):
        back_copy(k).wait_recv()

        @pl.loop(0, 8)
        def _(n):
            cols = pl.ds(pl.multiple_of(n * 256, 256), 256)
            scale = gate_col[k, pl.ds(PICK, PICK), :]
            other = (
                back_y[k, :, cols].astype(jnp.float32) * jnp.concatenate([scale, scale], axis=1)
            ).astype(jnp.bfloat16)
            both = jnp.concatenate([own_y[:, cols], other], axis=0)
            part[pl.ds(k * WIDE, WIDE), cols] = lax.dot_general(
                select[k], both, (((0,), (0,)), ((), ())), preferred_element_type=jnp.float32
            ).astype(jnp.bfloat16)

    def add_into(block, low, count, places):
        @pl.loop(0, count // 16)
        def _(i):
            span = pl.ds(pl.multiple_of(block * BLOCK + low + i * 16, 16), 16)
            total = part[span, :].astype(jnp.float32)
            for place in places:
                total += land[pl.ds(pl.multiple_of(place + i * 16, 16), 16), :].astype(jnp.float32)
            part[span, :] = total.astype(jnp.bfloat16)

    def sum_first(stage):
        sum_copy(stage, 0).start()
        sum_copy(stage, 1).start()

    def sum_second(stage):
        base, stride, _ = ring(stage)
        place = stage * 3 * BLOCK
        sum_copy(stage, 0).wait_recv()
        add_into(base + stride, 0, BLOCK // 2, (place,))
        sum_copy(stage, 2).start()
        sum_copy(stage, 1).wait_recv()
        add_into(base + 3 * stride, BLOCK // 2, BLOCK // 2, (place + BLOCK // 2,))
        sum_copy(stage, 3).start()

    def sum_last(stage):
        base, _, _ = ring(stage)
        place = stage * 3 * BLOCK
        sum_copy(stage, 2).wait_recv()
        sum_copy(stage, 3).wait_recv()
        if stage > 0:
            add_into(base, 0, BLOCK, (place + BLOCK, place + 2 * BLOCK))

    spread(0)
    spread(1)
    pass_on(0, 0)
    spread(2)
    pass_on(0, 1)
    spread(4)
    pass_on(1, 0)
    pass_on(1, 1)
    arrive_last(0)
    spread(3)
    arrive_last(1)
    choose(0)
    pass_on(2, 0)
    pass_on(2, 1)
    for copy in fetch:
        copy.wait()
    feed(0)
    pass_on(4, 0)
    pass_on(4, 1)
    arrive_last(2)
    choose(1)
    combine(0)
    sum_first(1)
    feed(1)
    pass_on(3, 0)
    pass_on(3, 1)
    arrive_last(4)
    choose(3)
    combine(1)
    sum_first(2)
    sum_second(1)
    feed(3)
    sum_last(1)
    sum_second(2)
    arrive_last(3)
    choose(2)
    combine(3)
    sum_first(4)
    feed(2)
    sum_last(2)
    sum_second(4)
    combine(2)
    sum_first(3)
    sum_last(4)
    sum_second(3)
    sum_last(3)
    sum_first(0)
    sum_second(0)
    sum_last(0)

    @pl.loop(0, BLOCK // 16)
    def _(i):
        span = pl.ds(pl.multiple_of(i * 16, 16), 16)
        total = part[span, :].astype(jnp.float32)
        for place in (BLOCK, 2 * BLOCK):
            total += land[pl.ds(pl.multiple_of(place + i * 16, 16), 16), :].astype(jnp.float32)
        out[span, :] = (hidden[span, :].astype(jnp.float32) + total).astype(jnp.bfloat16)

    for stage in range(5):
        for kind in range(4):
            row_copy(stage, kind).wait_send()
            sum_copy(stage, kind).wait_send()
        for kind in range(3):
            meta_copy(stage, kind).wait_send()
    for k in range(4):
        lent_copy(k).wait_send()
        back_copy(k).wait_send()


def experts(normed, gates, hidden, w_gate, w_up, w_down):
    ff = w_gate.shape[2]
    bf16 = jnp.bfloat16
    vmem = pl.BlockSpec(memory_space=pltpu.VMEM)
    hbm = pl.BlockSpec(memory_space=pl.ANY)
    dma = pltpu.SemaphoreType.DMA
    return pl.pallas_call(
        moe_kernel,
        out_shape=jax.ShapeDtypeStruct((BLOCK, D), bf16),
        in_specs=[vmem, vmem, vmem, hbm, hbm, hbm],
        out_specs=vmem,
        scratch_shapes=[
            pltpu.VMEM((16 * BLOCK, D), bf16),
            pltpu.VMEM((16, 32, BLOCK), jnp.float32),
            pltpu.VMEM((D, ff), bf16),
            pltpu.VMEM((D, ff), bf16),
            pltpu.VMEM((ff, D), bf16),
            pltpu.VMEM((4, 2 * PICK, D), bf16),
            pltpu.VMEM((4, PICK, D), bf16),
            pltpu.VMEM((2 * PICK, ff), bf16),
            pltpu.VMEM((PICK, D), bf16),
            pltpu.VMEM((4, PICK, D), bf16),
            pltpu.VMEM((4, PICK, D), bf16),
            pltpu.VMEM((4, 2 * PICK, WIDE), bf16),
            pltpu.VMEM((4, 2 * PICK, BLOCK), jnp.float32),
            pltpu.VMEM((16 * BLOCK, D), bf16),
            pltpu.VMEM((15 * BLOCK, D), bf16),
            dma((3,)),
            dma((20,)),
            dma((20,)),
            dma((15,)),
            dma((15,)),
            dma((4,)),
            dma((4,)),
            dma((4,)),
            dma((4,)),
            dma((20,)),
            dma((20,)),
        ],
        compiler_params=pltpu.CompilerParams(
            collective_id=0, has_side_effects=True, vmem_limit_bytes=60 * 1024 * 1024
        ),
        cost_estimate=pl.CostEstimate(
            flops=2 * 1280 * 3 * D * ff, bytes_accessed=3 * D * ff * 2, transcendentals=1280 * ff
        ),
    )(normed, gates, hidden, w_gate, w_up, w_down)


COLUMN = 8
TILE = D // COLUMN
FLAT = 16


def sigmoid(value):
    return 1.0 / (1.0 + jnp.exp(-value))


def split(value, count):
    pieces = []
    for _ in range(count):
        piece = value.astype(jnp.bfloat16)
        pieces.append(piece)
        value = value - piece.astype(jnp.float32)
    return jnp.concatenate(pieces, axis=1)


def mixer_kernel(
    entry,
    gate,
    residual,
    step,
    step_bias,
    decay_log,
    taps,
    tap_bias,
    skip,
    mixer_gain,
    expert_norm,
    router,
    ids,
    normed,
    hidden,
    gates,
    padded,
    mixed,
    cum,
    delta,
    cum_cols,
    tail_cols,
    entry_cols,
    last_cols,
    gram,
    piece,
    first,
    earlier,
    earlier_log,
    total,
    second,
    third,
    state,
    inner,
    value,
    halo_send,
    halo_recv,
    first_send,
    first_recv,
    second_send,
    second_recv,
    third_send,
    third_recv,
):
    ctx = lax.axis_index("ctx")
    depth = lax.axis_index("exp")
    core = ctx % 2
    column = ctx // 2
    me = core * 4 + depth
    f32, bf16 = jnp.float32, jnp.bfloat16

    def member(m):
        return (column * 2 + m // 4, m % 4)

    def peer(c):
        return (c * 2 + core, depth)

    last = (me == COLUMN - 1).astype(jnp.int32)
    after = (((column + last) % FLAT) * 2 + ((me + 1) % COLUMN) // 4, (me + 1) % 4)
    initial = (me == 0).astype(jnp.int32)
    ahead = (
        ((column - initial + FLAT) % FLAT) * 2 + ((me + COLUMN - 1) % COLUMN) // 4,
        (me + COLUMN - 1) % 4,
    )

    barrier = pltpu.get_barrier_semaphore()
    for i in range(1, COLUMN):
        pl.semaphore_signal(
            barrier, inc=1, device_id=member((me + i) % COLUMN), device_id_type=MESH
        )
    for i in range(1, FLAT):
        pl.semaphore_signal(
            barrier, inc=1, device_id=peer((column + i) % FLAT), device_id_type=MESH
        )

    @pl.when(me == COLUMN - 1)
    def _():
        pl.semaphore_signal(barrier, inc=1, device_id=after, device_id_type=MESH)

    @pl.when(me == 0)
    def _():
        pl.semaphore_signal(barrier, inc=1, device_id=ahead, device_id_type=MESH)

    padded[16:, :] = entry[...]
    pl.semaphore_wait(barrier, COLUMN + FLAT - 2 + last + initial)

    def remote(src, dst, send, recv, to):
        return pltpu.make_async_remote_copy(
            src_ref=src, dst_ref=dst, send_sem=send, recv_sem=recv, device_id=to, device_id_type=MESH
        )

    halo = remote(
        entry.at[pl.ds(BLOCK - 16, 16)], padded.at[pl.ds(0, 16)], halo_send.at[0], halo_recv.at[0], after
    )
    halo.start()

    row_id = lax.broadcasted_iota(jnp.int32, (BLOCK, BLOCK), 0)
    lane_id = lax.broadcasted_iota(jnp.int32, (BLOCK, BLOCK), 1)
    shifted = step[...] + step_bias[...]
    width = jnp.maximum(shifted, 0.0) + jnp.log1p(jnp.exp(-jnp.abs(shifted)))
    logs = -width * jnp.exp(decay_log[...])
    summed = jnp.dot(
        logs, (row_id <= lane_id).astype(f32), precision=EXACT, preferred_element_type=f32
    )
    cum[...] = summed
    delta[...] = width

    def upright(a):
        return jnp.concatenate([a, jnp.zeros((BLOCK - HEADS, BLOCK), f32)], axis=0).T[:, :HEADS]

    summed_t = upright(summed)
    width_t = upright(width)
    final = summed_t[BLOCK - 1 :, :]
    cum_cols[...] = split(summed_t, 3)
    tail_cols[...] = split(jnp.exp(final - summed_t) * width_t, 2)
    entry_cols[...] = split(jnp.exp(summed_t), 2)
    last_cols[...] = split(jnp.broadcast_to(final, (16, HEADS)), 3)

    def spread(m, copies, per, count):
        head = lax.broadcasted_iota(jnp.int32, (HEADS, count), 0)
        lane = lax.broadcasted_iota(jnp.int32, (HEADS, count), 1)
        one = (head == 4 * m + lane // per).astype(bf16)
        return jnp.concatenate([one] * copies, axis=0)

    halo.wait_recv()
    keep = (ctx + depth > 0).astype(f32)

    @pl.loop(0, CONV // 128)
    def _(n):
        cols = pl.ds(pl.multiple_of(n * 128, 128), 128)
        full = jnp.concatenate(
            [padded[0:16, cols].astype(f32) * keep, padded[16:, cols].astype(f32)], axis=0
        )
        acc = jnp.broadcast_to(tap_bias[:, cols], (BLOCK, 128))
        for j in range(KERNEL):
            acc = acc + taps[j : j + 1, cols] * full[13 + j : 13 + j + BLOCK]
        mixed[:, cols] = (acc * sigmoid(acc)).astype(bf16)

    in_map = mixed[:, D : D + STATE]
    out_map = mixed[:, D + STATE : D + 2 * STATE]
    cross = lax.dot_general(
        out_map, in_map, (((1,), (1,)), ((), ())), preferred_element_type=f32
    )
    gram[...] = jnp.where(row_id >= lane_id, cross, 0.0)
    in_twice = jnp.concatenate([in_map, in_map], axis=0)

    def first_copy(m, slot):
        return remote(piece.at[m], first.at[slot], first_send.at[m], first_recv.at[slot], member(m))

    @pl.loop(0, COLUMN)
    def _(i):
        m = (me + 1 + i) % COLUMN
        cols = pl.ds(pl.multiple_of(m * TILE, TILE), TILE)
        weight = jnp.dot(tail_cols[...], spread(m, 2, HEAD_DIM, TILE), preferred_element_type=f32)
        weighted = mixed[:, cols].astype(f32) * weight
        high = weighted.astype(bf16)
        low = (weighted - high.astype(f32)).astype(bf16)
        piece[m, 0:STATE, :] = lax.dot_general(
            in_twice,
            jnp.concatenate([high, low], axis=0),
            (((0,), (0,)), ((), ())),
            preferred_element_type=f32,
        )
        ends = jnp.dot(last_cols[...], spread(m, 3, HEAD_DIM, TILE), preferred_element_type=f32)
        piece[m, STATE : STATE + 8, :] = ends[0:8]

        @pl.when(i < COLUMN - 1)
        def _():
            first_copy(m, me).start()

    first[me] = piece[me]

    @pl.loop(0, COLUMN)
    def _(m):
        @pl.when(m != me)
        def _():
            first_copy(m, m).wait_recv()

    run = jnp.zeros((STATE, TILE), f32)
    run_log = jnp.zeros((8, TILE), f32)
    for m in range(COLUMN):
        earlier[m] = run
        earlier_log[m] = run_log
        log = first[m, STATE : STATE + 8, :]
        run = run * jnp.exp(log[0:1]) + first[m, 0:STATE, :]
        run_log = run_log + log
    total[0:STATE, :] = run
    total[STATE : STATE + 8, :] = run_log

    def second_copy(o):
        return remote(
            total, second.at[o], second_send.at[o], second_recv.at[o], peer((column + o) % FLAT)
        )

    @pl.loop(1, FLAT)
    def _(o):
        @pl.when(column + o < FLAT)
        def _():
            second_copy(o).start()

    @pl.loop(0, COLUMN)
    def _(m):
        cols = pl.ds(pl.multiple_of(m * TILE, TILE), TILE)
        upto = jnp.dot(cum_cols[...], spread(m, 3, BLOCK, 4 * BLOCK), preferred_element_type=f32)
        feature = mixed[:, cols]
        lane = lax.broadcasted_iota(jnp.int32, (BLOCK, TILE), 1) // HEAD_DIM
        highs, lows, blocks = [], [], []
        for j in range(4):
            head = pl.ds(4 * m + j, 1)
            gap = upto[:, BLOCK * j : BLOCK * (j + 1)] - cum[head, :]
            mix = jnp.exp(jnp.minimum(gap, 0.0)) * gram[...] * delta[head, :]
            mix = mix + jnp.where(row_id == lane_id, skip[4 * m + j], 0.0)
            high = mix.astype(bf16)
            highs.append(high)
            lows.append((mix - high.astype(f32)).astype(bf16))
            blocks.append(jnp.where(lane == j, feature, jnp.zeros_like(feature)))
        diagonal = jnp.concatenate(blocks, axis=0)
        inner[:, cols] = jnp.dot(
            jnp.concatenate(highs, axis=1), diagonal, preferred_element_type=f32
        ) + jnp.dot(jnp.concatenate(lows, axis=1), diagonal, preferred_element_type=f32)

    value[0:STATE, 0:TILE] = jnp.zeros((STATE, TILE), f32)

    @pl.loop(1, FLAT)
    def _(i):
        o = FLAT - i

        @pl.when(o <= column)
        def _():
            second_copy(o).wait_recv()
            value[0:STATE, 0:TILE] = (
                value[0:STATE, 0:TILE] * jnp.exp(second[o, STATE : STATE + 1, :])
                + second[o, 0:STATE, :]
            )

    def third_copy(m, slot):
        return remote(third.at[m], state.at[slot], third_send.at[m], third_recv.at[slot], member(m))

    @pl.loop(0, COLUMN)
    def _(i):
        m = (me + 1 + i) % COLUMN
        third[m] = (
            value[0:STATE, 0:TILE] * jnp.exp(earlier_log[m, 0:1, :]) + earlier[m]
        ).astype(bf16)

        @pl.when(i < COLUMN - 1)
        def _():
            third_copy(m, me).start()

    state[me] = third[me]

    @pl.loop(0, COLUMN)
    def _(m):
        @pl.when(m != me)
        def _():
            third_copy(m, m).wait_recv()

    def fold(a):
        return a[:, :128] + a[:, 128:]

    def carry(m, square):
        cols = pl.ds(pl.multiple_of(m * TILE, TILE), TILE)
        carried = jnp.dot(out_map, state[m], preferred_element_type=f32)
        weight = jnp.dot(entry_cols[...], spread(m, 2, HEAD_DIM, TILE), preferred_element_type=f32)
        branch = gate[:, cols].astype(f32)
        v = (inner[:, cols] + carried * weight) * (branch * sigmoid(branch))
        value[:, cols] = v
        return square + fold(v * v)

    zero = jnp.zeros((BLOCK, 128), f32)
    square = lax.fori_loop(0, COLUMN, carry, zero)
    scale = lax.rsqrt(jnp.sum(square, axis=1, keepdims=True) * (1.0 / D) + 1e-05)

    def join(m, square):
        cols = pl.ds(pl.multiple_of(m * TILE, TILE), TILE)
        out = value[:, cols] * scale * mixer_gain[:, cols]
        kept = (residual[:, cols].astype(f32) + out).astype(bf16)
        hidden[:, cols] = kept
        wide = kept.astype(f32)
        return square + fold(wide * wide)

    square = lax.fori_loop(0, COLUMN, join, zero)
    again = lax.rsqrt(jnp.sum(square, axis=1, keepdims=True) * (1.0 / D) + 1e-05)

    @pl.loop(0, COLUMN)
    def _(m):
        cols = pl.ds(pl.multiple_of(m * TILE, TILE), TILE)
        normed[:, cols] = (hidden[:, cols].astype(f32) * again * expert_norm[:, cols]).astype(bf16)

    logits = lax.dot_general(
        router[...], normed[...], (((1,), (1,)), ((), ())), preferred_element_type=f32
    )
    expert = lax.broadcasted_iota(jnp.int32, (32, BLOCK), 0)
    chosen = expert < 0
    for k in range(TOPK):
        chosen = chosen | (expert == ids[k : k + 1, :])
    score = jnp.where(chosen, sigmoid(logits), 0.0)
    gates[...] = score / jnp.sum(score, axis=0, keepdims=True)

    halo.wait_send()

    @pl.loop(0, COLUMN)
    def _(m):
        @pl.when(m != me)
        def _():
            first_copy(m, me).wait_send()
            third_copy(m, me).wait_send()

    @pl.loop(1, FLAT)
    def _(o):
        @pl.when(column + o < FLAT)
        def _():
            second_copy(o).wait_send()


def mixer(entry, gate, residual, step, bias, decay_log, taps, tap_bias, skip, gain, norm, router, ids):
    f32, bf16 = jnp.float32, jnp.bfloat16
    vmem = pl.BlockSpec(memory_space=pltpu.VMEM)
    smem = pl.BlockSpec(memory_space=pltpu.SMEM)
    dma = pltpu.SemaphoreType.DMA
    return pl.pallas_call(
        mixer_kernel,
        out_shape=(
            jax.ShapeDtypeStruct((BLOCK, D), bf16),
            jax.ShapeDtypeStruct((BLOCK, D), bf16),
            jax.ShapeDtypeStruct((32, BLOCK), f32),
        ),
        in_specs=[vmem] * 8 + [smem] + [vmem] * 4,
        out_specs=(vmem, vmem, vmem),
        scratch_shapes=[
            pltpu.VMEM((BLOCK + 16, CONV), bf16),
            pltpu.VMEM((BLOCK, CONV), bf16),
            pltpu.VMEM((HEADS, BLOCK), f32),
            pltpu.VMEM((HEADS, BLOCK), f32),
            pltpu.VMEM((BLOCK, 3 * HEADS), bf16),
            pltpu.VMEM((BLOCK, 2 * HEADS), bf16),
            pltpu.VMEM((BLOCK, 2 * HEADS), bf16),
            pltpu.VMEM((16, 3 * HEADS), bf16),
            pltpu.VMEM((BLOCK, BLOCK), f32),
            pltpu.VMEM((COLUMN, STATE + 8, TILE), f32),
            pltpu.VMEM((COLUMN, STATE + 8, TILE), f32),
            pltpu.VMEM((COLUMN, STATE, TILE), f32),
            pltpu.VMEM((COLUMN, 8, TILE), f32),
            pltpu.VMEM((STATE + 8, TILE), f32),
            pltpu.VMEM((FLAT, STATE + 8, TILE), f32),
            pltpu.VMEM((COLUMN, STATE, TILE), bf16),
            pltpu.VMEM((COLUMN, STATE, TILE), bf16),
            pltpu.VMEM((BLOCK, D), f32),
            pltpu.VMEM((BLOCK, D), f32),
            dma((1,)),
            dma((1,)),
            dma((COLUMN,)),
            dma((COLUMN,)),
            dma((FLAT,)),
            dma((FLAT,)),
            dma((COLUMN,)),
            dma((COLUMN,)),
        ],
        compiler_params=pltpu.CompilerParams(
            collective_id=1, has_side_effects=True, vmem_limit_bytes=48 * 1024 * 1024
        ),
        cost_estimate=pl.CostEstimate(
            flops=2 * BLOCK * 512 * D * 3, bytes_accessed=BLOCK * D * 12, transcendentals=BLOCK * D * 5
        ),
    )(
        entry,
        gate,
        residual,
        step,
        bias[:, None],
        decay_log[:, None],
        taps,
        tap_bias[None, :],
        skip,
        gain[None, :],
        norm[None, :],
        router.T,
        ids.T,
    )


def body(
    filter_entry_array,
    gate_input,
    step_unshifted,
    step_bias,
    decay_log,
    conv_weight,
    conv_bias,
    skip_gain,
    mixer_gain,
    residual,
    expert_norm,
    router_weight,
    expert_ids,
    w_gate,
    w_up,
    w_down,
):
    normed, hidden, gates = mixer(
        filter_entry_array,
        gate_input,
        residual,
        step_unshifted,
        step_bias,
        decay_log,
        conv_weight,
        conv_bias,
        skip_gain,
        mixer_gain,
        expert_norm,
        router_weight,
        expert_ids,
    )
    return experts(normed, gates, hidden, w_gate, w_up, w_down)


def solution(mesh):
    return jax.shard_map(
        body,
        mesh=mesh,
        in_specs=(
            P(("ctx", "exp"), None),
            P(("ctx", "exp"), None),
            P(None, ("ctx", "exp")),
            P(),
            P(),
            P(),
            P(),
            P(),
            P(),
            P(("ctx", "exp"), None),
            P(),
            P(),
            P(("ctx", "exp"), None),
            P("ctx", None, None),
            P("ctx", None, None),
            P("ctx", None, None),
        ),
        out_specs=P(("ctx", "exp"), None),
        check_vma=False,
    )
```

```python
import types

import jax
import jax.numpy as jnp
from jax import lax
from jax.experimental import pallas as pl
from jax.experimental.pallas import tpu as pltpu
from jax.sharding import PartitionSpec as P

D = 2048
HEADS = 32
HEAD_DIM = 64
STATE = 64
KERNEL = 4
TOPK = 8
CAP = 40
CONV = 2176
FF = 768
EXPERTS = 32
BLOCK = 128
HALF = BLOCK // 2
PICK = 4 * CAP
WIDE = 4 * BLOCK
COLUMN = 8
TILE = D // COLUMN
FLAT = 16
SENT = STATE + 16

EXACT = lax.Precision.HIGHEST
MESH = pl.DeviceIdType.MESH
f32 = jnp.float32
bf16 = jnp.bfloat16


def sigmoid(value):
    return 1.0 / (1.0 + jnp.exp(-value))


def split(value, count):
    pieces = []
    for _ in range(count):
        piece = value.astype(bf16)
        pieces.append(piece)
        value = value - piece.astype(f32)
    return pieces


def remote(src, dst, send, recv, to):
    return pltpu.make_async_remote_copy(
        src_ref=src, dst_ref=dst, send_sem=send, recv_sem=recv, device_id=to, device_id_type=MESH
    )


INPUTS = (
    "entry", "gate", "step", "step_bias", "decay_log", "taps", "tap_bias", "skip", "mixer_gain",
    "residual", "expert_norm", "router", "ids", "w_gate", "w_up", "w_down",
)


def scratch():
    vmem = pltpu.VMEM
    dma = pltpu.SemaphoreType.DMA
    return {
        "padded": vmem((BLOCK + 16, CONV), bf16),
        "gate_v": vmem((BLOCK, D), bf16),
        "step_v": vmem((HEADS, BLOCK), f32),
        "step_bias_v": vmem((1, HEADS), f32),
        "decay_log_v": vmem((1, HEADS), f32),
        "taps_v": vmem((KERNEL, CONV), f32),
        "tap_bias_v": vmem((1, CONV), f32),
        "mixer_gain_v": vmem((1, D), f32),
        "residual_v": vmem((BLOCK, D), bf16),
        "expert_norm_v": vmem((1, D), f32),
        "router_v": vmem((EXPERTS, D), bf16),
        "ids_v": vmem((TOPK, BLOCK), jnp.int32),
        "mixed": vmem((BLOCK, CONV), bf16),
        "cum": vmem((HEADS, BLOCK), f32),
        "delta": vmem((HEADS, BLOCK), f32),
        "cum_cols": vmem((BLOCK, 3 * HEADS), bf16),
        "tail_cols": vmem((BLOCK, 2 * HEADS), bf16),
        "entry_cols": vmem((BLOCK, 2 * HEADS), bf16),
        "last_rows": vmem((16, HEADS), bf16),
        "gram": vmem((BLOCK, BLOCK), f32),
        "piece": vmem((COLUMN, SENT, TILE), bf16),
        "first": vmem((COLUMN, SENT, TILE), bf16),
        "earlier": vmem((COLUMN, STATE, TILE), f32),
        "earlier_log": vmem((COLUMN, 8, TILE), f32),
        "total": vmem((SENT, TILE), bf16),
        "second": vmem((FLAT, SENT, TILE), bf16),
        "third": vmem((COLUMN, STATE, TILE), bf16),
        "state": vmem((COLUMN, STATE, TILE), bf16),
        "before": vmem((STATE, TILE), f32),
        "value": vmem((BLOCK, D), f32),
        "hidden": vmem((BLOCK, D), bf16),
        "rows": vmem((16 * BLOCK, D), bf16),
        "meta": vmem((16, EXPERTS, BLOCK), f32),
        "wg": vmem((D, FF), bf16),
        "wu": vmem((D, FF), bf16),
        "wd": vmem((FF, D), bf16),
        "picked": vmem((4, 2 * PICK, D), bf16),
        "lent": vmem((4, PICK, D), bf16),
        "activated": vmem((2 * PICK, FF), bf16),
        "own_y": vmem((PICK, D), bf16),
        "lent_y": vmem((4, PICK, D), bf16),
        "back_y": vmem((4, PICK, D), bf16),
        "select": vmem((4, 2 * PICK, WIDE), bf16),
        "gate_col": vmem((4, 2 * PICK, BLOCK), f32),
        "part": vmem((16 * BLOCK, D), bf16),
        "land": vmem((15 * BLOCK, D), bf16),
        "done": vmem((BLOCK, D), bf16),
        "load_sem": dma((16,)),
        "halo_send": dma((1,)),
        "halo_recv": dma((1,)),
        "first_send": dma((COLUMN,)),
        "first_recv": dma((COLUMN,)),
        "second_send": dma((FLAT,)),
        "second_recv": dma((FLAT,)),
        "third_send": dma((COLUMN,)),
        "third_recv": dma((COLUMN,)),
        "row_send": dma((30,)),
        "row_recv": dma((30,)),
        "meta_send": dma((15,)),
        "meta_recv": dma((15,)),
        "lent_send": dma((4,)),
        "lent_recv": dma((4,)),
        "back_send": dma((4,)),
        "back_recv": dma((4,)),
        "sum_send": dma((30,)),
        "sum_recv": dma((30,)),
    }


def layer_kernel(*refs):
    names = INPUTS + ("out",) + tuple(scratch())
    r = types.SimpleNamespace(**dict(zip(names, refs)))
    ctx = lax.axis_index("ctx")
    depth = lax.axis_index("exp")
    core = ctx % 2
    column = ctx // 2
    me = core * 4 + depth
    finish = mix_rows(r, ctx, depth, core, column, me)
    spread_rows(r, ctx, depth, core, column)
    finish()


def mix_rows(r, ctx, depth, core, column, me):
    def member(m):
        return (column * 2 + m // 4, m % 4)

    def peer(c):
        return (c * 2 + core, depth)

    last = (me == COLUMN - 1).astype(jnp.int32)
    after = (((column + last) % FLAT) * 2 + ((me + 1) % COLUMN) // 4, (me + 1) % 4)
    initial = (me == 0).astype(jnp.int32)
    ahead = (
        ((column - initial + FLAT) % FLAT) * 2 + ((me + COLUMN - 1) % COLUMN) // 4,
        (me + COLUMN - 1) % 4,
    )

    def load(i, src, dst):
        copy = pltpu.make_async_copy(src, dst, r.load_sem.at[i])
        copy.start()
        return copy

    load_entry = load(0, r.entry, r.padded.at[pl.ds(16, BLOCK)])
    load_steps = [
        load(1, r.step, r.step_v),
        load(2, r.step_bias, r.step_bias_v),
        load(3, r.decay_log, r.decay_log_v),
    ]
    load_taps = [load(4, r.taps, r.taps_v), load(5, r.tap_bias, r.tap_bias_v)]
    load_rest = [
        load(6, r.gate, r.gate_v),
        load(7, r.residual, r.residual_v),
        load(8, r.mixer_gain, r.mixer_gain_v),
        load(9, r.expert_norm, r.expert_norm_v),
        load(10, r.router, r.router_v),
        load(11, r.ids, r.ids_v),
    ]
    for i, (src, dst) in enumerate(((r.w_gate, r.wg), (r.w_up, r.wu), (r.w_down, r.wd))):
        load(12 + i, src.at[0], dst)

    barrier = pltpu.get_barrier_semaphore()

    @pl.loop(1, COLUMN)
    def _(i):
        pl.semaphore_signal(
            barrier, inc=1, device_id=member((me + i) % COLUMN), device_id_type=MESH
        )

    @pl.loop(1, FLAT)
    def _(i):
        pl.semaphore_signal(
            barrier, inc=1, device_id=peer((column + i) % FLAT), device_id_type=MESH
        )

    @pl.when(me == COLUMN - 1)
    def _():
        pl.semaphore_signal(barrier, inc=1, device_id=after, device_id_type=MESH)

    @pl.when(me == 0)
    def _():
        pl.semaphore_signal(barrier, inc=1, device_id=ahead, device_id_type=MESH)

    load_entry.wait()
    pl.semaphore_wait(barrier, COLUMN + FLAT - 2 + last + initial)

    halo = remote(
        r.padded.at[pl.ds(BLOCK, 16)],
        r.padded.at[pl.ds(0, 16)],
        r.halo_send.at[0],
        r.halo_recv.at[0],
        after,
    )
    halo.start()

    row_id = lax.broadcasted_iota(jnp.int32, (BLOCK, BLOCK), 0)
    lane_id = lax.broadcasted_iota(jnp.int32, (BLOCK, BLOCK), 1)
    square_id = [lax.broadcasted_iota(jnp.int32, (HEADS, HEADS), axis) for axis in (0, 1)]

    def upend(row):
        spot = jnp.where(square_id[0] == square_id[1], row, 0.0)
        return jnp.sum(spot, axis=1, keepdims=True)

    for copy in load_steps:
        copy.wait()
    shifted = r.step_v[...] + upend(r.step_bias_v[...])
    width = jnp.maximum(shifted, 0.0) + jnp.log1p(jnp.exp(-jnp.abs(shifted)))
    logs = -width * jnp.exp(upend(r.decay_log_v[...]))
    summed = jnp.dot(
        logs, (row_id <= lane_id).astype(f32), precision=EXACT, preferred_element_type=f32
    )
    r.cum[...] = summed
    r.delta[...] = width

    def upright(a):
        return jnp.concatenate([a, jnp.zeros((BLOCK - HEADS, BLOCK), f32)], axis=0).T[:, :HEADS]

    summed_t = upright(summed)
    width_t = upright(width)
    final = summed_t[BLOCK - 1 :, :]
    r.cum_cols[...] = jnp.concatenate(split(summed_t, 3), axis=1)
    r.tail_cols[...] = jnp.concatenate(split(jnp.exp(final - summed_t) * width_t, 2), axis=1)
    r.entry_cols[...] = jnp.concatenate(split(jnp.exp(summed_t), 2), axis=1)
    terms = split(final, 3)
    r.last_rows[...] = jnp.concatenate(
        terms + [jnp.zeros((13, HEADS), bf16)], axis=0
    )

    def spread(m, copies, per, count):
        head = lax.broadcasted_iota(jnp.int32, (HEADS, count), 0)
        lane = lax.broadcasted_iota(jnp.int32, (HEADS, count), 1)
        one = (head == 4 * m + lane // per).astype(bf16)
        return one if copies == 1 else jnp.concatenate([one] * copies, axis=0)

    for copy in load_taps:
        copy.wait()

    def convolve(full, count, cols):
        acc = jnp.broadcast_to(r.tap_bias_v[:, cols], (count, 128))
        for j in range(KERNEL):
            acc = acc + r.taps_v[j : j + 1, cols] * full[13 + j : 13 + j + count]
        return (acc * sigmoid(acc)).astype(bf16)

    @pl.loop(0, CONV // 128)
    def _(n):
        cols = pl.ds(pl.multiple_of(n * 128, 128), 128)
        r.mixed[16:, cols] = convolve(r.padded[16:, cols].astype(f32), BLOCK - 16, cols)

    halo.wait_recv()
    keep = (ctx + depth > 0).astype(f32)

    @pl.loop(0, CONV // 128)
    def _(n):
        cols = pl.ds(pl.multiple_of(n * 128, 128), 128)
        full = jnp.concatenate(
            [r.padded[0:16, cols].astype(f32) * keep, r.padded[16:32, cols].astype(f32)], axis=0
        )
        r.mixed[0:16, cols] = convolve(full, 16, cols)

    in_map = r.mixed[:, D : D + STATE]
    out_map = r.mixed[:, D + STATE : D + 2 * STATE]
    in_twice = jnp.concatenate([in_map, in_map], axis=0)

    def first_copy(m, slot):
        return remote(
            r.piece.at[m], r.first.at[slot], r.first_send.at[m], r.first_recv.at[slot], member(m)
        )

    @pl.loop(0, COLUMN)
    def _(i):
        m = (me + 1 + i) % COLUMN
        cols = pl.ds(pl.multiple_of(m * TILE, TILE), TILE)
        weight = jnp.dot(r.tail_cols[...], spread(m, 2, HEAD_DIM, TILE), preferred_element_type=f32)
        weighted = r.mixed[:, cols].astype(f32) * weight
        r.piece[m, 0:STATE, :] = lax.dot_general(
            in_twice,
            jnp.concatenate(split(weighted, 2), axis=0),
            (((0,), (0,)), ((), ())),
            preferred_element_type=f32,
        ).astype(bf16)
        r.piece[m, STATE:, :] = jnp.dot(
            r.last_rows[...], spread(m, 1, HEAD_DIM, TILE), preferred_element_type=f32
        ).astype(bf16)

        @pl.when(i < COLUMN - 1)
        def _():
            first_copy(m, me).start()

    r.first[me] = r.piece[me]

    cross = lax.dot_general(
        out_map, in_map, (((1,), (1,)), ((), ())), preferred_element_type=f32
    )
    r.gram[...] = jnp.where(row_id >= lane_id, cross, 0.0)

    def inside(m):
        cols = pl.ds(pl.multiple_of(m * TILE, TILE), TILE)
        upto = jnp.dot(r.cum_cols[...], spread(m, 3, BLOCK, 4 * BLOCK), preferred_element_type=f32)
        feature = r.mixed[:, cols]
        lane = lax.broadcasted_iota(jnp.int32, (BLOCK, TILE), 1) // HEAD_DIM
        highs, lows, blocks = [], [], []
        for j in range(4):
            head = pl.ds(4 * m + j, 1)
            gap = upto[:, BLOCK * j : BLOCK * (j + 1)] - r.cum[head, :]
            mix = jnp.exp(jnp.minimum(gap, 0.0)) * r.gram[...] * r.delta[head, :]
            mix = mix + jnp.where(row_id == lane_id, r.skip[4 * m + j], 0.0)
            high, low = split(mix, 2)
            highs.append(high)
            lows.append(low)
            blocks.append(jnp.where(lane == j, feature, jnp.zeros_like(feature)))
        diagonal = jnp.concatenate(blocks, axis=0)
        r.value[:, cols] = jnp.dot(
            jnp.concatenate(highs, axis=1), diagonal, preferred_element_type=f32
        ) + jnp.dot(jnp.concatenate(lows, axis=1), diagonal, preferred_element_type=f32)

    @pl.loop(0, COLUMN)
    def _(m):
        inside(m)

    @pl.loop(0, COLUMN)
    def _(m):
        @pl.when(m != me)
        def _():
            first_copy(m, m).wait_recv()

    def log_of(block):
        terms = block.astype(f32)
        return terms[0:1] + terms[1:2] + terms[2:3]

    run = jnp.zeros((STATE, TILE), f32)
    run_log = jnp.zeros((1, TILE), f32)
    for m in range(COLUMN):
        r.earlier[m] = run
        r.earlier_log[m] = jnp.broadcast_to(run_log, (8, TILE))
        log = log_of(r.first[m, STATE:, :])
        run = run * jnp.exp(log) + r.first[m, 0:STATE, :].astype(f32)
        run_log = run_log + log
    r.total[0:STATE, :] = run.astype(bf16)
    r.total[STATE:, :] = jnp.concatenate(
        split(run_log, 3) + [jnp.zeros((13, TILE), bf16)], axis=0
    )

    def second_copy(o):
        return remote(
            r.total,
            r.second.at[o],
            r.second_send.at[o],
            r.second_recv.at[o],
            peer((column + o) % FLAT),
        )

    @pl.loop(1, FLAT)
    def _(o):
        @pl.when(column + o < FLAT)
        def _():
            second_copy(o).start()

    for copy in load_rest:
        copy.wait()
    r.before[...] = jnp.zeros((STATE, TILE), f32)

    @pl.loop(1, FLAT)
    def _(i):
        o = FLAT - i

        @pl.when(o <= column)
        def _():
            second_copy(o).wait_recv()
            r.before[...] = (
                r.before[...] * jnp.exp(log_of(r.second[o, STATE:, :]))
                + r.second[o, 0:STATE, :].astype(f32)
            )

    def third_copy(m, slot):
        return remote(
            r.third.at[m], r.state.at[slot], r.third_send.at[m], r.third_recv.at[slot], member(m)
        )

    @pl.loop(0, COLUMN)
    def _(i):
        m = (me + 1 + i) % COLUMN
        r.third[m] = (r.before[...] * jnp.exp(r.earlier_log[m, 0:1, :]) + r.earlier[m]).astype(bf16)

        @pl.when(i < COLUMN - 1)
        def _():
            third_copy(m, me).start()

    r.state[me] = r.third[me]

    @pl.loop(0, COLUMN)
    def _(m):
        @pl.when(m != me)
        def _():
            third_copy(m, m).wait_recv()

    def fold(a):
        return a[:, :128] + a[:, 128:]

    def carry(m, square):
        cols = pl.ds(pl.multiple_of(m * TILE, TILE), TILE)
        carried = jnp.dot(out_map, r.state[m], preferred_element_type=f32)
        weight = jnp.dot(r.entry_cols[...], spread(m, 2, HEAD_DIM, TILE), preferred_element_type=f32)
        branch = r.gate_v[:, cols].astype(f32)
        v = (r.value[:, cols] + carried * weight) * (branch * sigmoid(branch))
        r.value[:, cols] = v
        return square + fold(v * v)

    zero = jnp.zeros((BLOCK, 128), f32)
    square = lax.fori_loop(0, COLUMN, carry, zero)
    scale = lax.rsqrt(jnp.sum(square, axis=1, keepdims=True) * (1.0 / D) + 1e-05)

    def join(m, square):
        cols = pl.ds(pl.multiple_of(m * TILE, TILE), TILE)
        out = r.value[:, cols] * scale * r.mixer_gain_v[:, cols]
        kept = (r.residual_v[:, cols].astype(f32) + out).astype(bf16)
        r.hidden[:, cols] = kept
        wide = kept.astype(f32)
        return square + fold(wide * wide)

    square = lax.fori_loop(0, COLUMN, join, zero)
    again = lax.rsqrt(jnp.sum(square, axis=1, keepdims=True) * (1.0 / D) + 1e-05)

    @pl.loop(0, COLUMN)
    def _(m):
        cols = pl.ds(pl.multiple_of(m * TILE, TILE), TILE)
        r.rows[0:BLOCK, cols] = (
            r.hidden[:, cols].astype(f32) * again * r.expert_norm_v[:, cols]
        ).astype(bf16)

    logits = lax.dot_general(
        r.router_v[...], r.rows[0:BLOCK, :], (((1,), (1,)), ((), ())), preferred_element_type=f32
    )
    expert = lax.broadcasted_iota(jnp.int32, (EXPERTS, BLOCK), 0)
    chosen = expert < 0
    for k in range(TOPK):
        chosen = chosen | (expert == r.ids_v[k : k + 1, :])
    score = jnp.where(chosen, sigmoid(logits), 0.0)
    r.meta[0] = score / jnp.sum(score, axis=0, keepdims=True)

    def finish():
        halo.wait_send()

        @pl.loop(0, COLUMN)
        def _(m):
            @pl.when(m != me)
            def _():
                first_copy(m, me).wait_send()
                third_copy(m, me).wait_send()

        @pl.loop(1, FLAT)
        def _(o):
            @pl.when(column + o < FLAT)
            def _():
                second_copy(o).wait_send()

    return finish


def spread_rows(r, ctx, depth, core, column):
    x = column % 4
    y = column // 4
    sibling = ctx + 1 - 2 * core

    def device(first, second):
        to_y = (y + core * first + (1 - core) * second + 4) % 4
        to_x = (x + core * second + (1 - core) * first + 4) % 4
        return ((to_y * 4 + to_x) * 2 + core, depth)

    forth = (device(1, 0), device(0, 1))
    back = (device(-1, 0), device(0, -1))
    across = (sibling, depth)

    def ring(stage):
        return (0, 4, 0) if stage == 0 else (4 * (stage - 1), 1, 1)

    def row_copy(stage, kind):
        base, stride, axis = ring(stage)
        sem = 6 * stage + kind
        to = (forth, back)[kind % 2][axis]
        source, target, low = (
            (0, 1, 0), (0, 3, HALF), (0, 1, HALF), (0, 3, 0), (1, 2, 0), (3, 2, HALF)
        )[kind]
        return remote(
            r.rows.at[pl.ds((base + stride * source) * BLOCK + low, HALF)],
            r.rows.at[pl.ds((base + stride * target) * BLOCK + low, HALF)],
            r.row_send.at[sem],
            r.row_recv.at[sem],
            to,
        )

    def meta_copy(stage, kind):
        base, stride, axis = ring(stage)
        sem = 3 * stage + kind
        source, target, to = ((0, 1, forth), (0, 3, back), (1, 2, forth))[kind]
        return remote(
            r.meta.at[base + stride * source],
            r.meta.at[base + stride * target],
            r.meta_send.at[sem],
            r.meta_recv.at[sem],
            to[axis],
        )

    def sum_copy(stage, kind):
        base, stride, axis = ring(stage)
        sem = 6 * stage + kind
        to = (back, forth)[kind % 2][axis]
        source, low, place = (
            (2, 0, 0),
            (2, HALF, HALF),
            (1, HALF, BLOCK + HALF),
            (3, 0, 2 * BLOCK),
            (1, 0, BLOCK),
            (3, HALF, 2 * BLOCK + HALF),
        )[kind]
        return remote(
            r.part.at[pl.ds((base + stride * source) * BLOCK + low, HALF)],
            r.land.at[pl.ds(stage * 3 * BLOCK + place, HALF)],
            r.sum_send.at[sem],
            r.sum_recv.at[sem],
            to,
        )

    def lent_copy(k):
        return remote(
            r.lent.at[k],
            r.picked.at[k, pl.ds(PICK, PICK)],
            r.lent_send.at[k],
            r.lent_recv.at[k],
            across,
        )

    def back_copy(k):
        return remote(
            r.lent_y.at[k], r.back_y.at[k], r.back_send.at[k], r.back_recv.at[k], across
        )

    def send_rows(stage, *kinds):
        for kind in kinds:
            row_copy(stage, kind).start()

    def send_meta(stage):
        meta_copy(stage, 0).start()
        meta_copy(stage, 1).start()

    def pass_rows(stage, kind):
        row_copy(stage, kind).wait_recv()
        row_copy(stage, kind + 4).start()

    def pass_both(stage):
        meta_copy(stage, 0).wait_recv()
        meta_copy(stage, 2).start()
        pass_rows(stage, 0)
        pass_rows(stage, 1)

    def arrive(stage):
        for kind in (1, 2):
            meta_copy(stage, kind).wait_recv()
        for kind in (2, 3, 4, 5):
            row_copy(stage, kind).wait_recv()

    before = (
        lax.broadcasted_iota(jnp.int32, (BLOCK, BLOCK), 0)
        < lax.broadcasted_iota(jnp.int32, (BLOCK, BLOCK), 1)
    ).astype(bf16)
    slot_row = lax.broadcasted_iota(jnp.int32, (PICK, WIDE), 0).astype(f32)

    def choose(k):
        gate = jnp.concatenate(
            [
                r.meta[4 * k + j, pl.ds(expert, 1), :]
                for expert in (ctx, sibling)
                for j in range(4)
            ],
            axis=0,
        )
        live = gate > 0.0
        rank = jnp.dot(live.astype(bf16), before, preferred_element_type=f32)
        shift = (lax.broadcasted_iota(jnp.int32, (8, BLOCK), 0) % 4).astype(f32) * CAP
        slot = jnp.where(live, rank + shift, -1.0)
        for half in range(2):
            lanes = jnp.concatenate([slot[4 * half + j : 4 * half + j + 1] for j in range(4)], axis=1)
            value = jnp.concatenate([gate[4 * half + j : 4 * half + j + 1] for j in range(4)], axis=1)
            hit = slot_row == lanes
            span = pl.ds(half * PICK, PICK)
            r.select[k, span, :] = jnp.where(hit, 1.0, 0.0).astype(bf16)
            total = jnp.sum(jnp.where(hit, value, 0.0), axis=1, keepdims=True)
            r.gate_col[k, span, :] = jnp.broadcast_to(total, (PICK, BLOCK))

        @pl.loop(0, 8)
        def _(n):
            cols = pl.ds(pl.multiple_of(n * 256, 256), 256)
            got = jnp.dot(
                r.select[k], r.rows[pl.ds(k * WIDE, WIDE), cols], preferred_element_type=f32
            ).astype(bf16)
            r.picked[k, pl.ds(0, PICK), cols] = got[:PICK]
            r.lent[k, :, cols] = got[PICK:]

        lent_copy(k).start()

    def feed(k):
        lent_copy(k).wait_recv()

        @pl.loop(0, 3)
        def _(f):
            cols = pl.ds(pl.multiple_of(f * 256, 256), 256)
            gate = jnp.dot(r.picked[k], r.wg[:, cols], preferred_element_type=f32)
            up = jnp.dot(r.picked[k], r.wu[:, cols], preferred_element_type=f32)
            r.activated[:, cols] = (gate * sigmoid(gate) * up).astype(bf16)

    def produce(k):
        @pl.loop(0, 8)
        def _(n):
            cols = pl.ds(pl.multiple_of(n * 256, 256), 256)
            made = jnp.dot(r.activated[...], r.wd[:, cols], preferred_element_type=f32)
            scale = r.gate_col[k, pl.ds(0, PICK), :]
            r.own_y[:, cols] = (
                made[:PICK] * jnp.concatenate([scale, scale], axis=1)
            ).astype(bf16)
            r.lent_y[k, :, cols] = made[PICK:].astype(bf16)

        back_copy(k).start()

    def combine(k):
        back_copy(k).wait_recv()

        @pl.loop(0, 8)
        def _(n):
            cols = pl.ds(pl.multiple_of(n * 256, 256), 256)
            scale = r.gate_col[k, pl.ds(PICK, PICK), :]
            other = (
                r.back_y[k, :, cols].astype(f32) * jnp.concatenate([scale, scale], axis=1)
            ).astype(bf16)
            both = jnp.concatenate([r.own_y[:, cols], other], axis=0)
            r.part[pl.ds(k * WIDE, WIDE), cols] = lax.dot_general(
                r.select[k], both, (((0,), (0,)), ((), ())), preferred_element_type=f32
            ).astype(bf16)

    def add_into(block, low, count, places):
        @pl.loop(0, count // 16)
        def _(i):
            span = pl.ds(pl.multiple_of(block * BLOCK + low + i * 16, 16), 16)
            total = r.part[span, :].astype(f32)
            for place in places:
                total += r.land[pl.ds(pl.multiple_of(place + i * 16, 16), 16), :].astype(f32)
            r.part[span, :] = total.astype(bf16)

    def sum_first(stage):
        for kind in range(4):
            sum_copy(stage, kind).start()

    def sum_second(stage):
        base, stride, _ = ring(stage)
        place = stage * 3 * BLOCK
        sum_copy(stage, 0).wait_recv()
        add_into(base + stride, 0, HALF, (place,))
        sum_copy(stage, 4).start()
        sum_copy(stage, 1).wait_recv()
        add_into(base + 3 * stride, HALF, HALF, (place + HALF,))
        sum_copy(stage, 5).start()

    def sum_last(stage):
        base, _, _ = ring(stage)
        place = stage * 3 * BLOCK
        for kind in (2, 3, 4, 5):
            sum_copy(stage, kind).wait_recv()
        if stage > 0:
            add_into(base, 0, BLOCK, (place + BLOCK, place + 2 * BLOCK))

    send_meta(0)
    send_rows(0, 0, 1, 2, 3)
    send_meta(1)
    send_rows(1, 0, 1)
    meta_copy(0, 0).wait_recv()
    meta_copy(0, 2).start()
    send_meta(2)
    pass_rows(0, 0)
    send_rows(2, 0, 3)
    meta_copy(0, 1).wait_recv()
    send_meta(4)
    pass_rows(0, 1)
    send_rows(4, 1, 2)
    send_rows(1, 2, 3)
    row_copy(0, 2).wait_recv()
    send_rows(2, 1, 2)
    row_copy(0, 3).wait_recv()
    send_rows(4, 0, 3)
    pass_both(1)
    meta_copy(0, 2).wait_recv()
    send_meta(3)
    row_copy(0, 4).wait_recv()
    send_rows(3, 0, 3)
    row_copy(0, 5).wait_recv()
    send_rows(3, 1, 2)
    pass_both(2)
    pass_both(4)
    arrive(1)
    choose(0)
    for i, (src, dst) in enumerate(((r.w_gate, r.wg), (r.w_up, r.wu), (r.w_down, r.wd))):
        pltpu.make_async_copy(src.at[0], dst, r.load_sem.at[12 + i]).wait()
    feed(0)
    pass_both(3)
    produce(0)
    arrive(2)
    choose(1)
    combine(0)
    feed(1)
    produce(1)
    arrive(4)
    choose(3)
    combine(1)
    sum_first(2)
    feed(3)
    produce(3)
    arrive(3)
    choose(2)
    combine(3)
    sum_first(4)
    sum_second(2)
    feed(2)
    produce(2)
    sum_second(4)
    combine(2)
    sum_first(3)
    sum_first(1)
    sum_last(2)
    sum_last(4)
    sum_second(3)
    sum_second(1)
    sum_last(3)
    sum_first(0)
    sum_last(1)
    sum_second(0)
    sum_last(0)

    @pl.loop(0, BLOCK // 16)
    def _(i):
        span = pl.ds(pl.multiple_of(i * 16, 16), 16)
        total = r.part[span, :].astype(f32)
        for place in (BLOCK, 2 * BLOCK):
            total += r.land[pl.ds(pl.multiple_of(place + i * 16, 16), 16), :].astype(f32)
        r.done[span, :] = (r.hidden[span, :].astype(f32) + total).astype(bf16)

    store = pltpu.make_async_copy(r.done, r.out, r.load_sem.at[15])
    store.start()
    for stage in range(5):
        for kind in range(6):
            row_copy(stage, kind).wait_send()
            sum_copy(stage, kind).wait_send()
        for kind in range(3):
            meta_copy(stage, kind).wait_send()
    for k in range(4):
        lent_copy(k).wait_send()
        back_copy(k).wait_send()
    store.wait()


def layer(
    filter_entry_array,
    gate_input,
    step_unshifted,
    step_bias,
    decay_log,
    conv_weight,
    conv_bias,
    skip_gain,
    mixer_gain,
    residual,
    expert_norm,
    router_weight,
    expert_ids,
    w_gate,
    w_up,
    w_down,
):
    hbm = pl.BlockSpec(memory_space=pl.ANY)
    specs = [hbm] * len(INPUTS)
    specs[INPUTS.index("skip")] = pl.BlockSpec(memory_space=pltpu.SMEM)
    return pl.pallas_call(
        layer_kernel,
        out_shape=jax.ShapeDtypeStruct((BLOCK, D), bf16),
        in_specs=specs,
        out_specs=hbm,
        scratch_shapes=list(scratch().values()),
        compiler_params=pltpu.CompilerParams(
            collective_id=0, has_side_effects=True, vmem_limit_bytes=62 * 1024 * 1024
        ),
    )(
        filter_entry_array,
        gate_input,
        step_unshifted,
        step_bias[None, :],
        decay_log[None, :],
        conv_weight,
        conv_bias[None, :],
        skip_gain,
        mixer_gain[None, :],
        residual,
        expert_norm[None, :],
        router_weight.T,
        expert_ids.T,
        w_gate,
        w_up,
        w_down,
    )


def solution(mesh):
    rows = P(("ctx", "exp"), None)
    shared = P()
    owner = P("ctx", None, None)
    return jax.shard_map(
        layer,
        mesh=mesh,
        in_specs=(
            rows,
            rows,
            P(None, ("ctx", "exp")),
            shared,
            shared,
            shared,
            shared,
            shared,
            shared,
            rows,
            shared,
            shared,
            rows,
            owner,
            owner,
            owner,
        ),
        out_specs=rows,
        check_vma=False,
    )
```

```python
import types

import jax
import jax.numpy as jnp
from jax import lax
from jax.experimental import pallas as pl
from jax.experimental.pallas import tpu as pltpu
from jax.sharding import PartitionSpec as P

D = 2048
HEADS = 32
HEAD_DIM = 64
STATE = 64
KERNEL = 4
TOPK = 8
CAP = 40
CONV = 2176
FF = 768
EXPERTS = 32
BLOCK = 128
HALF = BLOCK // 2
PICK = 4 * CAP
WIDE = 4 * BLOCK
COLUMN = 8
TILE = D // COLUMN
FLAT = 16
SENT = STATE + 16

EXACT = lax.Precision.HIGHEST
MESH = pl.DeviceIdType.MESH
f32 = jnp.float32
bf16 = jnp.bfloat16


def sigmoid(value):
    return 1.0 / (1.0 + jnp.exp(-value))


def split(value, count):
    pieces = []
    for _ in range(count):
        piece = value.astype(bf16)
        pieces.append(piece)
        value = value - piece.astype(f32)
    return pieces


def remote(src, dst, send, recv, to):
    return pltpu.make_async_remote_copy(
        src_ref=src, dst_ref=dst, send_sem=send, recv_sem=recv, device_id=to, device_id_type=MESH
    )


INPUTS = (
    "entry", "gate", "step", "step_bias", "decay_log", "taps", "tap_bias", "skip", "mixer_gain",
    "residual", "expert_norm", "router", "ids", "w_gate", "w_up", "w_down",
)


def scratch():
    vmem = pltpu.VMEM
    dma = pltpu.SemaphoreType.DMA
    return {
        "padded": vmem((BLOCK + 16, CONV), bf16),
        "gate_v": vmem((BLOCK, D), bf16),
        "step_v": vmem((HEADS, BLOCK), f32),
        "step_bias_v": vmem((1, HEADS), f32),
        "decay_log_v": vmem((1, HEADS), f32),
        "taps_v": vmem((KERNEL, CONV), f32),
        "tap_bias_v": vmem((CONV,), f32),
        "mixer_gain_v": vmem((1, D), f32),
        "residual_v": vmem((BLOCK, D), bf16),
        "expert_norm_v": vmem((1, D), f32),
        "router_v": vmem((EXPERTS, D), bf16),
        "ids_v": vmem((TOPK, BLOCK), jnp.int32),
        "mixed": vmem((BLOCK, CONV), bf16),
        "cum": vmem((HEADS, BLOCK), f32),
        "delta": vmem((HEADS, BLOCK), f32),
        "cum_cols": vmem((BLOCK, 3 * HEADS), bf16),
        "tail_cols": vmem((BLOCK, 2 * HEADS), bf16),
        "entry_cols": vmem((BLOCK, 2 * HEADS), bf16),
        "last_rows": vmem((16, HEADS), bf16),
        "gram": vmem((BLOCK, BLOCK), f32),
        "piece": vmem((COLUMN, SENT, TILE), bf16),
        "first": vmem((COLUMN, SENT, TILE), bf16),
        "earlier": vmem((COLUMN, STATE, TILE), f32),
        "earlier_log": vmem((COLUMN, 8, TILE), f32),
        "total": vmem((SENT, TILE), bf16),
        "second": vmem((FLAT, SENT, TILE), bf16),
        "third": vmem((COLUMN, STATE, TILE), bf16),
        "state": vmem((COLUMN, STATE, TILE), bf16),
        "before": vmem((STATE, TILE), f32),
        "value": vmem((BLOCK, D), f32),
        "branch": vmem((BLOCK, D), f32),
        "hidden": vmem((BLOCK, D), bf16),
        "rows": vmem((16 * BLOCK, D), bf16),
        "meta": vmem((16, EXPERTS, BLOCK), f32),
        "wg": vmem((D, FF), bf16),
        "wu": vmem((D, FF), bf16),
        "wd": vmem((FF, D), bf16),
        "picked": vmem((4, 2 * PICK, D), bf16),
        "lent": vmem((4, PICK, D), bf16),
        "activated": vmem((2 * PICK, FF), bf16),
        "own_y": vmem((PICK, D), bf16),
        "lent_y": vmem((4, PICK, D), bf16),
        "back_y": vmem((4, PICK, D), bf16),
        "select": vmem((4, 2 * PICK, WIDE), bf16),
        "gate_col": vmem((4, 2 * PICK, BLOCK), f32),
        "part": vmem((16 * BLOCK, D), bf16),
        "land": vmem((15 * BLOCK, D), bf16),
        "done": vmem((BLOCK, D), bf16),
        "load_sem": dma((16,)),
        "halo_send": dma((1,)),
        "halo_recv": dma((1,)),
        "first_send": dma((COLUMN,)),
        "first_recv": dma((COLUMN,)),
        "second_send": dma((FLAT,)),
        "second_recv": dma((FLAT,)),
        "third_send": dma((COLUMN,)),
        "third_recv": dma((COLUMN,)),
        "row_send": dma((30,)),
        "row_recv": dma((30,)),
        "meta_send": dma((15,)),
        "meta_recv": dma((15,)),
        "lent_send": dma((4,)),
        "lent_recv": dma((4,)),
        "back_send": dma((4,)),
        "back_recv": dma((4,)),
        "sum_send": dma((30,)),
        "sum_recv": dma((30,)),
    }


def layer_kernel(*refs):
    names = INPUTS + ("out",) + tuple(scratch())
    r = types.SimpleNamespace(**dict(zip(names, refs)))
    ctx = lax.axis_index("ctx")
    depth = lax.axis_index("exp")
    core = ctx % 2
    column = ctx // 2
    me = core * 4 + depth
    score_rows, finish = mix_rows(r, ctx, depth, core, column, me)
    spread_rows(r, ctx, depth, core, column, score_rows)
    finish()


def mix_rows(r, ctx, depth, core, column, me):
    def member(m):
        return (column * 2 + m // 4, m % 4)

    def peer(c):
        return (c * 2 + core, depth)

    last = (me == COLUMN - 1).astype(jnp.int32)
    after = (((column + last) % FLAT) * 2 + ((me + 1) % COLUMN) // 4, (me + 1) % 4)
    initial = (me == 0).astype(jnp.int32)
    ahead = (
        ((column - initial + FLAT) % FLAT) * 2 + ((me + COLUMN - 1) % COLUMN) // 4,
        (me + COLUMN - 1) % 4,
    )

    def load(i, src, dst):
        copy = pltpu.make_async_copy(src, dst, r.load_sem.at[i])
        copy.start()
        return copy

    load_entry = load(0, r.entry, r.padded.at[pl.ds(16, BLOCK)])
    load_steps = [
        load(1, r.step, r.step_v),
        load(2, r.step_bias, r.step_bias_v),
        load(3, r.decay_log, r.decay_log_v),
    ]
    load_taps = [load(4, r.taps, r.taps_v), load(5, r.tap_bias, r.tap_bias_v)]
    load_rest = [
        load(6, r.gate, r.gate_v),
        load(7, r.residual, r.residual_v),
        load(8, r.mixer_gain, r.mixer_gain_v),
        load(9, r.expert_norm, r.expert_norm_v),
        load(10, r.router, r.router_v),
        load(11, r.ids, r.ids_v),
    ]
    for i, (src, dst) in enumerate(((r.w_gate, r.wg), (r.w_up, r.wu), (r.w_down, r.wd))):
        load(12 + i, src.at[0], dst)

    barrier = pltpu.get_barrier_semaphore()

    @pl.loop(1, COLUMN)
    def _(i):
        pl.semaphore_signal(
            barrier, inc=1, device_id=member((me + i) % COLUMN), device_id_type=MESH
        )

    @pl.loop(1, FLAT)
    def _(i):
        pl.semaphore_signal(
            barrier, inc=1, device_id=peer((column + i) % FLAT), device_id_type=MESH
        )

    @pl.when(me == COLUMN - 1)
    def _():
        pl.semaphore_signal(barrier, inc=1, device_id=after, device_id_type=MESH)

    @pl.when(me == 0)
    def _():
        pl.semaphore_signal(barrier, inc=1, device_id=ahead, device_id_type=MESH)

    row_id = lax.broadcasted_iota(jnp.int32, (BLOCK, BLOCK), 0)
    lane_id = lax.broadcasted_iota(jnp.int32, (BLOCK, BLOCK), 1)
    square_id = [lax.broadcasted_iota(jnp.int32, (HEADS, HEADS), axis) for axis in (0, 1)]

    def upend(row):
        spot = jnp.where(square_id[0] == square_id[1], row, 0.0)
        return jnp.sum(spot, axis=1, keepdims=True)

    for copy in load_steps:
        copy.wait()
    shifted = r.step_v[...] + upend(r.step_bias_v[...])
    width = jnp.maximum(shifted, 0.0) + jnp.log1p(jnp.exp(-jnp.abs(shifted)))
    logs = -width * jnp.exp(upend(r.decay_log_v[...]))
    summed = jnp.dot(
        logs, (row_id <= lane_id).astype(f32), precision=EXACT, preferred_element_type=f32
    )
    r.cum[...] = summed
    r.delta[...] = width

    def upright(a):
        return jnp.concatenate([a, jnp.zeros((BLOCK - HEADS, BLOCK), f32)], axis=0).T[:, :HEADS]

    summed_t = upright(summed)
    width_t = upright(width)
    final = summed_t[BLOCK - 1 :, :]
    r.cum_cols[...] = jnp.concatenate(split(summed_t, 3), axis=1)
    r.tail_cols[...] = jnp.concatenate(split(jnp.exp(final - summed_t) * width_t, 2), axis=1)
    r.entry_cols[...] = jnp.concatenate(split(jnp.exp(summed_t), 2), axis=1)
    terms = split(final, 3)
    r.last_rows[...] = jnp.concatenate(
        terms + [jnp.zeros((13, HEADS), bf16)], axis=0
    )

    def spread(m, copies, per, count):
        head = lax.broadcasted_iota(jnp.int32, (HEADS, count), 0)
        lane = lax.broadcasted_iota(jnp.int32, (HEADS, count), 1)
        one = (head == 4 * m + lane // per).astype(bf16)
        return one if copies == 1 else jnp.concatenate([one] * copies, axis=0)

    for copy in load_taps:
        copy.wait()
    load_entry.wait()

    def convolve(full, count, cols):
        acc = jnp.broadcast_to(r.tap_bias_v[cols][None, :], (count, 128))
        for j in range(KERNEL):
            acc = acc + r.taps_v[j : j + 1, cols] * full[13 + j : 13 + j + count]
        return (acc * sigmoid(acc)).astype(bf16)

    @pl.loop(0, CONV // 128)
    def _(n):
        cols = pl.ds(pl.multiple_of(n * 128, 128), 128)
        r.mixed[16:, cols] = convolve(r.padded[16:, cols].astype(f32), BLOCK - 16, cols)

    def weighted(m, low, count):
        cols = pl.ds(pl.multiple_of(m * TILE, TILE), TILE)
        span = pl.ds(low, count)
        weight = jnp.dot(
            r.tail_cols[span, :], spread(m, 2, HEAD_DIM, TILE), preferred_element_type=f32
        )
        source = r.mixed[span, D : D + STATE]
        return lax.dot_general(
            jnp.concatenate([source, source], axis=0),
            jnp.concatenate(split(r.mixed[span, cols].astype(f32) * weight, 2), axis=0),
            (((0,), (0,)), ((), ())),
            preferred_element_type=f32,
        )

    @pl.loop(0, COLUMN)
    def _(m):
        r.earlier[m] = weighted(m, 16, BLOCK - 16)

    pl.semaphore_wait(barrier, COLUMN + FLAT - 2 + last + initial)
    halo = remote(
        r.padded.at[pl.ds(BLOCK, 16)],
        r.padded.at[pl.ds(0, 16)],
        r.halo_send.at[0],
        r.halo_recv.at[0],
        after,
    )
    halo.start()

    for copy in load_rest:
        copy.wait()

    @pl.loop(0, COLUMN)
    def _(m):
        cols = pl.ds(pl.multiple_of(m * TILE, TILE), TILE)
        branch = r.gate_v[:, cols].astype(f32)
        r.branch[:, cols] = branch * sigmoid(branch)

    halo.wait_recv()
    keep = (ctx + depth > 0).astype(f32)

    @pl.loop(0, CONV // 128)
    def _(n):
        cols = pl.ds(pl.multiple_of(n * 128, 128), 128)
        full = jnp.concatenate(
            [r.padded[0:16, cols].astype(f32) * keep, r.padded[16:32, cols].astype(f32)], axis=0
        )
        r.mixed[0:16, cols] = convolve(full, 16, cols)

    in_map = r.mixed[:, D : D + STATE]
    out_map = r.mixed[:, D + STATE : D + 2 * STATE]

    def first_copy(m, slot):
        return remote(
            r.piece.at[m], r.first.at[slot], r.first_send.at[m], r.first_recv.at[slot], member(m)
        )

    def around(i):
        q = i // 2
        return ((core + i) % 2) * 4 + (depth + q + q // 2 - 2 * (q // 3)) % 4

    @pl.loop(0, COLUMN)
    def _(i):
        m = around(COLUMN - 1 - i)
        r.piece[m, 0:STATE, :] = (r.earlier[m] + weighted(m, 0, 16)).astype(bf16)
        r.piece[m, STATE:, :] = jnp.dot(
            r.last_rows[...], spread(m, 1, HEAD_DIM, TILE), preferred_element_type=f32
        ).astype(bf16)

        @pl.when(i < COLUMN - 1)
        def _():
            first_copy(m, me).start()

    r.first[me] = r.piece[me]

    cross = lax.dot_general(
        out_map, in_map, (((1,), (1,)), ((), ())), preferred_element_type=f32
    )
    r.gram[...] = jnp.where(row_id >= lane_id, cross, 0.0)

    def inside(m):
        cols = pl.ds(pl.multiple_of(m * TILE, TILE), TILE)
        upto = jnp.dot(r.cum_cols[...], spread(m, 3, BLOCK, 4 * BLOCK), preferred_element_type=f32)
        feature = r.mixed[:, cols]
        lane = lax.broadcasted_iota(jnp.int32, (BLOCK, TILE), 1) // HEAD_DIM
        highs, lows, blocks = [], [], []
        for j in range(4):
            head = pl.ds(4 * m + j, 1)
            gap = upto[:, BLOCK * j : BLOCK * (j + 1)] - r.cum[head, :]
            mix = jnp.exp(jnp.minimum(gap, 0.0)) * r.gram[...] * r.delta[head, :]
            mix = mix + jnp.where(row_id == lane_id, r.skip[4 * m + j], 0.0)
            high, low = split(mix, 2)
            highs.append(high)
            lows.append(low)
            blocks.append(jnp.where(lane == j, feature, jnp.zeros_like(feature)))
        diagonal = jnp.concatenate(blocks, axis=0)
        r.value[:, cols] = jnp.dot(
            jnp.concatenate(highs, axis=1), diagonal, preferred_element_type=f32
        ) + jnp.dot(jnp.concatenate(lows, axis=1), diagonal, preferred_element_type=f32)

    @pl.loop(0, COLUMN)
    def _(m):
        inside(m)

    @pl.loop(0, COLUMN)
    def _(m):
        @pl.when(m != me)
        def _():
            first_copy(m, m).wait_recv()

    def log_of(block):
        terms = block.astype(f32)
        return terms[0:1] + terms[1:2] + terms[2:3]

    run = jnp.zeros((STATE, TILE), f32)
    run_log = jnp.zeros((1, TILE), f32)
    for m in range(COLUMN):
        r.earlier[m] = run
        r.earlier_log[m] = jnp.broadcast_to(run_log, (8, TILE))
        log = log_of(r.first[m, STATE:, :])
        run = run * jnp.exp(log) + r.first[m, 0:STATE, :].astype(f32)
        run_log = run_log + log
    r.total[0:STATE, :] = run.astype(bf16)
    r.total[STATE:, :] = jnp.concatenate(
        split(run_log, 3) + [jnp.zeros((13, TILE), bf16)], axis=0
    )

    def second_copy(o):
        return remote(
            r.total,
            r.second.at[o],
            r.second_send.at[o],
            r.second_recv.at[o],
            peer((column + o) % FLAT),
        )

    @pl.loop(1, FLAT)
    def _(i):
        o = FLAT - i

        @pl.when(column + o < FLAT)
        def _():
            second_copy(o).start()

    r.before[...] = jnp.zeros((STATE, TILE), f32)

    @pl.loop(1, FLAT)
    def _(i):
        o = FLAT - i

        @pl.when(o <= column)
        def _():
            second_copy(o).wait_recv()
            r.before[...] = (
                r.before[...] * jnp.exp(log_of(r.second[o, STATE:, :]))
                + r.second[o, 0:STATE, :].astype(f32)
            )

    def third_copy(m, slot):
        return remote(
            r.third.at[m], r.state.at[slot], r.third_send.at[m], r.third_recv.at[slot], member(m)
        )

    @pl.loop(0, COLUMN)
    def _(i):
        m = around(COLUMN - 1 - i)
        r.third[m] = (r.before[...] * jnp.exp(r.earlier_log[m, 0:1, :]) + r.earlier[m]).astype(bf16)

        @pl.when(i < COLUMN - 1)
        def _():
            third_copy(m, me).start()

    r.state[me] = r.third[me]

    def fold(a):
        return a[:, :128] + a[:, 128:]

    def carry(i, square):
        m = around(i)

        @pl.when(i > 0)
        def _():
            third_copy(m, m).wait_recv()

        cols = pl.ds(pl.multiple_of(m * TILE, TILE), TILE)
        carried = jnp.dot(out_map, r.state[m], preferred_element_type=f32)
        weight = jnp.dot(r.entry_cols[...], spread(m, 2, HEAD_DIM, TILE), preferred_element_type=f32)
        v = (r.value[:, cols] + carried * weight) * r.branch[:, cols]
        r.value[:, cols] = v
        return square + fold(v * v)

    zero = jnp.zeros((BLOCK, 128), f32)
    square = lax.fori_loop(0, COLUMN, carry, zero)
    scale = lax.rsqrt(jnp.sum(square, axis=1, keepdims=True) * (1.0 / D) + 1e-05)

    def join(m, square):
        cols = pl.ds(pl.multiple_of(m * TILE, TILE), TILE)
        out = r.value[:, cols] * scale * r.mixer_gain_v[:, cols]
        kept = (r.residual_v[:, cols].astype(f32) + out).astype(bf16)
        r.hidden[:, cols] = kept
        wide = kept.astype(f32)
        return square + fold(wide * wide)

    square = lax.fori_loop(0, COLUMN, join, zero)
    again = lax.rsqrt(jnp.sum(square, axis=1, keepdims=True) * (1.0 / D) + 1e-05)

    @pl.loop(0, COLUMN)
    def _(m):
        cols = pl.ds(pl.multiple_of(m * TILE, TILE), TILE)
        r.rows[0:BLOCK, cols] = (
            r.hidden[:, cols].astype(f32) * again * r.expert_norm_v[:, cols]
        ).astype(bf16)

    def score_rows():
        logits = lax.dot_general(
            r.router_v[...], r.rows[0:BLOCK, :], (((1,), (1,)), ((), ())), preferred_element_type=f32
        )
        expert = lax.broadcasted_iota(jnp.int32, (EXPERTS, BLOCK), 0)
        chosen = expert < 0
        for k in range(TOPK):
            chosen = chosen | (expert == r.ids_v[k : k + 1, :])
        score = jnp.where(chosen, sigmoid(logits), 0.0)
        r.meta[0] = score / jnp.sum(score, axis=0, keepdims=True)

    def finish():
        halo.wait_send()

        @pl.loop(0, COLUMN)
        def _(m):
            @pl.when(m != me)
            def _():
                first_copy(m, me).wait_send()
                third_copy(m, me).wait_send()

        @pl.loop(1, FLAT)
        def _(o):
            @pl.when(column + o < FLAT)
            def _():
                second_copy(o).wait_send()

    return score_rows, finish


def spread_rows(r, ctx, depth, core, column, score_rows):
    x = column % 4
    y = column // 4
    sibling = ctx + 1 - 2 * core

    def device(first, second):
        to_y = (y + core * first + (1 - core) * second + 4) % 4
        to_x = (x + core * second + (1 - core) * first + 4) % 4
        return ((to_y * 4 + to_x) * 2 + core, depth)

    forth = (device(1, 0), device(0, 1))
    back = (device(-1, 0), device(0, -1))
    across = (sibling, depth)

    def ring(stage):
        return (0, 4, 0) if stage == 0 else (4 * (stage - 1), 1, 1)

    def row_copy(stage, kind):
        base, stride, axis = ring(stage)
        sem = 6 * stage + kind
        to = (forth, back)[kind % 2][axis]
        source, target, low = (
            (0, 1, 0), (0, 3, HALF), (0, 1, HALF), (0, 3, 0), (1, 2, 0), (3, 2, HALF)
        )[kind]
        return remote(
            r.rows.at[pl.ds((base + stride * source) * BLOCK + low, HALF)],
            r.rows.at[pl.ds((base + stride * target) * BLOCK + low, HALF)],
            r.row_send.at[sem],
            r.row_recv.at[sem],
            to,
        )

    def meta_copy(stage, kind):
        base, stride, axis = ring(stage)
        sem = 3 * stage + kind
        source, target, to = ((0, 1, forth), (0, 3, back), (1, 2, forth))[kind]
        return remote(
            r.meta.at[base + stride * source],
            r.meta.at[base + stride * target],
            r.meta_send.at[sem],
            r.meta_recv.at[sem],
            to[axis],
        )

    def sum_copy(stage, kind):
        base, stride, axis = ring(stage)
        sem = 6 * stage + kind
        to = (back, forth)[kind % 2][axis]
        source, low, place = (
            (2, 0, 0),
            (2, HALF, HALF),
            (1, HALF, BLOCK + HALF),
            (3, 0, 2 * BLOCK),
            (1, 0, BLOCK),
            (3, HALF, 2 * BLOCK + HALF),
        )[kind]
        return remote(
            r.part.at[pl.ds((base + stride * source) * BLOCK + low, HALF)],
            r.land.at[pl.ds(stage * 3 * BLOCK + place, HALF)],
            r.sum_send.at[sem],
            r.sum_recv.at[sem],
            to,
        )

    def lent_copy(k):
        return remote(
            r.lent.at[k],
            r.picked.at[k, pl.ds(PICK, PICK)],
            r.lent_send.at[k],
            r.lent_recv.at[k],
            across,
        )

    def back_copy(k):
        return remote(
            r.lent_y.at[k], r.back_y.at[k], r.back_send.at[k], r.back_recv.at[k], across
        )

    def send_rows(stage, *kinds):
        for kind in kinds:
            row_copy(stage, kind).start()

    def send_meta(stage):
        meta_copy(stage, 0).start()
        meta_copy(stage, 1).start()

    def pass_rows(stage, kind):
        row_copy(stage, kind).wait_recv()
        row_copy(stage, kind + 4).start()

    def pass_both(stage):
        meta_copy(stage, 0).wait_recv()
        meta_copy(stage, 2).start()
        pass_rows(stage, 0)
        pass_rows(stage, 1)

    def arrive(stage):
        for kind in (1, 2):
            meta_copy(stage, kind).wait_recv()
        for kind in (2, 3, 4, 5):
            row_copy(stage, kind).wait_recv()

    before = (
        lax.broadcasted_iota(jnp.int32, (BLOCK, BLOCK), 0)
        < lax.broadcasted_iota(jnp.int32, (BLOCK, BLOCK), 1)
    ).astype(bf16)
    slot_row = lax.broadcasted_iota(jnp.int32, (PICK, WIDE), 0).astype(f32)

    def choose(k):
        gate = jnp.concatenate(
            [
                r.meta[4 * k + j, pl.ds(expert, 1), :]
                for expert in (ctx, sibling)
                for j in range(4)
            ],
            axis=0,
        )
        live = gate > 0.0
        rank = jnp.dot(live.astype(bf16), before, preferred_element_type=f32)
        shift = (lax.broadcasted_iota(jnp.int32, (8, BLOCK), 0) % 4).astype(f32) * CAP
        slot = jnp.where(live, rank + shift, -1.0)
        for half in range(2):
            lanes = jnp.concatenate([slot[4 * half + j : 4 * half + j + 1] for j in range(4)], axis=1)
            value = jnp.concatenate([gate[4 * half + j : 4 * half + j + 1] for j in range(4)], axis=1)
            hit = slot_row == lanes
            span = pl.ds(half * PICK, PICK)
            r.select[k, span, :] = jnp.where(hit, 1.0, 0.0).astype(bf16)
            total = jnp.sum(jnp.where(hit, value, 0.0), axis=1, keepdims=True)
            r.gate_col[k, span, :] = jnp.broadcast_to(total, (PICK, BLOCK))

        @pl.loop(0, 8)
        def _(n):
            cols = pl.ds(pl.multiple_of(n * 256, 256), 256)
            got = jnp.dot(
                r.select[k], r.rows[pl.ds(k * WIDE, WIDE), cols], preferred_element_type=f32
            ).astype(bf16)
            r.picked[k, pl.ds(0, PICK), cols] = got[:PICK]
            r.lent[k, :, cols] = got[PICK:]

        lent_copy(k).start()

    def feed(k):
        lent_copy(k).wait_recv()

        @pl.loop(0, 3)
        def _(f):
            cols = pl.ds(pl.multiple_of(f * 256, 256), 256)
            gate = jnp.dot(r.picked[k], r.wg[:, cols], preferred_element_type=f32)
            up = jnp.dot(r.picked[k], r.wu[:, cols], preferred_element_type=f32)
            r.activated[:, cols] = (gate * sigmoid(gate) * up).astype(bf16)

    def produce(k):
        @pl.loop(0, 8)
        def _(n):
            cols = pl.ds(pl.multiple_of(n * 256, 256), 256)
            made = jnp.dot(r.activated[...], r.wd[:, cols], preferred_element_type=f32)
            scale = r.gate_col[k, pl.ds(0, PICK), :]
            r.own_y[:, cols] = (
                made[:PICK] * jnp.concatenate([scale, scale], axis=1)
            ).astype(bf16)
            r.lent_y[k, :, cols] = made[PICK:].astype(bf16)

        back_copy(k).start()

    def combine(k):
        back_copy(k).wait_recv()

        @pl.loop(0, 8)
        def _(n):
            cols = pl.ds(pl.multiple_of(n * 256, 256), 256)
            scale = r.gate_col[k, pl.ds(PICK, PICK), :]
            other = (
                r.back_y[k, :, cols].astype(f32) * jnp.concatenate([scale, scale], axis=1)
            ).astype(bf16)
            both = jnp.concatenate([r.own_y[:, cols], other], axis=0)
            r.part[pl.ds(k * WIDE, WIDE), cols] = lax.dot_general(
                r.select[k], both, (((0,), (0,)), ((), ())), preferred_element_type=f32
            ).astype(bf16)

    def add_into(block, low, count, places):
        @pl.loop(0, count // 16)
        def _(i):
            span = pl.ds(pl.multiple_of(block * BLOCK + low + i * 16, 16), 16)
            total = r.part[span, :].astype(f32)
            for place in places:
                total += r.land[pl.ds(pl.multiple_of(place + i * 16, 16), 16), :].astype(f32)
            r.part[span, :] = total.astype(bf16)

    def sum_first(stage):
        for kind in range(4):
            sum_copy(stage, kind).start()

    def sum_second(stage):
        base, stride, _ = ring(stage)
        place = stage * 3 * BLOCK
        sum_copy(stage, 0).wait_recv()
        add_into(base + stride, 0, HALF, (place,))
        sum_copy(stage, 4).start()
        sum_copy(stage, 1).wait_recv()
        add_into(base + 3 * stride, HALF, HALF, (place + HALF,))
        sum_copy(stage, 5).start()

    def sum_last(stage):
        base, _, _ = ring(stage)
        place = stage * 3 * BLOCK
        for kind in (2, 3, 4, 5):
            sum_copy(stage, kind).wait_recv()
        if stage > 0:
            add_into(base, 0, BLOCK, (place + BLOCK, place + 2 * BLOCK))

    send_rows(0, 0, 1, 2, 3)
    send_rows(1, 0, 1, 2, 3)
    score_rows()
    send_meta(0)
    send_meta(1)
    meta_copy(0, 0).wait_recv()
    meta_copy(0, 2).start()
    send_meta(2)
    pass_rows(0, 0)
    send_rows(2, 0, 3)
    meta_copy(0, 1).wait_recv()
    send_meta(4)
    pass_rows(0, 1)
    row_copy(0, 2).wait_recv()
    send_rows(2, 1, 2)
    pass_both(1)
    row_copy(0, 3).wait_recv()
    send_rows(4, 1, 2, 0, 3)
    pass_both(2)
    meta_copy(0, 2).wait_recv()
    send_meta(3)
    row_copy(0, 4).wait_recv()
    send_rows(3, 0, 3)
    row_copy(0, 5).wait_recv()
    send_rows(3, 1, 2)
    arrive(1)
    choose(0)
    for i, (src, dst) in enumerate(((r.w_gate, r.wg), (r.w_up, r.wu), (r.w_down, r.wd))):
        pltpu.make_async_copy(src.at[0], dst, r.load_sem.at[12 + i]).wait()
    pass_both(4)
    feed(0)
    produce(0)
    arrive(2)
    choose(1)
    combine(0)
    pass_both(3)
    sum_first(1)
    feed(1)
    produce(1)
    arrive(4)
    choose(3)
    combine(1)
    sum_first(2)
    feed(3)
    produce(3)
    arrive(3)
    choose(2)
    combine(3)
    sum_first(4)
    sum_second(2)
    feed(2)
    produce(2)
    sum_second(4)
    combine(2)
    sum_first(3)
    sum_last(2)
    sum_last(4)
    sum_second(3)
    sum_second(1)
    sum_last(3)
    sum_first(0)
    sum_last(1)
    sum_second(0)
    sum_last(0)

    @pl.loop(0, BLOCK // 16)
    def _(i):
        span = pl.ds(pl.multiple_of(i * 16, 16), 16)
        total = r.part[span, :].astype(f32)
        for place in (BLOCK, 2 * BLOCK):
            total += r.land[pl.ds(pl.multiple_of(place + i * 16, 16), 16), :].astype(f32)
        r.done[span, :] = (r.hidden[span, :].astype(f32) + total).astype(bf16)

    store = pltpu.make_async_copy(r.done, r.out, r.load_sem.at[15])
    store.start()
    for stage in range(5):
        for kind in range(6):
            row_copy(stage, kind).wait_send()
            sum_copy(stage, kind).wait_send()
        for kind in range(3):
            meta_copy(stage, kind).wait_send()
    for k in range(4):
        lent_copy(k).wait_send()
        back_copy(k).wait_send()
    store.wait()


def layer(
    filter_entry_array,
    gate_input,
    step_unshifted,
    step_bias,
    decay_log,
    conv_weight,
    conv_bias,
    skip_gain,
    mixer_gain,
    residual,
    expert_norm,
    router_weight,
    expert_ids,
    w_gate,
    w_up,
    w_down,
):
    hbm = pl.BlockSpec(memory_space=pl.ANY)
    specs = [hbm] * len(INPUTS)
    specs[INPUTS.index("skip")] = pl.BlockSpec(memory_space=pltpu.SMEM)
    return pl.pallas_call(
        layer_kernel,
        out_shape=jax.ShapeDtypeStruct((BLOCK, D), bf16),
        in_specs=specs,
        out_specs=hbm,
        scratch_shapes=list(scratch().values()),
        compiler_params=pltpu.CompilerParams(
            collective_id=0, has_side_effects=True, vmem_limit_bytes=62 * 1024 * 1024
        ),
    )(
        filter_entry_array,
        gate_input,
        step_unshifted,
        step_bias[None, :],
        decay_log[None, :],
        conv_weight,
        conv_bias,
        skip_gain,
        mixer_gain[None, :],
        residual,
        expert_norm[None, :],
        router_weight.T,
        expert_ids.T,
        w_gate,
        w_up,
        w_down,
    )


def solution(mesh):
    rows = P(("ctx", "exp"), None)
    shared = P()
    owner = P("ctx", None, None)
    return jax.shard_map(
        layer,
        mesh=mesh,
        in_specs=(
            rows,
            rows,
            P(None, ("ctx", "exp")),
            shared,
            shared,
            shared,
            shared,
            shared,
            shared,
            rows,
            shared,
            shared,
            rows,
            owner,
            owner,
            owner,
        ),
        out_specs=rows,
        check_vma=False,
    )
```

```python
import types

import jax
import jax.numpy as jnp
from jax import lax
from jax.experimental import pallas as pl
from jax.experimental.pallas import tpu as pltpu
from jax.sharding import PartitionSpec as P

D = 2048
HEADS = 32
HEAD_DIM = 64
STATE = 64
KERNEL = 4
TOPK = 8
CAP = 40
CONV = 2176
FF = 768
EXPERTS = 32
BLOCK = 128
HALF = BLOCK // 2
PICK = 4 * CAP
WIDE = 4 * BLOCK
COLUMN = 8
TILE = D // COLUMN
FLAT = 16
SENT = STATE + 16
PAIR = 2 * CAP

EXACT = lax.Precision.HIGHEST
MESH = pl.DeviceIdType.MESH
f32 = jnp.float32
bf16 = jnp.bfloat16


def sigmoid(value):
    return 1.0 / (1.0 + jnp.exp(-value))


def split(value, count):
    pieces = []
    for _ in range(count):
        piece = value.astype(bf16)
        pieces.append(piece)
        value = value - piece.astype(f32)
    return pieces


def remote(src, dst, send, recv, to):
    return pltpu.make_async_remote_copy(
        src_ref=src, dst_ref=dst, send_sem=send, recv_sem=recv, device_id=to, device_id_type=MESH
    )


INPUTS = (
    "entry", "gate", "step", "step_bias", "decay_log", "taps", "tap_bias", "skip", "mixer_gain",
    "residual", "expert_norm", "router", "ids", "w_gate", "w_up", "w_down",
)


def scratch():
    vmem = pltpu.VMEM
    dma = pltpu.SemaphoreType.DMA
    return {
        "padded": vmem((BLOCK + 16, CONV), bf16),
        "gate_v": vmem((BLOCK, D), bf16),
        "step_v": vmem((HEADS, BLOCK), f32),
        "step_bias_v": vmem((1, HEADS), f32),
        "decay_log_v": vmem((1, HEADS), f32),
        "taps_v": vmem((KERNEL, CONV), f32),
        "tap_bias_v": vmem((CONV,), f32),
        "mixer_gain_v": vmem((1, D), f32),
        "residual_v": vmem((BLOCK, D), bf16),
        "expert_norm_v": vmem((1, D), f32),
        "router_v": vmem((EXPERTS, D), bf16),
        "ids_v": vmem((TOPK, BLOCK), jnp.int32),
        "mixed": vmem((BLOCK, CONV), bf16),
        "cum": vmem((HEADS, BLOCK), f32),
        "delta": vmem((HEADS, BLOCK), f32),
        "cum_cols": vmem((BLOCK, 3 * HEADS), bf16),
        "tail_cols": vmem((BLOCK, 2 * HEADS), bf16),
        "entry_cols": vmem((BLOCK, 2 * HEADS), bf16),
        "last_rows": vmem((16, HEADS), bf16),
        "gram": vmem((BLOCK, BLOCK), f32),
        "piece": vmem((COLUMN, SENT, TILE), bf16),
        "first": vmem((COLUMN, SENT, TILE), bf16),
        "earlier": vmem((COLUMN, STATE, TILE), f32),
        "earlier_log": vmem((COLUMN, 8, TILE), f32),
        "total": vmem((SENT, TILE), bf16),
        "second": vmem((FLAT, SENT, TILE), bf16),
        "third": vmem((COLUMN, STATE, TILE), bf16),
        "state": vmem((COLUMN, STATE, TILE), bf16),
        "before": vmem((STATE, TILE), f32),
        "value": vmem((BLOCK, D), f32),
        "branch": vmem((BLOCK, D), f32),
        "hidden": vmem((BLOCK, D), bf16),
        "rows": vmem((16 * BLOCK, D), bf16),
        "meta": vmem((16, EXPERTS, BLOCK), f32),
        "wg": vmem((D, FF), bf16),
        "wu": vmem((D, FF), bf16),
        "wd": vmem((FF, D), bf16),
        "picked": vmem((4, 2 * PICK, D), bf16),
        "lent": vmem((4, PICK, D), bf16),
        "activated": vmem((2 * PICK, FF), bf16),
        "own_y": vmem((PICK, D), bf16),
        "lent_y": vmem((4, PICK, D), bf16),
        "back_y": vmem((4, PICK, D), bf16),
        "select": vmem((4, 2 * PICK, WIDE), bf16),
        "weigh": vmem((4, WIDE, 2 * PICK), bf16),
        "part": vmem((16 * BLOCK, D), bf16),
        "land": vmem((3 * BLOCK + 4 * (2 * PAIR + BLOCK), D), bf16),
        "pack": vmem((8, PAIR, D), bf16),
        "fold": vmem((8, BLOCK, PAIR), bf16),
        "done": vmem((BLOCK, D), bf16),
        "load_sem": dma((16,)),
        "halo_send": dma((1,)),
        "halo_recv": dma((1,)),
        "first_send": dma((COLUMN,)),
        "first_recv": dma((COLUMN,)),
        "second_send": dma((FLAT,)),
        "second_recv": dma((FLAT,)),
        "third_send": dma((COLUMN,)),
        "third_recv": dma((COLUMN,)),
        "row_send": dma((22,)),
        "row_recv": dma((22,)),
        "meta_send": dma((15,)),
        "meta_recv": dma((15,)),
        "lent_send": dma((4,)),
        "lent_recv": dma((4,)),
        "back_send": dma((4,)),
        "back_recv": dma((4,)),
        "sum_send": dma((18,)),
        "sum_recv": dma((18,)),
    }


def layer_kernel(*refs):
    names = INPUTS + ("out",) + tuple(scratch())
    r = types.SimpleNamespace(**dict(zip(names, refs)))
    ctx = lax.axis_index("ctx")
    depth = lax.axis_index("exp")
    core = ctx % 2
    column = ctx // 2
    me = core * 4 + depth
    finish_rows, score_rows, finish = mix_rows(r, ctx, depth, core, column, me)
    spread_rows(r, ctx, depth, core, column, finish_rows, score_rows)
    finish()


def mix_rows(r, ctx, depth, core, column, me):
    def member(m):
        return (column * 2 + m // 4, m % 4)

    def peer(c):
        return (c * 2 + core, depth)

    last = (me == COLUMN - 1).astype(jnp.int32)
    after = (((column + last) % FLAT) * 2 + ((me + 1) % COLUMN) // 4, (me + 1) % 4)
    initial = (me == 0).astype(jnp.int32)
    ahead = (
        ((column - initial + FLAT) % FLAT) * 2 + ((me + COLUMN - 1) % COLUMN) // 4,
        (me + COLUMN - 1) % 4,
    )

    barrier = pltpu.get_barrier_semaphore()

    @pl.loop(1, COLUMN)
    def _(i):
        pl.semaphore_signal(
            barrier, inc=1, device_id=member((me + i) % COLUMN), device_id_type=MESH
        )

    @pl.loop(1, FLAT)
    def _(i):
        pl.semaphore_signal(
            barrier, inc=1, device_id=peer((column + i) % FLAT), device_id_type=MESH
        )

    @pl.when(me == COLUMN - 1)
    def _():
        pl.semaphore_signal(barrier, inc=1, device_id=after, device_id_type=MESH)

    @pl.when(me == 0)
    def _():
        pl.semaphore_signal(barrier, inc=1, device_id=ahead, device_id_type=MESH)

    def load(i, src, dst):
        copy = pltpu.make_async_copy(src, dst, r.load_sem.at[i])
        copy.start()
        return copy

    load_entry = load(0, r.entry, r.padded.at[pl.ds(16, BLOCK)])
    load_steps = [
        load(1, r.step, r.step_v),
        load(2, r.step_bias, r.step_bias_v),
        load(3, r.decay_log, r.decay_log_v),
    ]
    load_taps = [load(4, r.taps, r.taps_v), load(5, r.tap_bias, r.tap_bias_v)]
    load_rest = [
        load(6, r.gate, r.gate_v),
        load(7, r.residual, r.residual_v),
        load(8, r.mixer_gain, r.mixer_gain_v),
        load(9, r.expert_norm, r.expert_norm_v),
        load(10, r.router, r.router_v),
        load(11, r.ids, r.ids_v),
    ]
    for i, (src, dst) in enumerate(((r.w_gate, r.wg), (r.w_up, r.wu), (r.w_down, r.wd))):
        load(12 + i, src.at[0], dst)

    row_id = lax.broadcasted_iota(jnp.int32, (BLOCK, BLOCK), 0)
    lane_id = lax.broadcasted_iota(jnp.int32, (BLOCK, BLOCK), 1)
    square_id = [lax.broadcasted_iota(jnp.int32, (HEADS, HEADS), axis) for axis in (0, 1)]

    def upend(row):
        spot = jnp.where(square_id[0] == square_id[1], row, 0.0)
        return jnp.sum(spot, axis=1, keepdims=True)

    for copy in load_steps:
        copy.wait()
    shifted = r.step_v[...] + upend(r.step_bias_v[...])
    width = jnp.maximum(shifted, 0.0) + jnp.log1p(jnp.exp(-jnp.abs(shifted)))
    logs = -width * jnp.exp(upend(r.decay_log_v[...]))
    summed = jnp.dot(
        logs, (row_id <= lane_id).astype(f32), precision=EXACT, preferred_element_type=f32
    )
    r.cum[...] = summed
    r.delta[...] = width

    def upright(a):
        return jnp.concatenate([a, jnp.zeros((BLOCK - HEADS, BLOCK), f32)], axis=0).T[:, :HEADS]

    summed_t = upright(summed)
    width_t = upright(width)
    final = summed_t[BLOCK - 1 :, :]
    r.cum_cols[...] = jnp.concatenate(split(summed_t, 3), axis=1)
    r.tail_cols[...] = jnp.concatenate(split(jnp.exp(final - summed_t) * width_t, 2), axis=1)
    r.entry_cols[...] = jnp.concatenate(split(jnp.exp(summed_t), 2), axis=1)
    terms = split(final, 3)
    r.last_rows[...] = jnp.concatenate(
        terms + [jnp.zeros((13, HEADS), bf16)], axis=0
    )

    def spread(m, copies, per, count):
        head = lax.broadcasted_iota(jnp.int32, (HEADS, count), 0)
        lane = lax.broadcasted_iota(jnp.int32, (HEADS, count), 1)
        one = (head == 4 * m + lane // per).astype(bf16)
        return one if copies == 1 else jnp.concatenate([one] * copies, axis=0)

    for copy in load_taps:
        copy.wait()
    load_entry.wait()

    def convolve(full, count, cols):
        acc = jnp.broadcast_to(r.tap_bias_v[cols][None, :], (count, 128))
        for j in range(KERNEL):
            acc = acc + r.taps_v[j : j + 1, cols] * full[13 + j : 13 + j + count]
        return (acc * sigmoid(acc)).astype(bf16)

    @pl.loop(0, CONV // 128, unroll=1)
    def _(n):
        cols = pl.ds(pl.multiple_of(n * 128, 128), 128)
        r.mixed[16:, cols] = convolve(r.padded[16:, cols].astype(f32), BLOCK - 16, cols)

    def weighted(m, low, count):
        cols = pl.ds(pl.multiple_of(m * TILE, TILE), TILE)
        span = pl.ds(low, count)
        weight = jnp.dot(
            r.tail_cols[span, :], spread(m, 2, HEAD_DIM, TILE), preferred_element_type=f32
        )
        source = r.mixed[span, D : D + STATE]
        return lax.dot_general(
            jnp.concatenate([source, source], axis=0),
            jnp.concatenate(split(r.mixed[span, cols].astype(f32) * weight, 2), axis=0),
            (((0,), (0,)), ((), ())),
            preferred_element_type=f32,
        )

    @pl.loop(0, COLUMN, unroll=2)
    def _(m):
        r.earlier[m] = weighted(m, 16, BLOCK - 16)

    for k in range(4):
        for block in (2, 3 - 2 * (k % 2)):
            low = (4 * k + block) * BLOCK + PAIR
            r.rows[low : low + BLOCK - PAIR, :] = jnp.zeros((BLOCK - PAIR, D), bf16)

    pl.semaphore_wait(barrier, COLUMN + FLAT - 2 + last + initial)
    halo = remote(
        r.padded.at[pl.ds(BLOCK, 16)],
        r.padded.at[pl.ds(0, 16)],
        r.halo_send.at[0],
        r.halo_recv.at[0],
        after,
    )
    halo.start()

    for copy in load_rest:
        copy.wait()

    @pl.loop(0, COLUMN, unroll=2)
    def _(m):
        cols = pl.ds(pl.multiple_of(m * TILE, TILE), TILE)
        branch = r.gate_v[:, cols].astype(f32)
        r.branch[:, cols] = branch * sigmoid(branch)

    halo.wait_recv()
    keep = (ctx + depth > 0).astype(f32)

    @pl.loop(0, CONV // 128, unroll=1)
    def _(n):
        cols = pl.ds(pl.multiple_of(n * 128, 128), 128)
        full = jnp.concatenate(
            [r.padded[0:16, cols].astype(f32) * keep, r.padded[16:32, cols].astype(f32)], axis=0
        )
        r.mixed[0:16, cols] = convolve(full, 16, cols)

    in_map = r.mixed[:, D : D + STATE]
    out_map = r.mixed[:, D + STATE : D + 2 * STATE]

    def first_copy(m, slot):
        return remote(
            r.piece.at[m], r.first.at[slot], r.first_send.at[m], r.first_recv.at[slot], member(m)
        )

    def around(i):
        q = i // 2
        return ((core + i) % 2) * 4 + (depth + q + q // 2 - 2 * (q // 3)) % 4

    @pl.loop(0, COLUMN, unroll=2)
    def _(i):
        m = around(COLUMN - 1 - i)
        r.piece[m, 0:STATE, :] = (r.earlier[m] + weighted(m, 0, 16)).astype(bf16)
        r.piece[m, STATE:, :] = jnp.dot(
            r.last_rows[...], spread(m, 1, HEAD_DIM, TILE), preferred_element_type=f32
        ).astype(bf16)

        @pl.when(i < COLUMN - 1)
        def _():
            first_copy(m, me).start()

    r.first[me] = r.piece[me]

    cross = lax.dot_general(
        out_map, in_map, (((1,), (1,)), ((), ())), preferred_element_type=f32
    )
    r.gram[...] = jnp.where(row_id >= lane_id, cross, 0.0)

    def inside(m):
        cols = pl.ds(pl.multiple_of(m * TILE, TILE), TILE)
        upto = jnp.dot(r.cum_cols[...], spread(m, 3, BLOCK, 4 * BLOCK), preferred_element_type=f32)
        feature = r.mixed[:, cols]
        lane = lax.broadcasted_iota(jnp.int32, (BLOCK, TILE), 1) // HEAD_DIM
        highs, lows, blocks = [], [], []
        for j in range(4):
            head = pl.ds(4 * m + j, 1)
            gap = upto[:, BLOCK * j : BLOCK * (j + 1)] - r.cum[head, :]
            mix = jnp.exp(jnp.minimum(gap, 0.0)) * r.gram[...] * r.delta[head, :]
            mix = mix + jnp.where(row_id == lane_id, r.skip[4 * m + j], 0.0)
            high, low = split(mix, 2)
            highs.append(high)
            lows.append(low)
            blocks.append(jnp.where(lane == j, feature, jnp.zeros_like(feature)))
        diagonal = jnp.concatenate(blocks, axis=0)
        r.value[:, cols] = jnp.dot(
            jnp.concatenate(highs, axis=1), diagonal, preferred_element_type=f32
        ) + jnp.dot(jnp.concatenate(lows, axis=1), diagonal, preferred_element_type=f32)

    @pl.loop(0, COLUMN // 2, unroll=2)
    def _(m):
        inside(m)

    @pl.loop(0, COLUMN, unroll=2)
    def _(m):
        @pl.when(m != me)
        def _():
            first_copy(m, m).wait_recv()

    def log_of(block):
        terms = block.astype(f32)
        return terms[0:1] + terms[1:2] + terms[2:3]

    run = jnp.zeros((STATE, TILE), f32)
    run_log = jnp.zeros((1, TILE), f32)
    for m in range(COLUMN):
        r.earlier[m] = run
        r.earlier_log[m] = jnp.broadcast_to(run_log, (8, TILE))
        log = log_of(r.first[m, STATE:, :])
        run = run * jnp.exp(log) + r.first[m, 0:STATE, :].astype(f32)
        run_log = run_log + log
    r.total[0:STATE, :] = run.astype(bf16)
    r.total[STATE:, :] = jnp.concatenate(
        split(run_log, 3) + [jnp.zeros((13, TILE), bf16)], axis=0
    )

    def second_copy(o):
        return remote(
            r.total,
            r.second.at[o],
            r.second_send.at[o],
            r.second_recv.at[o],
            peer((column + o) % FLAT),
        )

    @pl.loop(1, FLAT)
    def _(i):
        o = FLAT - i

        @pl.when(column + o < FLAT)
        def _():
            second_copy(o).start()

    @pl.loop(COLUMN // 2, COLUMN, unroll=2)
    def _(m):
        inside(m)

    @pl.loop(0, COLUMN, unroll=2)
    def _(m):
        cols = pl.ds(pl.multiple_of(m * TILE, TILE), TILE)
        weight = jnp.dot(r.entry_cols[...], spread(m, 2, HEAD_DIM, TILE), preferred_element_type=f32)
        branch = r.branch[:, cols]
        r.value[:, cols] = r.value[:, cols] * branch
        r.branch[:, cols] = weight * branch

    r.before[...] = jnp.zeros((STATE, TILE), f32)

    @pl.loop(1, FLAT)
    def _(i):
        o = FLAT - i

        @pl.when(o <= column)
        def _():
            second_copy(o).wait_recv()
            r.before[...] = (
                r.before[...] * jnp.exp(log_of(r.second[o, STATE:, :]))
                + r.second[o, 0:STATE, :].astype(f32)
            )

    def third_copy(m, slot):
        return remote(
            r.third.at[m], r.state.at[slot], r.third_send.at[m], r.third_recv.at[slot], member(m)
        )

    @pl.loop(0, COLUMN, unroll=2)
    def _(i):
        m = around(COLUMN - 1 - i)
        r.third[m] = (r.before[...] * jnp.exp(r.earlier_log[m, 0:1, :]) + r.earlier[m]).astype(bf16)

        @pl.when(i < COLUMN - 1)
        def _():
            third_copy(m, me).start()

    r.state[me] = r.third[me]

    def fold(a):
        return a[:, :128] + a[:, 128:]

    def carry(i, square):
        m = around(i)

        @pl.when(i > 0)
        def _():
            third_copy(m, m).wait_recv()

        cols = pl.ds(pl.multiple_of(m * TILE, TILE), TILE)
        carried = jnp.dot(out_map, r.state[m], preferred_element_type=f32)
        v = r.value[:, cols] + carried * r.branch[:, cols]
        r.value[:, cols] = v
        return square + fold(v * v)

    zero = jnp.zeros((BLOCK, 128), f32)
    square = lax.fori_loop(0, COLUMN, carry, zero, unroll=2)
    scale = lax.rsqrt(jnp.sum(square, axis=1, keepdims=True) * (1.0 / D) + 1e-05)

    def finish_rows(half):
        span = pl.ds(half * HALF, HALF)
        mine = scale[half * HALF : (half + 1) * HALF]

        def join(m, square):
            cols = pl.ds(pl.multiple_of(m * TILE, TILE), TILE)
            out = r.value[span, cols] * mine * r.mixer_gain_v[:, cols]
            kept = (r.residual_v[span, cols].astype(f32) + out).astype(bf16)
            r.hidden[span, cols] = kept
            wide = kept.astype(f32)
            return square + fold(wide * wide)

        square = lax.fori_loop(0, COLUMN, join, jnp.zeros((HALF, 128), f32), unroll=2)
        again = lax.rsqrt(jnp.sum(square, axis=1, keepdims=True) * (1.0 / D) + 1e-05)

        @pl.loop(0, COLUMN, unroll=2)
        def _(m):
            cols = pl.ds(pl.multiple_of(m * TILE, TILE), TILE)
            r.rows[span, cols] = (
                r.hidden[span, cols].astype(f32) * again * r.expert_norm_v[:, cols]
            ).astype(bf16)

    def score_rows():
        logits = lax.dot_general(
            r.router_v[...], r.rows[0:BLOCK, :], (((1,), (1,)), ((), ())), preferred_element_type=f32
        )
        expert = lax.broadcasted_iota(jnp.int32, (EXPERTS, BLOCK), 0)
        chosen = expert < 0
        for k in range(TOPK):
            chosen = chosen | (expert == r.ids_v[k : k + 1, :])
        score = jnp.where(chosen, sigmoid(logits), 0.0)
        r.meta[0] = score / jnp.sum(score, axis=0, keepdims=True)

    def finish():
        halo.wait_send()

        @pl.loop(0, COLUMN, unroll=2)
        def _(m):
            @pl.when(m != me)
            def _():
                first_copy(m, me).wait_send()
                third_copy(m, me).wait_send()

        @pl.loop(1, FLAT)
        def _(o):
            @pl.when(column + o < FLAT)
            def _():
                second_copy(o).wait_send()

    return finish_rows, score_rows, finish


def spread_rows(r, ctx, depth, core, column, finish_rows, score_rows):
    x = column % 4
    y = column // 4
    sibling = ctx + 1 - 2 * core

    def device(first, second):
        to_y = (y + core * first + (1 - core) * second + 4) % 4
        to_x = (x + core * second + (1 - core) * first + 4) % 4
        return ((to_y * 4 + to_x) * 2 + core, depth)

    forth = (device(1, 0), device(0, 1))
    back = (device(-1, 0), device(0, -1))
    across = (sibling, depth)

    def ring(stage):
        return (0, 4, 0) if stage == 0 else (4 * (stage - 1), 1, 1)

    def sides(k):
        ahead, behind = (forth[1], back[1]) if k % 2 == 0 else (back[1], forth[1])
        return ahead, behind, 1 + 2 * (k % 2), 3 - 2 * (k % 2)

    def block_rows(block, low, count):
        return pl.ds(block * BLOCK + low, count)

    def row_copy(kind):
        to = (forth, back)[kind % 2][0]
        source, target, low = (
            (0, 4, 0), (0, 12, HALF), (0, 4, HALF), (0, 12, 0), (4, 8, 0), (12, 8, HALF)
        )[kind]
        return remote(
            r.rows.at[block_rows(source, low, HALF)],
            r.rows.at[block_rows(target, low, HALF)],
            r.row_send.at[kind],
            r.row_recv.at[kind],
            to,
        )

    def group_copy(k, kind):
        ahead, behind, whole, picked = sides(k)
        sem = 6 + 4 * k + kind
        if kind < 2:
            source = r.rows.at[block_rows(4 * k, kind * HALF, HALF)]
            target, to = block_rows(4 * k + whole, kind * HALF, HALF), ahead
        elif kind == 2:
            source, target, to = r.pack.at[k], block_rows(4 * k + picked, 0, PAIR), behind
        else:
            source, target, to = r.pack.at[4 + k], block_rows(4 * k + 2, 0, PAIR), ahead
        return remote(source, r.rows.at[target], r.row_send.at[sem], r.row_recv.at[sem], to)

    def meta_copy(stage, kind):
        base, stride, axis = ring(stage)
        sem = 3 * stage + kind
        source, target, to = ((0, 1, forth), (0, 3, back), (1, 2, forth))[kind]
        return remote(
            r.meta.at[base + stride * source],
            r.meta.at[base + stride * target],
            r.meta_send.at[sem],
            r.meta_recv.at[sem],
            to[axis],
        )

    def sum_copy(kind):
        to = (back, forth)[kind % 2][0]
        source, low, place = (
            (8, 0, 0),
            (8, HALF, HALF),
            (4, HALF, BLOCK + HALF),
            (12, 0, 2 * BLOCK),
            (4, 0, BLOCK),
            (12, HALF, 2 * BLOCK + HALF),
        )[kind]
        return remote(
            r.part.at[block_rows(source, low, HALF)],
            r.land.at[pl.ds(place, HALF)],
            r.sum_send.at[kind],
            r.sum_recv.at[kind],
            to,
        )

    def group_land(k, kind):
        return 3 * BLOCK + k * (2 * PAIR + BLOCK) + kind * PAIR

    def group_sum(k, kind):
        ahead, behind, whole, picked = sides(k)
        sem = 6 + 3 * k + kind
        block, count, to = ((2, PAIR, behind), (picked, PAIR, ahead), (whole, BLOCK, behind))[kind]
        return remote(
            r.part.at[block_rows(4 * k + block, 0, count)],
            r.land.at[pl.ds(group_land(k, kind), count)],
            r.sum_send.at[sem],
            r.sum_recv.at[sem],
            to,
        )

    def lent_copy(k):
        return remote(
            r.lent.at[k],
            r.picked.at[k, pl.ds(PICK, PICK)],
            r.lent_send.at[k],
            r.lent_recv.at[k],
            across,
        )

    def back_copy(k):
        return remote(
            r.lent_y.at[k], r.back_y.at[k], r.back_send.at[k], r.back_recv.at[k], across
        )

    def send_meta(stage):
        meta_copy(stage, 0).start()
        meta_copy(stage, 1).start()

    before = (
        lax.broadcasted_iota(jnp.int32, (BLOCK, BLOCK), 0)
        < lax.broadcasted_iota(jnp.int32, (BLOCK, BLOCK), 1)
    ).astype(bf16)
    slot_row = lax.broadcasted_iota(jnp.int32, (PICK, WIDE), 0).astype(f32)
    slot_lane = lax.broadcasted_iota(jnp.int32, (BLOCK, 2 * PICK), 1).astype(f32)

    tall = lax.broadcasted_iota(jnp.int32, (BLOCK, BLOCK), 0).astype(f32)

    def ranks(live):
        return jnp.dot(live.astype(bf16), before, preferred_element_type=f32)

    def gate_row(block, expert):
        return r.meta[block, pl.ds(expert, 1), :]

    def wanted(either):
        live = jnp.broadcast_to(either, (8, BLOCK)) > 0.0
        return jnp.where(tall == jnp.where(live, ranks(live), -1.0)[0:1], 1.0, 0.0)

    def pack_rows(slot, block, to):
        expert = (to[0] // 2) * 2
        pick = wanted(jnp.maximum(gate_row(block, expert), gate_row(block, expert + 1)))
        r.fold[slot] = pick.T[:, :PAIR].astype(bf16)
        pick = pick[:PAIR].astype(bf16)

        r.pack[slot] = jnp.dot(
            pick, r.rows[block_rows(block, 0, BLOCK), :], preferred_element_type=f32
        ).astype(bf16)

    def send_picked(k):
        pack_rows(k, 4 * k, sides(k)[1])
        group_copy(k, 2).start()

    def pass_picked(k):
        group_copy(k, 0).wait_recv()
        group_copy(k, 1).wait_recv()
        pack_rows(4 + k, 4 * k + sides(k)[2], sides(k)[0])
        group_copy(k, 3).start()

    def compacted(own, other):
        pick = wanted(jnp.maximum(own, other)).astype(bf16)
        rest = jnp.concatenate([own, other], axis=0)
        terms = []
        for _ in range(3):
            term = rest.astype(bf16).astype(f32)
            terms.append(term)
            rest = rest - term
        terms = jnp.concatenate(terms + [jnp.zeros((2, BLOCK), f32)], axis=0).astype(bf16)
        got = lax.dot_general(terms, pick, (((1,), (1,)), ((), ())), preferred_element_type=f32)
        return (
            got[0:1] + got[2:3] + got[4:5],
            got[1:2] + got[3:4] + got[5:6],
        )

    def choose(k):
        pairs = []
        for j in range(4):
            pair = (gate_row(4 * k + j, ctx), gate_row(4 * k + j, sibling))
            pairs.append(compacted(*pair) if j in (2, sides(k)[3]) else pair)
        gate = jnp.concatenate([pair[e] for e in range(2) for pair in pairs], axis=0)
        live = gate > 0.0
        rank = ranks(live)
        shift = (lax.broadcasted_iota(jnp.int32, (8, BLOCK), 0) % 4).astype(f32) * CAP
        slot = jnp.where(live, rank + shift, -1.0)
        for half in range(2):
            lanes = jnp.concatenate([slot[4 * half + j : 4 * half + j + 1] for j in range(4)], axis=1)
            span = pl.ds(half * PICK, PICK)
            r.select[k, span, :] = jnp.where(slot_row == lanes, 1.0, 0.0).astype(bf16)
        upright = jnp.concatenate([slot, gate, jnp.zeros((BLOCK - 16, BLOCK), f32)], axis=0).T
        for j in range(4):
            own = jnp.where(slot_lane == upright[:, j : j + 1], upright[:, 8 + j : 9 + j], 0.0)
            other = jnp.where(
                slot_lane - PICK == upright[:, 4 + j : 5 + j], upright[:, 12 + j : 13 + j], 0.0
            )
            r.weigh[k, pl.ds(j * BLOCK, BLOCK), :] = jnp.where(
                slot_lane < PICK, own, other
            ).astype(bf16)

        got = jnp.dot(
            r.select[k], r.rows[pl.ds(k * WIDE, WIDE), :], preferred_element_type=f32
        ).astype(bf16)
        r.picked[k, pl.ds(0, PICK), :] = got[:PICK]
        r.lent[k] = got[PICK:]

        lent_copy(k).start()

    def feed(k):
        lent_copy(k).wait_recv()

        gate = jnp.dot(r.picked[k], r.wg[...], preferred_element_type=f32)
        up = jnp.dot(r.picked[k], r.wu[...], preferred_element_type=f32)
        r.activated[...] = (gate * sigmoid(gate) * up).astype(bf16)

    def produce(k):
        made = jnp.dot(r.activated[...], r.wd[...], preferred_element_type=f32)
        r.own_y[...] = made[:PICK].astype(bf16)
        r.lent_y[k] = made[PICK:].astype(bf16)

        back_copy(k).start()

    def combine(k):
        back_copy(k).wait_recv()

        both = jnp.concatenate([r.own_y[...], r.back_y[k]], axis=0)
        r.part[pl.ds(k * WIDE, WIDE), :] = jnp.dot(
            r.weigh[k], both, preferred_element_type=f32
        ).astype(bf16)

    def add_into(block, low, count, places):
        @pl.loop(0, count // 16)
        def _(i):
            span = pl.ds(pl.multiple_of(block * BLOCK + low + i * 16, 16), 16)
            total = r.part[span, :].astype(f32)
            for place in places:
                total += r.land[pl.ds(pl.multiple_of(place + i * 16, 16), 16), :].astype(f32)
            r.part[span, :] = total.astype(bf16)

    def expand(block, place, slot):
        span = block_rows(block, 0, BLOCK)
        more = jnp.dot(
            r.fold[slot], r.land[pl.ds(place, PAIR), :], preferred_element_type=f32
        )
        r.part[span, :] = (r.part[span, :].astype(f32) + more).astype(bf16)

    def sum_whole(k):
        group_sum(k, 0).wait_recv()
        expand(4 * k + sides(k)[2], group_land(k, 0), 4 + k)
        group_sum(k, 2).start()

    def sum_picked(k):
        group_sum(k, 1).wait_recv()
        expand(4 * k, group_land(k, 1), k)

    def sum_block(k):
        group_sum(k, 2).wait_recv()
        add_into(4 * k, 0, BLOCK, (group_land(k, 2),))

    def sum_pass(side):
        sum_copy(side).wait_recv()
        add_into(12 if side else 4, side * HALF, HALF, (side * HALF,))
        sum_copy(side + 4).start()

    def load_weights():
        for i, (src, dst) in enumerate(((r.w_gate, r.wg), (r.w_up, r.wu), (r.w_down, r.wd))):
            pltpu.make_async_copy(src.at[0], dst, r.load_sem.at[12 + i]).wait()

    finish_rows(0)
    finish_rows(1)
    row_copy(1).start()
    group_copy(0, 0).start()
    row_copy(0).start()
    score_rows()
    send_meta(0)
    send_meta(1)
    row_copy(3).start()
    row_copy(2).start()
    send_picked(0)
    meta_copy(0, 0).wait_recv()
    meta_copy(0, 2).start()
    send_meta(2)
    row_copy(0).wait_recv()
    group_copy(1, 0).start()
    group_copy(0, 1).start()
    row_copy(2).wait_recv()
    group_copy(1, 1).start()
    row_copy(1).wait_recv()
    row_copy(5).start()
    row_copy(4).start()
    meta_copy(1, 0).wait_recv()
    meta_copy(1, 2).start()
    pass_picked(0)
    meta_copy(0, 1).wait_recv()
    send_meta(4)
    group_copy(3, 1).start()
    row_copy(3).wait_recv()
    group_copy(3, 0).start()
    meta_copy(0, 2).wait_recv()
    send_meta(3)
    row_copy(4).wait_recv()
    group_copy(2, 0).start()
    send_picked(1)
    row_copy(5).wait_recv()
    group_copy(2, 1).start()
    meta_copy(1, 1).wait_recv()
    meta_copy(1, 2).wait_recv()
    group_copy(0, 2).wait_recv()
    group_copy(0, 3).wait_recv()
    choose(0)
    meta_copy(2, 0).wait_recv()
    meta_copy(2, 2).start()
    meta_copy(2, 1).wait_recv()
    pass_picked(1)
    send_picked(3)
    load_weights()
    feed(0)
    produce(0)
    meta_copy(4, 0).wait_recv()
    meta_copy(4, 2).start()
    meta_copy(4, 1).wait_recv()
    pass_picked(3)
    combine(0)
    group_sum(0, 1).start()
    group_sum(0, 0).start()
    meta_copy(2, 2).wait_recv()
    group_copy(1, 2).wait_recv()
    group_copy(1, 3).wait_recv()
    choose(1)
    send_picked(2)
    meta_copy(3, 0).wait_recv()
    meta_copy(3, 2).start()
    pass_picked(2)
    feed(1)
    produce(1)
    meta_copy(4, 2).wait_recv()
    group_copy(3, 2).wait_recv()
    group_copy(3, 3).wait_recv()
    choose(3)
    sum_whole(0)
    combine(1)
    feed(3)
    produce(3)
    meta_copy(3, 1).wait_recv()
    meta_copy(3, 2).wait_recv()
    group_copy(2, 2).wait_recv()
    group_copy(2, 3).wait_recv()
    choose(2)
    group_sum(1, 1).start()
    group_sum(1, 0).start()
    combine(3)
    group_sum(3, 1).start()
    feed(2)
    group_sum(3, 0).start()
    produce(2)
    combine(2)
    group_sum(2, 0).start()
    group_sum(2, 1).start()
    sum_whole(3)
    sum_block(0)
    sum_whole(1)
    sum_picked(1)
    sum_whole(2)
    sum_picked(2)
    sum_picked(3)
    sum_block(2)
    sum_copy(0).start()
    sum_copy(1).start()
    sum_block(1)
    sum_block(3)
    sum_copy(3).start()
    sum_copy(2).start()
    sum_pass(0)
    sum_pass(1)
    sum_picked(0)
    sum_copy(2).wait_recv()
    sum_copy(3).wait_recv()
    sum_copy(4).wait_recv()
    sum_copy(5).wait_recv()

    @pl.loop(0, BLOCK // 16)
    def _(i):
        span = pl.ds(pl.multiple_of(i * 16, 16), 16)
        total = r.part[span, :].astype(f32)
        for place in (BLOCK, 2 * BLOCK):
            total += r.land[pl.ds(pl.multiple_of(place + i * 16, 16), 16), :].astype(f32)
        r.done[span, :] = (r.hidden[span, :].astype(f32) + total).astype(bf16)

    store = pltpu.make_async_copy(r.done, r.out, r.load_sem.at[15])
    store.start()
    for kind in range(6):
        row_copy(kind).wait_send()
        sum_copy(kind).wait_send()
    for stage in range(5):
        for kind in range(3):
            meta_copy(stage, kind).wait_send()
    for k in range(4):
        for kind in range(4):
            group_copy(k, kind).wait_send()
        for kind in range(3):
            group_sum(k, kind).wait_send()
    for k in range(4):
        lent_copy(k).wait_send()
        back_copy(k).wait_send()
    store.wait()


def layer(
    filter_entry_array,
    gate_input,
    step_unshifted,
    step_bias,
    decay_log,
    conv_weight,
    conv_bias,
    skip_gain,
    mixer_gain,
    residual,
    expert_norm,
    router_weight,
    expert_ids,
    w_gate,
    w_up,
    w_down,
):
    hbm = pl.BlockSpec(memory_space=pl.ANY)
    specs = [hbm] * len(INPUTS)
    specs[INPUTS.index("skip")] = pl.BlockSpec(memory_space=pltpu.SMEM)
    return pl.pallas_call(
        layer_kernel,
        out_shape=jax.ShapeDtypeStruct((BLOCK, D), bf16),
        in_specs=specs,
        out_specs=hbm,
        scratch_shapes=list(scratch().values()),
        compiler_params=pltpu.CompilerParams(
            collective_id=0, has_side_effects=True, vmem_limit_bytes=62 * 1024 * 1024
        ),
    )(
        filter_entry_array,
        gate_input,
        step_unshifted,
        step_bias[None, :],
        decay_log[None, :],
        conv_weight,
        conv_bias,
        skip_gain,
        mixer_gain[None, :],
        residual,
        expert_norm[None, :],
        router_weight.T,
        expert_ids.T,
        w_gate,
        w_up,
        w_down,
    )


def solution(mesh):
    rows = P(("ctx", "exp"), None)
    shared = P()
    owner = P("ctx", None, None)
    return jax.shard_map(
        layer,
        mesh=mesh,
        in_specs=(
            rows,
            rows,
            P(None, ("ctx", "exp")),
            shared,
            shared,
            shared,
            shared,
            shared,
            shared,
            rows,
            shared,
            shared,
            rows,
            owner,
            owner,
            owner,
        ),
        out_specs=rows,
        check_vma=False,
    )
```

```python
import types

import jax
import jax.numpy as jnp
from jax import lax
from jax.experimental import pallas as pl
from jax.experimental.pallas import tpu as pltpu
from jax.sharding import PartitionSpec as P

D = 2048
HEADS = 32
HEAD_DIM = 64
STATE = 64
KERNEL = 4
TOPK = 8
CAP = 40
CONV = 2176
FF = 768
EXPERTS = 32
BLOCK = 128
HALF = BLOCK // 2
PICK = 4 * CAP
WIDE = 4 * BLOCK
COLUMN = 8
TILE = D // COLUMN
FLAT = 16
SENT = STATE + 16
PAIR = 2 * CAP

EXACT = lax.Precision.HIGHEST
MESH = pl.DeviceIdType.MESH
f32 = jnp.float32
bf16 = jnp.bfloat16


def sigmoid(value):
    return 1.0 / (1.0 + jnp.exp(-value))


def split(value, count):
    pieces = []
    for _ in range(count):
        piece = value.astype(bf16)
        pieces.append(piece)
        value = value - piece.astype(f32)
    return pieces


def remote(src, dst, send, recv, to):
    return pltpu.make_async_remote_copy(
        src_ref=src, dst_ref=dst, send_sem=send, recv_sem=recv, device_id=to, device_id_type=MESH
    )


INPUTS = (
    "entry", "gate", "step", "step_bias", "decay_log", "taps", "tap_bias", "skip", "mixer_gain",
    "residual", "expert_norm", "router", "ids", "w_gate", "w_up", "w_down",
)


def scratch():
    vmem = pltpu.VMEM
    dma = pltpu.SemaphoreType.DMA
    return {
        "padded": vmem((BLOCK + 16, CONV), bf16),
        "gate_v": vmem((BLOCK, D), bf16),
        "step_v": vmem((HEADS, BLOCK), f32),
        "step_bias_v": vmem((1, HEADS), f32),
        "decay_log_v": vmem((1, HEADS), f32),
        "taps_v": vmem((KERNEL, CONV), f32),
        "tap_bias_v": vmem((CONV,), f32),
        "mixer_gain_v": vmem((1, D), f32),
        "residual_v": vmem((BLOCK, D), bf16),
        "expert_norm_v": vmem((1, D), f32),
        "router_v": vmem((EXPERTS, D), bf16),
        "ids_v": vmem((TOPK, BLOCK), jnp.int32),
        "mixed": vmem((BLOCK, CONV), bf16),
        "cum": vmem((HEADS, BLOCK), f32),
        "delta": vmem((HEADS, BLOCK), f32),
        "cum_cols": vmem((BLOCK, 3 * HEADS), bf16),
        "tail_cols": vmem((BLOCK, 2 * HEADS), bf16),
        "entry_cols": vmem((BLOCK, 2 * HEADS), bf16),
        "last_rows": vmem((16, HEADS), bf16),
        "gram": vmem((BLOCK, BLOCK), f32),
        "piece": vmem((COLUMN, SENT, TILE), bf16),
        "first": vmem((COLUMN, SENT, TILE), bf16),
        "earlier": vmem((COLUMN, STATE, TILE), f32),
        "earlier_log": vmem((COLUMN, 8, TILE), f32),
        "total": vmem((SENT, TILE), bf16),
        "second": vmem((FLAT, SENT, TILE), bf16),
        "third": vmem((COLUMN, STATE, TILE), bf16),
        "state": vmem((COLUMN, STATE, TILE), bf16),
        "before": vmem((STATE, TILE), f32),
        "value": vmem((BLOCK, D), f32),
        "branch": vmem((BLOCK, D), f32),
        "hidden": vmem((BLOCK, D), bf16),
        "rows": vmem((16 * BLOCK, D), bf16),
        "meta": vmem((16, EXPERTS, BLOCK), f32),
        "wg": vmem((D, FF), bf16),
        "wu": vmem((D, FF), bf16),
        "wd": vmem((FF, D), bf16),
        "picked": vmem((4, 2 * PICK, D), bf16),
        "lent": vmem((4, PICK, D), bf16),
        "activated": vmem((2 * PICK, FF), bf16),
        "own_y": vmem((PICK, D), bf16),
        "lent_y": vmem((4, PICK, D), bf16),
        "back_y": vmem((4, PICK, D), bf16),
        "select": vmem((4, 2 * PICK, WIDE), bf16),
        "weigh": vmem((4, WIDE, 2 * PICK), bf16),
        "part": vmem((16 * BLOCK, D), bf16),
        "land": vmem((3 * BLOCK + 4 * (2 * PAIR + BLOCK), D), bf16),
        "pack": vmem((8, PAIR, D), bf16),
        "fold": vmem((8, BLOCK, PAIR), bf16),
        "done": vmem((BLOCK, D), bf16),
        "load_sem": dma((16,)),
        "halo_send": dma((1,)),
        "halo_recv": dma((1,)),
        "first_send": dma((COLUMN,)),
        "first_recv": dma((COLUMN,)),
        "second_send": dma((FLAT,)),
        "second_recv": dma((FLAT,)),
        "third_send": dma((COLUMN,)),
        "third_recv": dma((COLUMN,)),
        "row_send": dma((22,)),
        "row_recv": dma((22,)),
        "meta_send": dma((15,)),
        "meta_recv": dma((15,)),
        "lent_send": dma((4,)),
        "lent_recv": dma((4,)),
        "back_send": dma((4,)),
        "back_recv": dma((4,)),
        "sum_send": dma((18,)),
        "sum_recv": dma((18,)),
    }


def layer_kernel(*refs):
    names = INPUTS + ("out",) + tuple(scratch())
    r = types.SimpleNamespace(**dict(zip(names, refs)))
    ctx = lax.axis_index("ctx")
    depth = lax.axis_index("exp")
    core = ctx % 2
    column = ctx // 2
    me = core * 4 + depth
    finish_rows, score_rows, finish = mix_rows(r, ctx, depth, core, column, me)
    spread_rows(r, ctx, depth, core, column, finish_rows, score_rows)
    finish()


def mix_rows(r, ctx, depth, core, column, me):
    def member(m):
        return (column * 2 + m // 4, m % 4)

    def peer(c):
        return (c * 2 + core, depth)

    last = (me == COLUMN - 1).astype(jnp.int32)
    after = (((column + last) % FLAT) * 2 + ((me + 1) % COLUMN) // 4, (me + 1) % 4)
    initial = (me == 0).astype(jnp.int32)
    ahead = (
        ((column - initial + FLAT) % FLAT) * 2 + ((me + COLUMN - 1) % COLUMN) // 4,
        (me + COLUMN - 1) % 4,
    )

    barrier = pltpu.get_barrier_semaphore()

    @pl.loop(1, COLUMN)
    def _(i):
        pl.semaphore_signal(
            barrier, inc=1, device_id=member((me + i) % COLUMN), device_id_type=MESH
        )

    @pl.loop(1, FLAT)
    def _(i):
        pl.semaphore_signal(
            barrier, inc=1, device_id=peer((column + i) % FLAT), device_id_type=MESH
        )

    @pl.when(me == COLUMN - 1)
    def _():
        pl.semaphore_signal(barrier, inc=1, device_id=after, device_id_type=MESH)

    @pl.when(me == 0)
    def _():
        pl.semaphore_signal(barrier, inc=1, device_id=ahead, device_id_type=MESH)

    def load(i, src, dst):
        copy = pltpu.make_async_copy(src, dst, r.load_sem.at[i])
        copy.start()
        return copy

    load_entry = load(0, r.entry, r.padded.at[pl.ds(16, BLOCK)])
    load_steps = [
        load(1, r.step, r.step_v),
        load(2, r.step_bias, r.step_bias_v),
        load(3, r.decay_log, r.decay_log_v),
    ]
    load_taps = [load(4, r.taps, r.taps_v), load(5, r.tap_bias, r.tap_bias_v)]
    load_rest = [
        load(6, r.gate, r.gate_v),
        load(7, r.residual, r.residual_v),
        load(8, r.mixer_gain, r.mixer_gain_v),
        load(9, r.expert_norm, r.expert_norm_v),
        load(10, r.router, r.router_v),
        load(11, r.ids, r.ids_v),
    ]
    for i, (src, dst) in enumerate(((r.w_gate, r.wg), (r.w_up, r.wu), (r.w_down, r.wd))):
        load(12 + i, src.at[0], dst)

    row_id = lax.broadcasted_iota(jnp.int32, (BLOCK, BLOCK), 0)
    lane_id = lax.broadcasted_iota(jnp.int32, (BLOCK, BLOCK), 1)
    square_id = [lax.broadcasted_iota(jnp.int32, (HEADS, HEADS), axis) for axis in (0, 1)]

    def upend(row):
        spot = jnp.where(square_id[0] == square_id[1], row, 0.0)
        return jnp.sum(spot, axis=1, keepdims=True)

    for copy in load_steps:
        copy.wait()
    shifted = r.step_v[...] + upend(r.step_bias_v[...])
    width = jnp.maximum(shifted, 0.0) + jnp.log1p(jnp.exp(-jnp.abs(shifted)))
    logs = -width * jnp.exp(upend(r.decay_log_v[...]))
    summed = jnp.dot(
        logs, (row_id <= lane_id).astype(f32), precision=EXACT, preferred_element_type=f32
    )
    r.cum[...] = summed
    r.delta[...] = width

    def upright(a):
        return jnp.concatenate([a, jnp.zeros((BLOCK - HEADS, BLOCK), f32)], axis=0).T[:, :HEADS]

    summed_t = upright(summed)
    width_t = upright(width)
    final = summed_t[BLOCK - 1 :, :]
    r.cum_cols[...] = jnp.concatenate(split(summed_t, 3), axis=1)
    r.tail_cols[...] = jnp.concatenate(split(jnp.exp(final - summed_t) * width_t, 2), axis=1)
    r.entry_cols[...] = jnp.concatenate(split(jnp.exp(summed_t), 2), axis=1)
    terms = split(final, 3)
    r.last_rows[...] = jnp.concatenate(
        terms + [jnp.zeros((13, HEADS), bf16)], axis=0
    )

    def spread(m, copies, per, count):
        head = lax.broadcasted_iota(jnp.int32, (HEADS, count), 0)
        lane = lax.broadcasted_iota(jnp.int32, (HEADS, count), 1)
        one = (head == 4 * m + lane // per).astype(bf16)
        return one if copies == 1 else jnp.concatenate([one] * copies, axis=0)

    for copy in load_taps:
        copy.wait()
    load_entry.wait()

    def convolve(full, count, cols):
        acc = jnp.broadcast_to(r.tap_bias_v[cols][None, :], (count, 128))
        for j in range(KERNEL):
            acc = acc + r.taps_v[j : j + 1, cols] * full[13 + j : 13 + j + count]
        return (acc * sigmoid(acc)).astype(bf16)

    @pl.loop(0, CONV // 128, unroll=1)
    def _(n):
        cols = pl.ds(pl.multiple_of(n * 128, 128), 128)
        r.mixed[16:, cols] = convolve(r.padded[16:, cols].astype(f32), BLOCK - 16, cols)

    def weighted(m, low, count):
        cols = pl.ds(pl.multiple_of(m * TILE, TILE), TILE)
        span = pl.ds(low, count)
        weight = jnp.dot(
            r.tail_cols[span, :], spread(m, 2, HEAD_DIM, TILE), preferred_element_type=f32
        )
        source = r.mixed[span, D : D + STATE]
        return lax.dot_general(
            jnp.concatenate([source, source], axis=0),
            jnp.concatenate(split(r.mixed[span, cols].astype(f32) * weight, 2), axis=0),
            (((0,), (0,)), ((), ())),
            preferred_element_type=f32,
        )

    @pl.loop(0, COLUMN, unroll=2)
    def _(m):
        r.earlier[m] = weighted(m, 16, BLOCK - 16)

    for k in range(4):
        for block in (2, 3 - 2 * (k % 2)):
            low = (4 * k + block) * BLOCK + PAIR
            r.rows[low : low + BLOCK - PAIR, :] = jnp.zeros((BLOCK - PAIR, D), bf16)

    pl.semaphore_wait(barrier, COLUMN + FLAT - 2 + last + initial)
    halo = remote(
        r.padded.at[pl.ds(BLOCK, 16)],
        r.padded.at[pl.ds(0, 16)],
        r.halo_send.at[0],
        r.halo_recv.at[0],
        after,
    )
    halo.start()

    for copy in load_rest:
        copy.wait()

    @pl.loop(0, COLUMN, unroll=2)
    def _(m):
        cols = pl.ds(pl.multiple_of(m * TILE, TILE), TILE)
        branch = r.gate_v[:, cols].astype(f32)
        r.branch[:, cols] = branch * sigmoid(branch)

    halo.wait_recv()
    keep = (ctx + depth > 0).astype(f32)

    @pl.loop(0, CONV // 128, unroll=1)
    def _(n):
        cols = pl.ds(pl.multiple_of(n * 128, 128), 128)
        full = jnp.concatenate(
            [r.padded[0:16, cols].astype(f32) * keep, r.padded[16:32, cols].astype(f32)], axis=0
        )
        r.mixed[0:16, cols] = convolve(full, 16, cols)

    in_map = r.mixed[:, D : D + STATE]
    out_map = r.mixed[:, D + STATE : D + 2 * STATE]

    def first_copy(m, slot):
        return remote(
            r.piece.at[m], r.first.at[slot], r.first_send.at[m], r.first_recv.at[slot], member(m)
        )

    def around(i):
        q = i // 2
        return ((core + i) % 2) * 4 + (depth + q + q // 2 - 2 * (q // 3)) % 4

    @pl.loop(0, COLUMN, unroll=2)
    def _(i):
        m = around(COLUMN - 1 - i)
        r.piece[m, 0:STATE, :] = (r.earlier[m] + weighted(m, 0, 16)).astype(bf16)
        r.piece[m, STATE:, :] = jnp.dot(
            r.last_rows[...], spread(m, 1, HEAD_DIM, TILE), preferred_element_type=f32
        ).astype(bf16)

        @pl.when(i < COLUMN - 1)
        def _():
            first_copy(m, me).start()

    r.first[me] = r.piece[me]

    cross = lax.dot_general(
        out_map, in_map, (((1,), (1,)), ((), ())), preferred_element_type=f32
    )
    r.gram[...] = jnp.where(row_id >= lane_id, cross, 0.0)

    def inside(m):
        cols = pl.ds(pl.multiple_of(m * TILE, TILE), TILE)
        upto = jnp.dot(r.cum_cols[...], spread(m, 3, BLOCK, 4 * BLOCK), preferred_element_type=f32)
        feature = r.mixed[:, cols]
        lane = lax.broadcasted_iota(jnp.int32, (BLOCK, TILE), 1) // HEAD_DIM
        highs, lows, blocks = [], [], []
        for j in range(4):
            head = pl.ds(4 * m + j, 1)
            gap = upto[:, BLOCK * j : BLOCK * (j + 1)] - r.cum[head, :]
            mix = jnp.exp(jnp.minimum(gap, 0.0)) * r.gram[...] * r.delta[head, :]
            mix = mix + jnp.where(row_id == lane_id, r.skip[4 * m + j], 0.0)
            high, low = split(mix, 2)
            highs.append(high)
            lows.append(low)
            blocks.append(jnp.where(lane == j, feature, jnp.zeros_like(feature)))
        diagonal = jnp.concatenate(blocks, axis=0)
        r.value[:, cols] = jnp.dot(
            jnp.concatenate(highs, axis=1), diagonal, preferred_element_type=f32
        ) + jnp.dot(jnp.concatenate(lows, axis=1), diagonal, preferred_element_type=f32)

    @pl.loop(0, COLUMN // 2, unroll=2)
    def _(m):
        inside(m)

    @pl.loop(0, COLUMN, unroll=2)
    def _(m):
        @pl.when(m != me)
        def _():
            first_copy(m, m).wait_recv()

    def log_of(block):
        terms = block.astype(f32)
        return terms[0:1] + terms[1:2] + terms[2:3]

    run = jnp.zeros((STATE, TILE), f32)
    run_log = jnp.zeros((1, TILE), f32)
    for m in range(COLUMN):
        r.earlier[m] = run
        r.earlier_log[m] = jnp.broadcast_to(run_log, (8, TILE))
        log = log_of(r.first[m, STATE:, :])
        run = run * jnp.exp(log) + r.first[m, 0:STATE, :].astype(f32)
        run_log = run_log + log
    r.total[0:STATE, :] = run.astype(bf16)
    r.total[STATE:, :] = jnp.concatenate(
        split(run_log, 3) + [jnp.zeros((13, TILE), bf16)], axis=0
    )

    def second_copy(o):
        return remote(
            r.total,
            r.second.at[o],
            r.second_send.at[o],
            r.second_recv.at[o],
            peer((column + o) % FLAT),
        )

    @pl.loop(1, FLAT)
    def _(i):
        o = FLAT - i

        @pl.when(column + o < FLAT)
        def _():
            second_copy(o).start()

    @pl.loop(COLUMN // 2, COLUMN, unroll=2)
    def _(m):
        inside(m)

    @pl.loop(0, COLUMN, unroll=2)
    def _(m):
        cols = pl.ds(pl.multiple_of(m * TILE, TILE), TILE)
        weight = jnp.dot(r.entry_cols[...], spread(m, 2, HEAD_DIM, TILE), preferred_element_type=f32)
        branch = r.branch[:, cols]
        r.value[:, cols] = r.value[:, cols] * branch
        r.branch[:, cols] = weight * branch

    r.before[...] = jnp.zeros((STATE, TILE), f32)

    @pl.loop(1, FLAT)
    def _(i):
        o = FLAT - i

        @pl.when(o <= column)
        def _():
            second_copy(o).wait_recv()
            r.before[...] = (
                r.before[...] * jnp.exp(log_of(r.second[o, STATE:, :]))
                + r.second[o, 0:STATE, :].astype(f32)
            )

    def third_copy(m, slot):
        return remote(
            r.third.at[m], r.state.at[slot], r.third_send.at[m], r.third_recv.at[slot], member(m)
        )

    @pl.loop(0, COLUMN, unroll=2)
    def _(i):
        m = around(COLUMN - 1 - i)
        r.third[m] = (r.before[...] * jnp.exp(r.earlier_log[m, 0:1, :]) + r.earlier[m]).astype(bf16)

        @pl.when(i < COLUMN - 1)
        def _():
            third_copy(m, me).start()

    r.state[me] = r.third[me]

    def fold(a):
        return a[:, :128] + a[:, 128:]

    def carry(i, square):
        m = around(i)

        @pl.when(i > 0)
        def _():
            third_copy(m, m).wait_recv()

        cols = pl.ds(pl.multiple_of(m * TILE, TILE), TILE)
        carried = jnp.dot(out_map, r.state[m], preferred_element_type=f32)
        v = r.value[:, cols] + carried * r.branch[:, cols]
        r.value[:, cols] = v
        return square + fold(v * v)

    zero = jnp.zeros((BLOCK, 128), f32)
    square = lax.fori_loop(0, COLUMN, carry, zero, unroll=2)
    scale = lax.rsqrt(jnp.sum(square, axis=1, keepdims=True) * (1.0 / D) + 1e-05)

    def finish_rows(half):
        span = pl.ds(half * HALF, HALF)
        mine = scale[half * HALF : (half + 1) * HALF]

        def join(m, square):
            cols = pl.ds(pl.multiple_of(m * TILE, TILE), TILE)
            out = r.value[span, cols] * mine * r.mixer_gain_v[:, cols]
            kept = (r.residual_v[span, cols].astype(f32) + out).astype(bf16)
            r.hidden[span, cols] = kept
            wide = kept.astype(f32)
            return square + fold(wide * wide)

        square = lax.fori_loop(0, COLUMN, join, jnp.zeros((HALF, 128), f32), unroll=2)
        again = lax.rsqrt(jnp.sum(square, axis=1, keepdims=True) * (1.0 / D) + 1e-05)

        @pl.loop(0, COLUMN, unroll=2)
        def _(m):
            cols = pl.ds(pl.multiple_of(m * TILE, TILE), TILE)
            r.rows[span, cols] = (
                r.hidden[span, cols].astype(f32) * again * r.expert_norm_v[:, cols]
            ).astype(bf16)

    def score_rows():
        logits = lax.dot_general(
            r.router_v[...], r.rows[0:BLOCK, :], (((1,), (1,)), ((), ())), preferred_element_type=f32
        )
        expert = lax.broadcasted_iota(jnp.int32, (EXPERTS, BLOCK), 0)
        chosen = expert < 0
        for k in range(TOPK):
            chosen = chosen | (expert == r.ids_v[k : k + 1, :])
        score = jnp.where(chosen, sigmoid(logits), 0.0)
        r.meta[0] = score / jnp.sum(score, axis=0, keepdims=True)

    def finish():
        halo.wait_send()

        @pl.loop(0, COLUMN, unroll=2)
        def _(m):
            @pl.when(m != me)
            def _():
                first_copy(m, me).wait_send()
                third_copy(m, me).wait_send()

        @pl.loop(1, FLAT)
        def _(o):
            @pl.when(column + o < FLAT)
            def _():
                second_copy(o).wait_send()

    return finish_rows, score_rows, finish


def spread_rows(r, ctx, depth, core, column, finish_rows, score_rows):
    x = column % 4
    y = column // 4
    sibling = ctx + 1 - 2 * core

    def device(first, second):
        to_y = (y + core * first + (1 - core) * second + 4) % 4
        to_x = (x + core * second + (1 - core) * first + 4) % 4
        return ((to_y * 4 + to_x) * 2 + core, depth)

    forth = (device(1, 0), device(0, 1))
    back = (device(-1, 0), device(0, -1))
    across = (sibling, depth)

    def ring(stage):
        return (0, 4, 0) if stage == 0 else (4 * (stage - 1), 1, 1)

    def sides(k):
        ahead, behind = (forth[1], back[1]) if k % 2 == 0 else (back[1], forth[1])
        return ahead, behind, 1 + 2 * (k % 2), 3 - 2 * (k % 2)

    def block_rows(block, low, count):
        return pl.ds(block * BLOCK + low, count)

    def row_copy(kind):
        to = (forth, back)[kind % 2][0]
        source, target, low = (
            (0, 4, 0), (0, 12, HALF), (0, 4, HALF), (0, 12, 0), (4, 8, 0), (12, 8, HALF)
        )[kind]
        return remote(
            r.rows.at[block_rows(source, low, HALF)],
            r.rows.at[block_rows(target, low, HALF)],
            r.row_send.at[kind],
            r.row_recv.at[kind],
            to,
        )

    def group_copy(k, kind):
        ahead, behind, whole, picked = sides(k)
        sem = 6 + 4 * k + kind
        if kind < 2:
            source = r.rows.at[block_rows(4 * k, kind * HALF, HALF)]
            target, to = block_rows(4 * k + whole, kind * HALF, HALF), ahead
        elif kind == 2:
            source, target, to = r.pack.at[k], block_rows(4 * k + picked, 0, PAIR), behind
        else:
            source, target, to = r.pack.at[4 + k], block_rows(4 * k + 2, 0, PAIR), ahead
        return remote(source, r.rows.at[target], r.row_send.at[sem], r.row_recv.at[sem], to)

    def meta_copy(stage, kind):
        base, stride, axis = ring(stage)
        sem = 3 * stage + kind
        source, target, to = ((0, 1, forth), (0, 3, back), (1, 2, forth))[kind]
        return remote(
            r.meta.at[base + stride * source],
            r.meta.at[base + stride * target],
            r.meta_send.at[sem],
            r.meta_recv.at[sem],
            to[axis],
        )

    def sum_copy(kind):
        to = (back, forth)[kind % 2][0]
        source, low, place = (
            (8, 0, 0),
            (8, HALF, HALF),
            (4, HALF, BLOCK + HALF),
            (12, 0, 2 * BLOCK),
            (4, 0, BLOCK),
            (12, HALF, 2 * BLOCK + HALF),
        )[kind]
        return remote(
            r.part.at[block_rows(source, low, HALF)],
            r.land.at[pl.ds(place, HALF)],
            r.sum_send.at[kind],
            r.sum_recv.at[kind],
            to,
        )

    def group_land(k, kind):
        return 3 * BLOCK + k * (2 * PAIR + BLOCK) + kind * PAIR

    def group_sum(k, kind):
        ahead, behind, whole, picked = sides(k)
        sem = 6 + 3 * k + kind
        block, count, to = ((2, PAIR, behind), (picked, PAIR, ahead), (whole, BLOCK, behind))[kind]
        return remote(
            r.part.at[block_rows(4 * k + block, 0, count)],
            r.land.at[pl.ds(group_land(k, kind), count)],
            r.sum_send.at[sem],
            r.sum_recv.at[sem],
            to,
        )

    def lent_copy(k):
        return remote(
            r.lent.at[k],
            r.picked.at[k, pl.ds(PICK, PICK)],
            r.lent_send.at[k],
            r.lent_recv.at[k],
            across,
        )

    def back_copy(k):
        return remote(
            r.lent_y.at[k], r.back_y.at[k], r.back_send.at[k], r.back_recv.at[k], across
        )

    def send_meta(stage):
        meta_copy(stage, 0).start()
        meta_copy(stage, 1).start()

    before = (
        lax.broadcasted_iota(jnp.int32, (BLOCK, BLOCK), 0)
        < lax.broadcasted_iota(jnp.int32, (BLOCK, BLOCK), 1)
    ).astype(bf16)
    slot_row = lax.broadcasted_iota(jnp.int32, (PICK, WIDE), 0).astype(f32)
    slot_lane = lax.broadcasted_iota(jnp.int32, (BLOCK, 2 * PICK), 1).astype(f32)

    tall = lax.broadcasted_iota(jnp.int32, (BLOCK, BLOCK), 0).astype(f32)

    def ranks(live):
        return jnp.dot(live.astype(bf16), before, preferred_element_type=f32)

    def gate_row(block, expert):
        return r.meta[block, pl.ds(expert, 1), :]

    def wanted(either):
        live = jnp.broadcast_to(either, (8, BLOCK)) > 0.0
        return jnp.where(tall == jnp.where(live, ranks(live), -1.0)[0:1], 1.0, 0.0)

    def pack_rows(slot, block, to):
        expert = (to[0] // 2) * 2
        pick = wanted(jnp.maximum(gate_row(block, expert), gate_row(block, expert + 1)))
        r.fold[slot] = pick.T[:, :PAIR].astype(bf16)
        pick = pick[:PAIR].astype(bf16)

        r.pack[slot] = jnp.dot(
            pick, r.rows[block_rows(block, 0, BLOCK), :], preferred_element_type=f32
        ).astype(bf16)

    def send_picked(k):
        pack_rows(k, 4 * k, sides(k)[1])
        group_copy(k, 2).start()

    def pass_picked(k):
        group_copy(k, 0).wait_recv()
        group_copy(k, 1).wait_recv()
        pack_rows(4 + k, 4 * k + sides(k)[2], sides(k)[0])
        group_copy(k, 3).start()

    def compacted(own, other):
        pick = wanted(jnp.maximum(own, other)).astype(bf16)
        rest = jnp.concatenate([own, other], axis=0)
        terms = []
        for _ in range(3):
            term = rest.astype(bf16).astype(f32)
            terms.append(term)
            rest = rest - term
        terms = jnp.concatenate(terms + [jnp.zeros((2, BLOCK), f32)], axis=0).astype(bf16)
        got = lax.dot_general(terms, pick, (((1,), (1,)), ((), ())), preferred_element_type=f32)
        return (
            got[0:1] + got[2:3] + got[4:5],
            got[1:2] + got[3:4] + got[5:6],
        )

    def choose(k):
        pairs = []
        for j in range(4):
            pair = (gate_row(4 * k + j, ctx), gate_row(4 * k + j, sibling))
            pairs.append(compacted(*pair) if j in (2, sides(k)[3]) else pair)
        gate = jnp.concatenate([pair[e] for e in range(2) for pair in pairs], axis=0)
        live = gate > 0.0
        rank = ranks(live)
        shift = (lax.broadcasted_iota(jnp.int32, (8, BLOCK), 0) % 4).astype(f32) * CAP
        slot = jnp.where(live, rank + shift, -1.0)
        for half in range(2):
            lanes = jnp.concatenate([slot[4 * half + j : 4 * half + j + 1] for j in range(4)], axis=1)
            span = pl.ds(half * PICK, PICK)
            r.select[k, span, :] = jnp.where(slot_row == lanes, 1.0, 0.0).astype(bf16)
        upright = jnp.concatenate([slot, gate, jnp.zeros((BLOCK - 16, BLOCK), f32)], axis=0).T
        for j in range(4):
            own = jnp.where(slot_lane == upright[:, j : j + 1], upright[:, 8 + j : 9 + j], 0.0)
            other = jnp.where(
                slot_lane - PICK == upright[:, 4 + j : 5 + j], upright[:, 12 + j : 13 + j], 0.0
            )
            r.weigh[k, pl.ds(j * BLOCK, BLOCK), :] = jnp.where(
                slot_lane < PICK, own, other
            ).astype(bf16)

        got = jnp.dot(
            r.select[k], r.rows[pl.ds(k * WIDE, WIDE), :], preferred_element_type=f32
        ).astype(bf16)
        r.picked[k, pl.ds(0, PICK), :] = got[:PICK]
        r.lent[k] = got[PICK:]

        lent_copy(k).start()

    def feed(k):
        lent_copy(k).wait_recv()

        gate = jnp.dot(r.picked[k], r.wg[...], preferred_element_type=f32)
        up = jnp.dot(r.picked[k], r.wu[...], preferred_element_type=f32)
        r.activated[...] = (gate * sigmoid(gate) * up).astype(bf16)

    def produce(k):
        made = jnp.dot(r.activated[...], r.wd[...], preferred_element_type=f32)
        r.own_y[...] = made[:PICK].astype(bf16)
        r.lent_y[k] = made[PICK:].astype(bf16)

        back_copy(k).start()

    def combine(k):
        back_copy(k).wait_recv()

        both = jnp.concatenate([r.own_y[...], r.back_y[k]], axis=0)
        r.part[pl.ds(k * WIDE, WIDE), :] = jnp.dot(
            r.weigh[k], both, preferred_element_type=f32
        ).astype(bf16)

    def add_into(block, low, count, places):
        @pl.loop(0, count // 16)
        def _(i):
            span = pl.ds(pl.multiple_of(block * BLOCK + low + i * 16, 16), 16)
            total = r.part[span, :].astype(f32)
            for place in places:
                total += r.land[pl.ds(pl.multiple_of(place + i * 16, 16), 16), :].astype(f32)
            r.part[span, :] = total.astype(bf16)

    def expand(block, place, slot):
        span = block_rows(block, 0, BLOCK)
        more = jnp.dot(
            r.fold[slot], r.land[pl.ds(place, PAIR), :], preferred_element_type=f32
        )
        r.part[span, :] = (r.part[span, :].astype(f32) + more).astype(bf16)

    def sum_whole(k):
        group_sum(k, 0).wait_recv()
        expand(4 * k + sides(k)[2], group_land(k, 0), 4 + k)
        group_sum(k, 2).start()

    def sum_picked(k):
        group_sum(k, 1).wait_recv()
        expand(4 * k, group_land(k, 1), k)

    def sum_block(k):
        group_sum(k, 2).wait_recv()
        add_into(4 * k, 0, BLOCK, (group_land(k, 2),))

    def sum_pass(side):
        sum_copy(side).wait_recv()
        add_into(12 if side else 4, side * HALF, HALF, (side * HALF,))
        sum_copy(side + 4).start()

    def load_weights():
        for i, (src, dst) in enumerate(((r.w_gate, r.wg), (r.w_up, r.wu), (r.w_down, r.wd))):
            pltpu.make_async_copy(src.at[0], dst, r.load_sem.at[12 + i]).wait()

    finish_rows(0)
    row_copy(3).start()
    group_copy(0, 0).start()
    row_copy(0).start()
    finish_rows(1)
    score_rows()
    send_meta(0)
    send_meta(1)
    row_copy(1).start()
    group_copy(0, 1).start()
    row_copy(2).start()
    send_picked(0)
    meta_copy(0, 1).wait_recv()
    send_meta(4)
    row_copy(3).wait_recv()
    group_copy(3, 0).start()
    row_copy(0).wait_recv()
    row_copy(4).start()
    meta_copy(0, 0).wait_recv()
    meta_copy(0, 2).start()
    send_meta(2)
    group_copy(1, 0).start()
    row_copy(2).wait_recv()
    group_copy(1, 1).start()
    meta_copy(1, 0).wait_recv()
    meta_copy(1, 2).start()
    pass_picked(0)
    row_copy(1).wait_recv()
    group_copy(3, 1).start()
    send_picked(1)
    meta_copy(2, 0).wait_recv()
    meta_copy(2, 2).start()
    meta_copy(2, 1).wait_recv()
    pass_picked(1)
    meta_copy(1, 1).wait_recv()
    meta_copy(1, 2).wait_recv()
    group_copy(0, 2).wait_recv()
    group_copy(0, 3).wait_recv()
    choose(0)
    send_picked(3)
    meta_copy(0, 2).wait_recv()
    send_meta(3)
    row_copy(4).wait_recv()
    group_copy(2, 0).start()
    row_copy(5).start()
    load_weights()
    feed(0)
    produce(0)
    meta_copy(2, 2).wait_recv()
    group_copy(1, 2).wait_recv()
    group_copy(1, 3).wait_recv()
    choose(1)
    meta_copy(4, 0).wait_recv()
    meta_copy(4, 2).start()
    meta_copy(4, 1).wait_recv()
    pass_picked(3)
    row_copy(5).wait_recv()
    group_copy(2, 1).start()
    combine(0)
    group_sum(0, 0).start()
    send_picked(2)
    group_sum(0, 1).start()
    feed(1)
    produce(1)
    meta_copy(3, 0).wait_recv()
    meta_copy(3, 2).start()
    pass_picked(2)
    meta_copy(4, 2).wait_recv()
    group_copy(3, 2).wait_recv()
    group_copy(3, 3).wait_recv()
    choose(3)
    combine(1)
    sum_whole(0)
    group_sum(1, 1).start()
    group_sum(1, 0).start()
    feed(3)
    produce(3)
    meta_copy(3, 1).wait_recv()
    meta_copy(3, 2).wait_recv()
    group_copy(2, 2).wait_recv()
    group_copy(2, 3).wait_recv()
    choose(2)
    combine(3)
    group_sum(3, 1).start()
    group_sum(3, 0).start()
    feed(2)
    produce(2)
    combine(2)
    group_sum(2, 0).start()
    group_sum(2, 1).start()
    sum_block(0)
    sum_whole(3)
    sum_whole(2)
    sum_picked(1)
    sum_picked(2)
    sum_whole(1)
    sum_block(2)
    sum_copy(0).start()
    sum_copy(1).start()
    sum_block(3)
    sum_picked(3)
    sum_copy(3).start()
    sum_block(1)
    sum_copy(2).start()
    sum_picked(0)
    sum_pass(0)
    sum_pass(1)
    sum_copy(2).wait_recv()
    sum_copy(3).wait_recv()
    sum_copy(4).wait_recv()
    sum_copy(5).wait_recv()

    @pl.loop(0, BLOCK // 16)
    def _(i):
        span = pl.ds(pl.multiple_of(i * 16, 16), 16)
        total = r.part[span, :].astype(f32)
        for place in (BLOCK, 2 * BLOCK):
            total += r.land[pl.ds(pl.multiple_of(place + i * 16, 16), 16), :].astype(f32)
        r.done[span, :] = (r.hidden[span, :].astype(f32) + total).astype(bf16)

    store = pltpu.make_async_copy(r.done, r.out, r.load_sem.at[15])
    store.start()
    for kind in range(6):
        row_copy(kind).wait_send()
        sum_copy(kind).wait_send()
    for stage in range(5):
        for kind in range(3):
            meta_copy(stage, kind).wait_send()
    for k in range(4):
        for kind in range(4):
            group_copy(k, kind).wait_send()
        for kind in range(3):
            group_sum(k, kind).wait_send()
    for k in range(4):
        lent_copy(k).wait_send()
        back_copy(k).wait_send()
    store.wait()


def layer(
    filter_entry_array,
    gate_input,
    step_unshifted,
    step_bias,
    decay_log,
    conv_weight,
    conv_bias,
    skip_gain,
    mixer_gain,
    residual,
    expert_norm,
    router_weight,
    expert_ids,
    w_gate,
    w_up,
    w_down,
):
    hbm = pl.BlockSpec(memory_space=pl.ANY)
    specs = [hbm] * len(INPUTS)
    specs[INPUTS.index("skip")] = pl.BlockSpec(memory_space=pltpu.SMEM)
    return pl.pallas_call(
        layer_kernel,
        out_shape=jax.ShapeDtypeStruct((BLOCK, D), bf16),
        in_specs=specs,
        out_specs=hbm,
        scratch_shapes=list(scratch().values()),
        compiler_params=pltpu.CompilerParams(
            collective_id=0, has_side_effects=True, vmem_limit_bytes=62 * 1024 * 1024
        ),
    )(
        filter_entry_array,
        gate_input,
        step_unshifted,
        step_bias[None, :],
        decay_log[None, :],
        conv_weight,
        conv_bias,
        skip_gain,
        mixer_gain[None, :],
        residual,
        expert_norm[None, :],
        router_weight.T,
        expert_ids.T,
        w_gate,
        w_up,
        w_down,
    )


def solution(mesh):
    rows = P(("ctx", "exp"), None)
    shared = P()
    owner = P("ctx", None, None)
    return jax.shard_map(
        layer,
        mesh=mesh,
        in_specs=(
            rows,
            rows,
            P(None, ("ctx", "exp")),
            shared,
            shared,
            shared,
            shared,
            shared,
            shared,
            rows,
            shared,
            shared,
            rows,
            owner,
            owner,
            owner,
        ),
        out_specs=rows,
        check_vma=False,
    )
```
